128 devices in a mesh: row: 16 (over z, y_hi, core), col: 8 (over x, y_lo).
Axes of the slice: x: 4, y: 4 (y_hi: 2, y_lo: 2; y = y_hi * 2 + y_lo), z: 4, core: 2. Of those that a mesh axis runs over, the one named last changes fastest.
Arguments:
- roll_hidden: bfloat16 [5376, 4096], P(('row', 'col')), may hold values from -6 to 6
- roll_cotangent: bfloat16 [5376, 4096], P(('row', 'col')), may hold values from -6 to 6
- lengths: int32 [128], P(('row', 'col')), may hold values from 1 to 42, as said below
- owners: int32 [128], P(('row', 'col')), may hold values from 0 to 15, as said below
- prompts: int32 [128], P(('row', 'col')), may hold values from 0 to 15
- rewards: float32 [128], P(('row', 'col')), may hold values from -5 to 5
- gate_weight: bfloat16 [4096, 14784], P('col', 'row'), may hold values from -0.09375 to 0.09375
- up_weight: bfloat16 [4096, 14784], P('col', 'row'), may hold values from -0.09375 to 0.09375
- down_weight: bfloat16 [14784, 4096], P('row', 'col'), may hold values from -0.046875 to 0.046875
Outputs:
- grad_input: bfloat16 [2048, 4096], P('row', 'col')
- grad_gate: bfloat16 [4096, 14784], P('col', 'row')
- grad_up: bfloat16 [4096, 14784], P('col', 'row')
- grad_down: bfloat16 [14784, 4096], P('row', 'col')
The draws below stay inside these ranges and needn't reach their ends.
Inputs may be any that keep to these rules, and one draw needn't show every extreme that they name: `owners`: each owner value names exactly 8 rows; the lengths of one owner's rows sum to at most 128, and to exactly 128 for some owner in every draw. `lengths`: some row has length 42 in every draw.
All inputs are finite; a program needn't handle non-finite values.
Results may differ from the reference program's by a relative error of at most 0.025.
Values may be sent and summed in bfloat16 or wider, within the bound.
No kernel may reach another device: no remote copies, remote signals or barrier semaphores. Data moves between devices by JAX's collectives and lax.ppermute only.
A program may use at most 128 MiB of HBM per device.

```python
import jax
import jax.numpy as jnp
from jax import lax

D = 4096
FF = 14784
CAPR = 128
MAXLEN = 42
OWNERS = 16
PER_OWNER = 8
ROWS = 128
PROMPTS = 16
TOKENS = 2048
N_COL = 8


def owner_table(key):
    key_perm = jax.random.fold_in(key, 101)
    key_special = jax.random.fold_in(key, 202)
    key_total = jax.random.fold_in(key, 303)
    key_share = jax.random.fold_in(key, 404)
    order = jax.random.permutation(key_perm, ROWS).astype(jnp.int32)
    owner = (order // PER_OWNER).astype(jnp.int32)
    place = (order % PER_OWNER).astype(jnp.int32)
    special = jax.random.randint(key_special, (), 0, OWNERS, dtype=jnp.int32)
    ids = jnp.arange(OWNERS, dtype=jnp.int32)
    total = jax.random.randint(key_total, (OWNERS,), CAPR // 2, CAPR + 1, dtype=jnp.int32)
    total = jnp.where(ids == special, CAPR, total)
    has_big = (ids == special).astype(jnp.int32)
    columns = jnp.arange(PER_OWNER, dtype=jnp.int32)
    is_big = (has_big[:, None] == 1) & (columns[None, :] == 0)
    shares = jax.random.randint(key_share, (OWNERS, PER_OWNER), 1, 4, dtype=jnp.int32)
    shares = jnp.where(has_big[:, None] == 1, 1, shares)
    shares = jnp.where(is_big, 0, shares)
    share_sum = jnp.sum(shares, 1)
    small_count = PER_OWNER - has_big
    extra = total - has_big * MAXLEN - small_count
    portion = extra[:, None] * shares // share_sum[:, None]
    remain = extra - jnp.sum(portion, 1)
    ranks = columns[None, :] - has_big[:, None]
    bump = ((ranks < remain[:, None]) & jnp.logical_not(is_big)).astype(jnp.int32)
    raw = jnp.minimum(1 + portion + bump, MAXLEN)
    parts = jnp.where(is_big, MAXLEN, raw).astype(jnp.int32)
    lengths = parts[owner, place].astype(jnp.int32)
    return (lengths, owner)


def draw_lengths(key, part):
    return owner_table(key)[0]


def draw_owners(key, part):
    return owner_table(key)[1]


def place_ends(entries, key, least, largest):
    longest = entries.shape.index(max(entries.shape))
    spots = []
    for shift in (0, 1):
        where = [jax.random.randint(jax.random.fold_in(key, axis), (), 0, length) for axis, length in enumerate(entries.shape)]
        where[longest] = (where[longest] + shift) % entries.shape[longest]
        spots.append(tuple(where))
    return entries.at[spots[0]].set(least).at[spots[1]].set(largest)


def block_scale(stream_key, dims, split, smallest, top_value):
    gain, own = 1.0, jax.random.fold_in(stream_key, 6)
    for axis_at, blocks in split:
        draws = jnp.exp(jax.random.uniform(jax.random.fold_in(own, axis_at), (blocks,), jnp.float32, smallest / len(split), top_value / len(split)))
        gain = gain * jnp.repeat(draws, dims[axis_at] // blocks).reshape([-1 if axis == axis_at else 1 for axis in range(len(dims))])
    return gain


def normal_values(key, shape, deviation, most, pieces=(), kind=jnp.bfloat16):
    values = deviation * jax.random.normal(key, shape, jnp.float32)
    if pieces:
        values = values * block_scale(key, shape, pieces, -0.22, 0.18)
    return jnp.clip(values, -most, most).astype(kind)


def setup_inputs(seed: int = 0) -> dict:
    streams_of = jax.random.split(jax.random.key(seed), 10)
    roll_hidden = normal_values(streams_of[0], (ROWS * MAXLEN, D), 1.0, 6.0, ((0, 128),))
    roll_cotangent = normal_values(streams_of[1], (ROWS * MAXLEN, D), 1.0, 6.0, ((0, 128),))
    lengths = draw_lengths(jax.random.fold_in(streams_of[9], 71), 0)
    owners = draw_owners(jax.random.fold_in(streams_of[9], 71), 0)
    prompts = place_ends(jax.random.randint(streams_of[4], (ROWS,), 0, PROMPTS), jax.random.fold_in(streams_of[4], 1), 0, PROMPTS - 1).astype(jnp.int32)
    rewards = normal_values(streams_of[5], (ROWS,), 1.0, 5.0, ((0, 128),), jnp.float32)
    gate_weight = normal_values(streams_of[6], (D, FF), D ** -0.5, 0.09375, ((0, 8), (1, 16)))
    up_weight = normal_values(streams_of[7], (D, FF), D ** -0.5, 0.09375, ((0, 8), (1, 16)))
    down_weight = normal_values(streams_of[8], (FF, D), FF ** -0.5, 0.046875, ((0, 16), (1, 8)))
    return {"roll_hidden": roll_hidden, "roll_cotangent": roll_cotangent, "lengths": lengths, "owners": owners, "prompts": prompts, "rewards": rewards, "gate_weight": gate_weight, "up_weight": up_weight, "down_weight": down_weight}


spread_floor = 0.7

def row_weights(lengths, prompts, rewards, count_prompts):
    onehot = (prompts[:, None] == jnp.arange(count_prompts, dtype=jnp.int32)[None, :]).astype(jnp.float32)
    counts = jnp.maximum(lax.optimization_barrier(jnp.sum(onehot, 0)), 1.0)
    means = lax.optimization_barrier(jnp.sum(onehot * rewards[:, None], 0)) / counts
    centred = rewards - lax.optimization_barrier(jnp.sum(onehot * means[None, :], 1))
    spreads = jnp.sqrt(lax.optimization_barrier(jnp.sum(onehot * (centred * centred)[:, None], 0)) / counts)
    divisor = jnp.maximum(lax.optimization_barrier(jnp.sum(onehot * spreads[None, :], 1)), spread_floor)
    return centred / divisor / lengths.astype(jnp.float32)

def row_offsets(lengths, owners):
    count = lengths.shape[0]
    places = jnp.arange(count, dtype=jnp.int32)
    earlier = (owners[None, :] == owners[:, None]) & (places[None, :] < places[:, None])
    return lax.optimization_barrier(jnp.sum(jnp.where(earlier, lengths[None, :], 0), 1)).astype(jnp.int32)

def block_sum(left, right, blocks, transpose_right):
    width = left.shape[1] // blocks
    total = None
    for index in range(blocks):
        piece = left[:, index * width:(index + 1) * width]
        if transpose_right:
            other = right[:, index * width:(index + 1) * width]
            term = lax.dot_general(piece, other, (((1,), (1,)), ((), ())), preferred_element_type=jnp.float32)
        else:
            other = right[index * width:(index + 1) * width, :]
            term = jnp.dot(piece, other, preferred_element_type=jnp.float32)
        term = lax.optimization_barrier(term.astype(jnp.bfloat16)).astype(jnp.float32)
        total = term if total is None else total + term
    return total

def reference(roll_hidden, roll_cotangent, lengths, owners, prompts, rewards, gate_weight, up_weight, down_weight):
    weight = row_weights(lengths, prompts, rewards, PROMPTS)
    offsets = row_offsets(lengths, owners)
    slots = jnp.arange(MAXLEN, dtype=jnp.int32)
    live = slots[None, :] < lengths[:, None]
    target = jnp.where(live, owners[:, None] * CAPR + offsets[:, None] + slots[None, :], TOKENS).astype(jnp.int32)
    hidden_rows = roll_hidden.reshape(ROWS, MAXLEN, D)
    cot_rows = roll_cotangent.reshape(ROWS, MAXLEN, D).astype(jnp.float32)
    upstream = jnp.where(live[:, :, None], cot_rows * weight[:, None, None], 0.0).astype(jnp.bfloat16)
    flat_target = target.reshape(-1)
    packed = jnp.zeros((TOKENS, D), jnp.bfloat16).at[flat_target].set(hidden_rows.reshape(-1, D), mode='drop')
    packed_grad = jnp.zeros((TOKENS, D), jnp.bfloat16).at[flat_target].set(upstream.reshape(-1, D), mode='drop')
    gate = block_sum(packed, gate_weight, N_COL, False)
    upval = block_sum(packed, up_weight, N_COL, False)
    sig = jax.nn.sigmoid(gate)
    silu = gate * sig
    hidden = (silu * upval).astype(jnp.bfloat16)
    grad_hidden = block_sum(packed_grad, down_weight, N_COL, True)
    grad_gate_act = (grad_hidden * upval * sig * (1.0 + gate * (1.0 - sig))).astype(jnp.bfloat16)
    grad_up_act = (grad_hidden * silu).astype(jnp.bfloat16)
    contract_rows = (((0,), (0,)), ((), ()))
    grad_down = lax.dot_general(hidden, packed_grad, contract_rows, preferred_element_type=jnp.float32).astype(jnp.bfloat16)
    grad_gate = lax.dot_general(packed, grad_gate_act, contract_rows, preferred_element_type=jnp.float32).astype(jnp.bfloat16)
    grad_up = lax.dot_general(packed, grad_up_act, contract_rows, preferred_element_type=jnp.float32).astype(jnp.bfloat16)
    contract_cols = (((1,), (1,)), ((), ()))
    grad_input = lax.dot_general(grad_gate_act, gate_weight, contract_cols, preferred_element_type=jnp.float32)
    grad_input = grad_input + lax.dot_general(grad_up_act, up_weight, contract_cols, preferred_element_type=jnp.float32)
    return (grad_input.astype(jnp.bfloat16), grad_gate, grad_up, grad_down)
```

```python
import jax
import jax.numpy as jnp
from jax import lax
from jax.experimental import pallas as pl
from jax.experimental.pallas import tpu as pltpu
from jax.sharding import PartitionSpec as P

CAPR = 128
OWNERS = 16
PER_OWNER = 8
PROMPTS = 16
SLOTS = 48
spread_floor = 0.7
BF = jnp.bfloat16
F32 = jnp.float32

X_UP = [(i, ((i // 2 + 1) % 4) * 2 + i % 2) for i in range(8)]
X_DOWN = [(i, ((i // 2 + 3) % 4) * 2 + i % 2) for i in range(8)]
Y_LO = [(i, i ^ 1) for i in range(8)]
Z_UP = [(i, ((i // 4 + 1) % 4) * 4 + i % 4) for i in range(16)]
Z_DOWN = [(i, ((i // 4 + 3) % 4) * 4 + i % 4) for i in range(16)]
Y_HI = [(i, i ^ 2) for i in range(16)]
CORE = [(i, i ^ 1) for i in range(16)]


def col(value, pairs):
    return lax.ppermute(value, "col", pairs)


def row(value, pairs):
    return lax.ppermute(value, "row", pairs)


def add(*terms):
    total = terms[0].astype(F32)
    for term in terms[1:]:
        total = total + term.astype(F32)
    return total


def row_weights(lengths, prompts, rewards):
    onehot = (prompts[:, None] == jnp.arange(PROMPTS, dtype=jnp.int32)[None, :]).astype(F32)
    counts = jnp.maximum(jnp.sum(onehot, 0), 1.0)
    means = jnp.sum(onehot * rewards[:, None], 0) / counts
    centred = rewards - jnp.sum(onehot * means[None, :], 1)
    spreads = jnp.sqrt(jnp.sum(onehot * (centred * centred)[:, None], 0) / counts)
    divisor = jnp.maximum(jnp.sum(onehot * spreads[None, :], 1), spread_floor)
    return centred / divisor / lengths.astype(F32)


def pack_kernel(weighted, rows_ref, weight_ref, target_ref, table_ref, out_ref, held):
    step = pl.program_id(0)
    for k in range(PER_OWNER):
        block = table_ref[rows_ref[step * PER_OWNER + k]]
        if weighted:
            block = (block.astype(F32) * weight_ref[step * PER_OWNER + k]).astype(BF)
        held[k * SLOTS : (k + 1) * SLOTS, :] = block
    places = lax.broadcasted_iota(jnp.int32, (CAPR, PER_OWNER * SLOTS), 0)
    onehot = (places == target_ref[0]).astype(F32).astype(BF)
    out_ref[...] = jnp.dot(onehot, held[...], preferred_element_type=F32).astype(BF)


def pack(rows, weights, targets, table, weighted):
    width = table.shape[2]
    return pl.pallas_call(
        lambda *refs: pack_kernel(weighted, *refs),
        grid_spec=pltpu.PrefetchScalarGridSpec(
            num_scalar_prefetch=2,
            grid=(OWNERS,),
            in_specs=[
                pl.BlockSpec((1, 1, PER_OWNER * SLOTS), lambda s, *_: (s, 0, 0)),
                pl.BlockSpec(table.shape, lambda s, *_: (0, 0, 0)),
            ],
            out_specs=pl.BlockSpec((CAPR, width), lambda s, *_: (s, 0)),
            scratch_shapes=[pltpu.VMEM((PER_OWNER * SLOTS, width), BF)],
        ),
        out_shape=jax.ShapeDtypeStruct((OWNERS * CAPR, width), BF),
        compiler_params=pltpu.CompilerParams(vmem_limit_bytes=40 << 20),
        cost_estimate=pl.CostEstimate(
            flops=2 * 2048 * 384 * 512, bytes_accessed=9 << 20, transcendentals=0
        ),
    )(rows, weights, targets, table)


def gathered_rows(piece):
    pair = jnp.stack([piece, row(piece, Y_HI)])
    below = row(pair, Z_UP)
    above = row(pair, Z_DOWN)
    far0 = row(below[0], Z_UP)
    far1 = row(above[1], Z_DOWN)
    mine = jnp.concatenate([pair, above, far0[None], far1[None], below])
    return jnp.concatenate([mine, row(mine, CORE)])


def per_device(
    roll_hidden,
    roll_cotangent,
    lengths,
    owners,
    prompts,
    rewards,
    gate_weight,
    up_weight,
    down_weight,
):
    slot_count, full = roll_hidden.shape
    cols = lax.axis_size("col")
    width = full // cols
    r_at, c_at = lax.axis_index("row"), lax.axis_index("col")

    high = lax.reduce_precision(rewards, 8, 7)
    middle = lax.reduce_precision(rewards - high, 8, 7)
    low = rewards - high - middle
    numbers = jnp.stack(
        [lengths.astype(F32), owners.astype(F32), prompts.astype(F32), high, middle, low], axis=1
    )
    numbers = jnp.pad(numbers.astype(BF), ((0, SLOTS - slot_count - 1), (0, width - 6)))
    numbers = jnp.broadcast_to(numbers[None], (cols, SLOTS - slot_count, width))

    def blocks(array):
        return jnp.moveaxis(array.reshape(slot_count, cols, width), 1, 0)

    both = jnp.concatenate(
        [
            blocks(roll_hidden),
            numbers,
            blocks(roll_cotangent),
            jnp.zeros((cols, SLOTS - slot_count, width), BF),
        ],
        axis=1,
    )
    both = lax.all_to_all(both, "col", 0, 0, tiled=True)
    hidden_piece, grad_piece = both[:, :SLOTS], both[:, SLOTS:]

    told = both[:, slot_count, :8].astype(F32)
    told = lax.all_to_all(
        jnp.broadcast_to(told[None], (OWNERS, cols, 8)), "row", 0, 0, tiled=True
    ).reshape(OWNERS * cols, 8)
    all_lengths = told[:, 0].astype(jnp.int32)
    all_owners = told[:, 1].astype(jnp.int32)
    all_prompts = told[:, 2].astype(jnp.int32)
    weights = row_weights(all_lengths, all_prompts, told[:, 3] + told[:, 4] + told[:, 5])
    ids = jnp.arange(OWNERS * cols, dtype=jnp.int32)
    earlier = (all_owners[None, :] == all_owners[:, None]) & (ids[None, :] < ids[:, None])
    offsets = jnp.sum(jnp.where(earlier, all_lengths[None, :], 0), 1)
    ranks = jnp.sum(earlier.astype(jnp.int32), 1)
    from_row = ids // cols
    place = (
        ((from_row % 2) ^ (r_at % 2)) * 8
        + ((from_row // 4 - r_at // 4) % 4) * 2
        + ((from_row // 2 % 2) ^ (r_at // 2 % 2))
    ) * cols + ids % cols
    spot = (
        ((all_owners // 4 - c_at // 2) % 4) * 4
        + ((all_owners // 2 % 2) ^ (c_at % 2)) * 2
        + all_owners % 2
    ) * PER_OWNER + ranks
    chosen = spot[None, :] == ids[:, None]

    def sort(values):
        return jnp.sum(jnp.where(chosen, values[None, :], 0), 1)

    rows_x, lengths_x, offsets_x, weights_x = (
        sort(place),
        sort(all_lengths),
        sort(offsets),
        sort(weights),
    )
    slots = jnp.arange(SLOTS, dtype=jnp.int32)[None, :]
    targets_x = jnp.where(slots < lengths_x[:, None], offsets_x[:, None] + slots, -1)
    targets_x = targets_x.reshape(OWNERS, 1, PER_OWNER * SLOTS)

    def halves_first(array):
        tail = array.shape[1:]
        n = array.shape[0] // 8
        return jnp.swapaxes(array.reshape(4, 2, n, *tail), 0, 1).reshape(array.shape)

    hidden_table = gathered_rows(hidden_piece).reshape(-1, SLOTS, width)
    grad_table = gathered_rows(grad_piece).reshape(-1, SLOTS, width)
    packed = pack(rows_x, weights_x, targets_x, hidden_table, False)
    packed_grad = pack(
        halves_first(rows_x), halves_first(weights_x), halves_first(targets_x), grad_table, True
    )

    def first(weight, tokens):
        out = lax.dot_general(weight, tokens, (((0,), (1,)), ((), ())), preferred_element_type=F32)
        return out.astype(BF)

    chunk = [packed[d * 512 : (d + 1) * 512] for d in range(4)]
    gate_2, up_2 = first(gate_weight, chunk[2]), first(up_weight, chunk[2])
    gate_far, up_far = col(gate_2, X_UP), col(up_2, X_DOWN)
    up_from_below = col(first(up_weight, chunk[1]), X_UP)
    gate_from_above = col(first(gate_weight, chunk[3]), X_DOWN)
    gate_from_below = col(add(first(gate_weight, chunk[1]), gate_far).astype(BF), X_UP)
    up_from_above = col(add(first(up_weight, chunk[3]), up_far).astype(BF), X_DOWN)
    gate_sum = add(first(gate_weight, chunk[0]), gate_from_above, gate_from_below)
    up_sum = add(first(up_weight, chunk[0]), up_from_below, up_from_above)
    gate_other = col(gate_sum[:, 256:].astype(BF), Y_LO)
    up_other = col(up_sum[:, 256:].astype(BF), Y_LO)

    def last(tokens):
        out = lax.dot_general(
            down_weight, tokens, (((1,), (1,)), ((), ())), preferred_element_type=F32
        )
        return out.astype(BF)

    grad_other = col(last(packed_grad[1024:]), Y_LO)
    grad_pair = add(last(packed_grad[:1024]), grad_other).astype(BF)
    piece = [grad_pair[:, d * 256 : (d + 1) * 256] for d in range(4)]
    far_a, far_b = col(piece[2][:, :128], X_UP), col(piece[2][:, 128:], X_DOWN)
    send_up = jnp.concatenate([add(piece[1][:, :128], far_a).astype(BF), piece[1][:, 128:]], 1)
    send_down = jnp.concatenate([piece[3][:, :128], add(piece[3][:, 128:], far_b).astype(BF)], 1)
    grad_hidden = add(piece[0], col(send_up, X_UP), col(send_down, X_DOWN))

    gate = add(gate_sum[:, :256], gate_other)
    upval = add(up_sum[:, :256], up_other)
    sig = jax.nn.sigmoid(gate)
    silu = gate * sig
    hidden = (silu * upval).astype(BF)
    grad_gate_act = (grad_hidden * upval * sig * (1.0 + gate * (1.0 - sig))).astype(BF)
    grad_up_act = (grad_hidden * silu).astype(BF)

    below, above = col(hidden, X_UP), col(hidden, X_DOWN)
    far = [col(below[:, :128], X_UP), col(above[:, 128:], X_DOWN)]
    hidden_x = jnp.concatenate([hidden, above, *far, below], 1)
    hidden_all = jnp.concatenate([hidden_x, col(hidden_x, Y_LO)], 1)

    gate_pair = jnp.concatenate([grad_gate_act, col(grad_gate_act, Y_LO)], 1)
    up_pair = jnp.concatenate([grad_up_act, col(grad_up_act, Y_LO)], 1)
    gate_below, up_above = col(gate_pair, X_UP), col(up_pair, X_DOWN)
    up_below, gate_above = col(up_pair, X_UP), col(gate_pair, X_DOWN)
    gate_two, up_two = col(gate_below, X_UP), col(up_above, X_DOWN)
    gate_chunks = [gate_pair, gate_above, gate_two, gate_below]
    up_chunks = [up_pair, up_above, up_two, up_below]

    grad_down = jnp.dot(hidden_all, packed_grad, preferred_element_type=F32).astype(BF)

    def weight_grad(chunks):
        act = jnp.concatenate(chunks, 1)
        out = lax.dot_general(packed, act, (((0,), (1,)), ((), ())), preferred_element_type=F32)
        return out.astype(BF)

    def input_grad(gate_part, up_part):
        dims = (((0,), (1,)), ((), ()))
        out = lax.dot_general(gate_part, gate_weight, dims, preferred_element_type=F32)
        return (
            out + lax.dot_general(up_part, up_weight, dims, preferred_element_type=F32)
        ).astype(BF)

    tiles = jnp.stack([input_grad(g, u) for g, u in zip(gate_chunks, up_chunks)])
    tiles = tiles.reshape(4, 2, 2 * CAPR, width)
    tiles = jnp.where(c_at % 2 == 1, tiles[:, ::-1], tiles)
    tiles = lax.dynamic_slice_in_dim(jnp.concatenate([tiles, tiles]), (4 - c_at // 2) % 4, 4, 0)
    tiles = lax.all_to_all(tiles.reshape(OWNERS, CAPR, width), "row", 0, 0, tiled=True)
    grad_input = jnp.sum(tiles.astype(F32), axis=0).astype(BF)
    return grad_input, weight_grad(gate_chunks), weight_grad(up_chunks), grad_down


def solution(mesh):
    return jax.shard_map(
        per_device,
        mesh=mesh,
        in_specs=(
            P(("row", "col"), None),
            P(("row", "col"), None),
            P(("row", "col")),
            P(("row", "col")),
            P(("row", "col")),
            P(("row", "col")),
            P("col", "row"),
            P("col", "row"),
            P("row", "col"),
        ),
        out_specs=(P("row", "col"), P("col", "row"), P("col", "row"), P("row", "col")),
        check_vma=False,
    )
```

```python
import jax
import jax.numpy as jnp
from jax import lax
from jax.experimental import pallas as pl
from jax.experimental.pallas import tpu as pltpu
from jax.sharding import PartitionSpec as P

CAPR = 128
OWNERS = 16
PER_OWNER = 8
PROMPTS = 16
SLOTS = 48
spread_floor = 0.7
BF = jnp.bfloat16
F32 = jnp.float32

X_UP = [(i, ((i // 2 + 1) % 4) * 2 + i % 2) for i in range(8)]
X_DOWN = [(i, ((i // 2 + 3) % 4) * 2 + i % 2) for i in range(8)]
Y_LO = [(i, i ^ 1) for i in range(8)]
Z_UP = [(i, ((i // 4 + 1) % 4) * 4 + i % 4) for i in range(16)]
Z_DOWN = [(i, ((i // 4 + 3) % 4) * 4 + i % 4) for i in range(16)]
Y_HI = [(i, i ^ 2) for i in range(16)]
CORE = [(i, i ^ 1) for i in range(16)]


def after(value, *earlier):
    return lax.optimization_barrier((value, *earlier))[0]


class Link:
    def __init__(self, axis, pairs, most=2):
        self.axis, self.pairs, self.most, self.got = axis, pairs, most, []

    def __call__(self, value):
        if len(self.got) >= self.most:
            value = after(value, self.got[-self.most])
        self.got.append(lax.ppermute(value, self.axis, self.pairs))
        return self.got[-1]


def add(*terms):
    total = terms[0].astype(F32)
    for term in terms[1:]:
        total = total + term.astype(F32)
    return total


def row_weights(lengths, prompts, rewards):
    onehot = (prompts[:, None] == jnp.arange(PROMPTS, dtype=jnp.int32)[None, :]).astype(F32)
    counts = jnp.maximum(jnp.sum(onehot, 0), 1.0)
    means = jnp.sum(onehot * rewards[:, None], 0) / counts
    centred = rewards - jnp.sum(onehot * means[None, :], 1)
    spreads = jnp.sqrt(jnp.sum(onehot * (centred * centred)[:, None], 0) / counts)
    divisor = jnp.maximum(jnp.sum(onehot * spreads[None, :], 1), spread_floor)
    return centred / divisor / lengths.astype(F32)


def pack_kernel(weighted, rows_ref, weight_ref, target_ref, table_ref, out_ref, held):
    step = pl.program_id(0)
    for k in range(PER_OWNER):
        block = table_ref[rows_ref[step * PER_OWNER + k]]
        if weighted:
            block = (block.astype(F32) * weight_ref[step * PER_OWNER + k]).astype(BF)
        held[k * SLOTS : (k + 1) * SLOTS, :] = block
    places = lax.broadcasted_iota(jnp.int32, (CAPR, PER_OWNER * SLOTS), 0)
    onehot = (places == target_ref[0]).astype(F32).astype(BF)
    out_ref[...] = jnp.dot(onehot, held[...], preferred_element_type=F32).astype(BF)


def pack(rows, weights, targets, table, weighted):
    width = table.shape[2]
    return pl.pallas_call(
        lambda *refs: pack_kernel(weighted, *refs),
        grid_spec=pltpu.PrefetchScalarGridSpec(
            num_scalar_prefetch=2,
            grid=(OWNERS,),
            in_specs=[
                pl.BlockSpec((1, 1, PER_OWNER * SLOTS), lambda s, *_: (s, 0, 0)),
                pl.BlockSpec(table.shape, lambda s, *_: (0, 0, 0)),
            ],
            out_specs=pl.BlockSpec((CAPR, width), lambda s, *_: (s, 0)),
            scratch_shapes=[pltpu.VMEM((PER_OWNER * SLOTS, width), BF)],
        ),
        out_shape=jax.ShapeDtypeStruct((OWNERS * CAPR, width), BF),
        compiler_params=pltpu.CompilerParams(vmem_limit_bytes=40 << 20),
        cost_estimate=pl.CostEstimate(
            flops=2 * 2048 * 384 * 512, bytes_accessed=9 << 20, transcendentals=0
        ),
    )(rows, weights, targets, table)


def gathered_rows(piece, z_up, z_down, y_hi, core):
    other = y_hi(piece)
    below, above = z_up(piece), z_down(piece)
    first = core(jnp.concatenate([piece, other]))
    below_other, above_other = z_up(other), z_down(other)
    second = core(jnp.concatenate([above, below]))
    far, far_other = z_up(below), z_down(above_other)
    third = core(jnp.concatenate([above_other, below_other]))
    fourth = core(jnp.concatenate([far, far_other]))
    n = piece.shape[0]
    mine = [piece, other, above, above_other, far, far_other, below, below_other]
    theirs = [first[:n], first[n:], second[:n], third[:n]]
    theirs += [fourth[:n], fourth[n:], second[n:], third[n:]]
    return jnp.concatenate(mine + theirs), other


def per_device(
    roll_hidden,
    roll_cotangent,
    lengths,
    owners,
    prompts,
    rewards,
    gate_weight,
    up_weight,
    down_weight,
):
    slot_count, full = roll_hidden.shape
    cols = lax.axis_size("col")
    width = full // cols
    r_at, c_at = lax.axis_index("row"), lax.axis_index("col")

    high = lax.reduce_precision(rewards, 8, 7)
    middle = lax.reduce_precision(rewards - high, 8, 7)
    low = rewards - high - middle
    numbers = jnp.stack(
        [lengths.astype(F32), owners.astype(F32), prompts.astype(F32), high, middle, low], axis=1
    )
    numbers = jnp.pad(numbers.astype(BF), ((0, SLOTS - slot_count - 1), (0, width - 6)))
    numbers = jnp.broadcast_to(numbers[None], (cols, SLOTS - slot_count, width))

    def blocks(array):
        return jnp.moveaxis(array.reshape(slot_count, cols, width), 1, 0)

    both = jnp.concatenate(
        [
            blocks(roll_hidden),
            numbers,
            blocks(roll_cotangent),
            jnp.zeros((cols, SLOTS - slot_count, width), BF),
        ],
        axis=1,
    )
    both = lax.all_to_all(both, "col", 0, 0, tiled=True)
    hidden_piece, grad_piece = both[:, :SLOTS], both[:, SLOTS:]

    z_up, z_down, core = Link("row", Z_UP), Link("row", Z_DOWN), Link("row", CORE)
    y_hi = Link("row", Y_HI, 1)
    hidden_table, other = gathered_rows(hidden_piece, z_up, z_down, y_hi, core)
    grad_table, _ = gathered_rows(grad_piece, z_up, z_down, y_hi, core)

    told = after(both[:, slot_count, :8].astype(F32), other)
    told = lax.all_to_all(
        jnp.broadcast_to(told[None], (OWNERS, cols, 8)), "row", 0, 0, tiled=True
    ).reshape(OWNERS * cols, 8)
    all_lengths = told[:, 0].astype(jnp.int32)
    all_owners = told[:, 1].astype(jnp.int32)
    all_prompts = told[:, 2].astype(jnp.int32)
    weights = row_weights(all_lengths, all_prompts, told[:, 3] + told[:, 4] + told[:, 5])
    ids = jnp.arange(OWNERS * cols, dtype=jnp.int32)
    earlier = (all_owners[None, :] == all_owners[:, None]) & (ids[None, :] < ids[:, None])
    offsets = jnp.sum(jnp.where(earlier, all_lengths[None, :], 0), 1)
    ranks = jnp.sum(earlier.astype(jnp.int32), 1)
    from_row = ids // cols
    place = (
        ((from_row % 2) ^ (r_at % 2)) * 8
        + ((from_row // 4 - r_at // 4) % 4) * 2
        + ((from_row // 2 % 2) ^ (r_at // 2 % 2))
    ) * cols + ids % cols
    spot = (
        ((all_owners // 4 - c_at // 2) % 4) * 4
        + ((all_owners // 2 % 2) ^ (c_at % 2)) * 2
        + all_owners % 2
    ) * PER_OWNER + ranks
    chosen = spot[None, :] == ids[:, None]

    def sort(values):
        return jnp.sum(jnp.where(chosen, values[None, :], 0), 1)

    sorted_rows, sorted_weights = sort(place), sort(weights)
    sorted_lengths, sorted_offsets = sort(all_lengths)[:, None], sort(offsets)[:, None]
    slots = jnp.arange(SLOTS, dtype=jnp.int32)[None, :]
    targets = jnp.where(slots < sorted_lengths, sorted_offsets + slots, -1)
    targets = targets.reshape(OWNERS, 1, PER_OWNER * SLOTS)
    packed = pack(sorted_rows, sorted_weights, targets, hidden_table, False)
    packed_grad = pack(sorted_rows, sorted_weights, targets, grad_table, True)

    def first(weight, tokens, d, h):
        part = tokens[(d * 2 + h) * 256 : (d * 2 + h + 1) * 256]
        dims = (((0 if tokens is packed else 1,), (1,)), ((), ()))
        return lax.dot_general(weight, part, dims, preferred_element_type=F32).astype(BF)

    x_up, x_down, y_lo = Link("col", X_UP), Link("col", X_DOWN), Link("col", Y_LO)

    def x_first(weight, tokens):
        far_0, far_1 = (
            x_up(first(weight, tokens, 2, 0)),
            x_down(first(weight, tokens, 2, 1)),
        )
        below_1, above_0 = (
            x_up(first(weight, tokens, 1, 1)),
            x_down(first(weight, tokens, 3, 0)),
        )
        below_0 = x_up(add(first(weight, tokens, 1, 0), far_0).astype(BF))
        above_1 = x_down(add(first(weight, tokens, 3, 1), far_1).astype(BF))
        return (
            add(first(weight, tokens, 0, 0), below_0, above_0),
            add(first(weight, tokens, 0, 1), below_1, above_1),
        )

    gate_2 = y_lo(first(gate_weight, packed, 2, 1))
    up_mine, up_others = x_first(up_weight, packed)
    gate_13 = y_lo(
        jnp.concatenate(
            [first(gate_weight, packed, 1, 1), first(gate_weight, packed, 3, 1)], 1
        )
    )
    gate_0 = y_lo(first(gate_weight, packed, 0, 1))
    upval = add(up_mine, y_lo(up_others.astype(BF)))
    grad_mine, grad_others = x_first(down_weight, packed_grad)
    grad_hidden = add(grad_mine, y_lo(grad_others.astype(BF)))
    gate_2 = add(first(gate_weight, packed, 2, 0), gate_2).astype(BF)
    far_a, far_b = x_up(gate_2[:, :128]), x_down(gate_2[:, 128:])
    gate_1 = add(first(gate_weight, packed, 1, 0), gate_13[:, :256])
    gate_3 = add(first(gate_weight, packed, 3, 0), gate_13[:, 256:])
    gate_1 = jnp.concatenate([add(gate_1[:, :128], far_a), gate_1[:, 128:]], 1).astype(BF)
    gate_3 = jnp.concatenate([gate_3[:, :128], add(gate_3[:, 128:], far_b)], 1).astype(BF)
    gate = add(first(gate_weight, packed, 0, 0), gate_0, x_up(gate_1), x_down(gate_3))

    sig = jax.nn.sigmoid(gate)
    silu = gate * sig
    hidden = (silu * upval).astype(BF)
    grad_gate_act = (grad_hidden * upval * sig * (1.0 + gate * (1.0 - sig))).astype(BF)
    grad_up_act = (grad_hidden * silu).astype(BF)

    up_below, up_above = x_up(grad_up_act), x_down(grad_up_act)
    gate_y = y_lo(grad_gate_act)
    gate_below, gate_above = x_up(grad_gate_act), x_down(grad_gate_act)
    up_far = jnp.concatenate([x_up(up_below[:, :128]), x_down(up_above[:, 128:])], 1)
    up_y = y_lo(grad_up_act)
    gate_y_below, gate_y_above = x_up(gate_y), x_down(gate_y)
    up_y_near = y_lo(jnp.concatenate([up_below, up_above], 1))
    gate_far, gate_y_far = x_up(gate_below), x_down(gate_y_above)
    up_y_far = y_lo(up_far)
    gate_chunks = [
        [grad_gate_act, gate_y],
        [gate_above, gate_y_above],
        [gate_far, gate_y_far],
        [gate_below, gate_y_below],
    ]
    up_chunks = [
        [grad_up_act, up_y],
        [up_above, up_y_near[:, 256:]],
        [up_far, up_y_far],
        [up_below, up_y_near[:, :256]],
    ]
    hidden_below, hidden_above = x_up(hidden), x_down(hidden)
    hidden_y = y_lo(hidden)
    hidden_y_below, hidden_y_above = x_up(hidden_y), x_down(hidden_y)
    hidden_far, hidden_y_far = x_up(hidden_below), x_down(hidden_y_above)
    hidden_chunks = [
        [hidden, hidden_y],
        [hidden_above, hidden_y_above],
        [hidden_far, hidden_y_far],
        [hidden_below, hidden_y_below],
    ]

    def whole(chunks):
        return jnp.concatenate([part for pair in chunks for part in pair], 1)

    gate_chunks, up_chunks = whole(gate_chunks), whole(up_chunks)
    hidden_all = whole(hidden_chunks)

    grad_down = jnp.dot(hidden_all, packed_grad, preferred_element_type=F32).astype(BF)

    def weight_grad(act):
        out = lax.dot_general(packed, act, (((0,), (1,)), ((), ())), preferred_element_type=F32)
        return out.astype(BF)

    dims = (((0,), (1,)), ((), ()))
    tiles = lax.dot_general(gate_chunks, gate_weight, dims, preferred_element_type=F32)
    tiles = tiles + lax.dot_general(up_chunks, up_weight, dims, preferred_element_type=F32)
    tiles = tiles.astype(BF)
    tiles = tiles.reshape(4, 2, 2 * CAPR, width)
    tiles = jnp.where(c_at % 2 == 1, tiles[:, ::-1], tiles)
    tiles = lax.dynamic_slice_in_dim(jnp.concatenate([tiles, tiles]), (4 - c_at // 2) % 4, 4, 0)
    tiles = lax.all_to_all(tiles.reshape(OWNERS, CAPR, width), "row", 0, 0, tiled=True)
    grad_input = jnp.sum(tiles.astype(F32), axis=0).astype(BF)
    return grad_input, weight_grad(gate_chunks), weight_grad(up_chunks), grad_down


def solution(mesh):
    return jax.shard_map(
        per_device,
        mesh=mesh,
        in_specs=(
            P(("row", "col"), None),
            P(("row", "col"), None),
            P(("row", "col")),
            P(("row", "col")),
            P(("row", "col")),
            P(("row", "col")),
            P("col", "row"),
            P("col", "row"),
            P("row", "col"),
        ),
        out_specs=(P("row", "col"), P("col", "row"), P("col", "row"), P("row", "col")),
        check_vma=False,
    )
```

```python
import jax
import jax.numpy as jnp
from jax import lax
from jax.experimental import pallas as pl
from jax.experimental.pallas import tpu as pltpu
from jax.sharding import PartitionSpec as P

CAPR = 128
OWNERS = 16
PER_OWNER = 8
PROMPTS = 16
SLOTS = 48
spread_floor = 0.7
BF = jnp.bfloat16
F32 = jnp.float32

X_UP = [(i, ((i // 2 + 1) % 4) * 2 + i % 2) for i in range(8)]
X_DOWN = [(i, ((i // 2 + 3) % 4) * 2 + i % 2) for i in range(8)]
Y_LO = [(i, i ^ 1) for i in range(8)]
Z_UP = [(i, ((i // 4 + 1) % 4) * 4 + i % 4) for i in range(16)]
Z_DOWN = [(i, ((i // 4 + 3) % 4) * 4 + i % 4) for i in range(16)]
Y_HI = [(i, i ^ 2) for i in range(16)]
CORE = [(i, i ^ 1) for i in range(16)]


def after(value, *earlier):
    return lax.optimization_barrier((value, *earlier))[0]


class Link:
    def __init__(self, axis, pairs, most=2):
        self.axis, self.pairs, self.most, self.got = axis, pairs, most, []

    def __call__(self, value):
        if len(self.got) >= self.most:
            value = after(value, self.got[-self.most])
        self.got.append(lax.ppermute(value, self.axis, self.pairs))
        return self.got[-1]


def add(*terms):
    total = terms[0].astype(F32)
    for term in terms[1:]:
        total = total + term.astype(F32)
    return total


def row_weights(lengths, prompts, rewards):
    onehot = (prompts[:, None] == jnp.arange(PROMPTS, dtype=jnp.int32)[None, :]).astype(F32)
    counts = jnp.maximum(jnp.sum(onehot, 0), 1.0)
    means = jnp.sum(onehot * rewards[:, None], 0) / counts
    centred = rewards - jnp.sum(onehot * means[None, :], 1)
    spreads = jnp.sqrt(jnp.sum(onehot * (centred * centred)[:, None], 0) / counts)
    divisor = jnp.maximum(jnp.sum(onehot * spreads[None, :], 1), spread_floor)
    return centred / divisor / lengths.astype(F32)


def pack_kernel(weighted, rows_ref, weight_ref, target_ref, table_ref, out_ref, held):
    step = pl.program_id(0)
    for k in range(PER_OWNER):
        block = table_ref[rows_ref[step * PER_OWNER + k]]
        if weighted:
            block = (block.astype(F32) * weight_ref[step * PER_OWNER + k]).astype(BF)
        held[k * SLOTS : (k + 1) * SLOTS, :] = block
    places = lax.broadcasted_iota(jnp.int32, (CAPR, PER_OWNER * SLOTS), 0)
    onehot = (places == target_ref[0]).astype(F32).astype(BF)
    out_ref[...] = jnp.dot(onehot, held[...], preferred_element_type=F32).astype(BF)


def pack(rows, weights, targets, table, weighted):
    width = table.shape[2]
    return pl.pallas_call(
        lambda *refs: pack_kernel(weighted, *refs),
        grid_spec=pltpu.PrefetchScalarGridSpec(
            num_scalar_prefetch=2,
            grid=(OWNERS,),
            in_specs=[
                pl.BlockSpec((1, 1, PER_OWNER * SLOTS), lambda s, *_: (s, 0, 0)),
                pl.BlockSpec(table.shape, lambda s, *_: (0, 0, 0)),
            ],
            out_specs=pl.BlockSpec((CAPR, width), lambda s, *_: (s, 0)),
            scratch_shapes=[pltpu.VMEM((PER_OWNER * SLOTS, width), BF)],
        ),
        out_shape=jax.ShapeDtypeStruct((OWNERS * CAPR, width), BF),
        compiler_params=pltpu.CompilerParams(vmem_limit_bytes=40 << 20),
        cost_estimate=pl.CostEstimate(
            flops=2 * 2048 * 384 * 512, bytes_accessed=9 << 20, transcendentals=0
        ),
    )(rows, weights, targets, table)


def gathered_rows(piece, z_up, z_down, y_hi, core):
    other = y_hi(piece)
    below, above = z_up(piece), z_down(piece)
    first = core(jnp.concatenate([piece, other]))
    below_other, above_other = z_up(other), z_down(other)
    second = core(jnp.concatenate([above, below]))
    far, far_other = z_up(below), z_down(above_other)
    third = core(jnp.concatenate([above_other, below_other]))
    fourth = core(jnp.concatenate([far, far_other]))
    n = piece.shape[0]
    mine = [piece, other, above, above_other, far, far_other, below, below_other]
    theirs = [first[:n], first[n:], second[:n], third[:n]]
    theirs += [fourth[:n], fourth[n:], second[n:], third[n:]]
    return jnp.concatenate(mine + theirs), (far, far_other)


def per_device(
    roll_hidden,
    roll_cotangent,
    lengths,
    owners,
    prompts,
    rewards,
    gate_weight,
    up_weight,
    down_weight,
):
    slot_count, full = roll_hidden.shape
    cols = lax.axis_size("col")
    width = full // cols
    r_at, c_at = lax.axis_index("row"), lax.axis_index("col")

    high = lax.reduce_precision(rewards, 8, 7)
    middle = lax.reduce_precision(rewards - high, 8, 7)
    low = rewards - high - middle
    numbers = jnp.stack(
        [lengths.astype(F32), owners.astype(F32), prompts.astype(F32), high, middle, low], axis=1
    )
    numbers = jnp.pad(numbers.astype(BF), ((0, SLOTS - slot_count - 1), (0, width - 6)))
    numbers = jnp.broadcast_to(numbers[None], (cols, SLOTS - slot_count, width))

    def blocks(array):
        return jnp.moveaxis(array.reshape(slot_count, cols, width), 1, 0)

    both = jnp.concatenate(
        [
            blocks(roll_hidden),
            numbers,
            blocks(roll_cotangent),
            jnp.zeros((cols, SLOTS - slot_count, width), BF),
        ],
        axis=1,
    )
    both = lax.all_to_all(both, "col", 0, 0, tiled=True)
    hidden_piece, grad_piece = both[:, :SLOTS], both[:, SLOTS:]

    x_at, odd = c_at // 2, c_at % 2 == 1
    half = down_weight.shape[0] // 2
    x_up, x_down, y_lo = Link("col", X_UP), Link("col", X_DOWN), Link("col", Y_LO, 1)
    z_up, z_down, core = Link("row", Z_UP), Link("row", Z_DOWN), Link("row", CORE)
    y_hi = Link("row", Y_HI, 1)

    def split_units(weight, axis):
        one = lax.slice_in_dim(weight, 0, half, axis=axis)
        two = lax.slice_in_dim(weight, half, 2 * half, axis=axis)
        mine, sent = jnp.where(odd, two, one), jnp.where(odd, one, two)
        return mine, y_lo(after(sent, both))

    gate_weights = split_units(gate_weight, 1)
    up_weights = split_units(up_weight, 1)
    down_weights = split_units(down_weight, 0)

    hidden_table, sent = gathered_rows(hidden_piece, z_up, z_down, y_hi, core)
    grad_table, _ = gathered_rows(after(grad_piece, *sent), z_up, z_down, y_hi, core)

    told = hidden_table[:, slot_count, :8].astype(F32)
    all_lengths = told[:, 0].astype(jnp.int32)
    all_owners = told[:, 1].astype(jnp.int32)
    all_prompts = told[:, 2].astype(jnp.int32)
    weights = row_weights(all_lengths, all_prompts, told[:, 3] + told[:, 4] + told[:, 5])
    places = jnp.arange(OWNERS * cols, dtype=jnp.int32)
    step = places // cols
    ids = (
        ((r_at // 4 + step // 2 % 4) % 4) * 4
        + ((r_at // 2 % 2) ^ (step % 2)) * 2
        + ((r_at % 2) ^ (step // 8))
    ) * cols + places % cols
    earlier = (all_owners[None, :] == all_owners[:, None]) & (ids[None, :] < ids[:, None])
    offsets = jnp.sum(jnp.where(earlier, all_lengths[None, :], 0), 1)
    ranks = jnp.sum(earlier.astype(jnp.int32), 1)
    spot = (((all_owners // 4 - x_at) % 4) * 4 + all_owners % 4) * PER_OWNER + ranks
    chosen = spot[None, :] == places[:, None]

    def sort(values):
        return jnp.sum(jnp.where(chosen, values[None, :], 0), 1)

    sorted_rows, sorted_weights = sort(places), sort(weights)
    sorted_lengths, sorted_offsets = sort(all_lengths)[:, None], sort(offsets)[:, None]
    slots = jnp.arange(SLOTS, dtype=jnp.int32)[None, :]
    targets = jnp.where(slots < sorted_lengths, sorted_offsets + slots, -1)
    targets = targets.reshape(OWNERS, 1, PER_OWNER * SLOTS)
    packed = pack(sorted_rows, sorted_weights, targets, hidden_table, False)
    packed_grad = pack(sorted_rows, sorted_weights, targets, grad_table, True)

    def chunks_of(tokens):
        parts = [tokens[d * 512 : (d + 1) * 512] for d in range(4)]
        others = {d: y_lo(parts[d]) for d in (2, 1, 3, 0)}
        return parts, [others[d] for d in range(4)]

    def first(weights, chunks, d, axis, part=slice(None)):
        dims = (((axis,), (1,)), ((), ()))
        out = lax.dot_general(
            weights[0], chunks[0][d][part], dims, preferred_element_type=F32
        ) + lax.dot_general(weights[1], chunks[1][d][part], dims, preferred_element_type=F32)
        return out.astype(BF)

    xs = chunks_of(packed)
    gate_far = x_up(first(gate_weights, xs, 2, 0))
    up_far = x_down(first(up_weights, xs, 2, 0))
    up_below = x_up(first(up_weights, xs, 1, 0))
    gate_above = x_down(first(gate_weights, xs, 3, 0))
    gate_below = x_up(add(first(gate_weights, xs, 1, 0), gate_far).astype(BF))
    up_above = x_down(add(first(up_weights, xs, 3, 0), up_far).astype(BF))
    gate = add(first(gate_weights, xs, 0, 0), gate_below, gate_above)
    upval = add(first(up_weights, xs, 0, 0), up_below, up_above)

    gs = chunks_of(packed_grad)
    one, two = slice(0, 256), slice(256, 512)
    far_1, far_2 = (
        x_up(first(down_weights, gs, 2, 1, one)),
        x_down(first(down_weights, gs, 2, 1, two)),
    )
    below_2 = x_up(first(down_weights, gs, 1, 1, two))
    above_1 = x_down(first(down_weights, gs, 3, 1, one))
    below_1 = x_up(add(first(down_weights, gs, 1, 1, one), far_1).astype(BF))
    above_2 = x_down(add(first(down_weights, gs, 3, 1, two), far_2).astype(BF))
    grad_hidden = jnp.concatenate(
        [
            add(first(down_weights, gs, 0, 1, one), below_1, above_1),
            add(first(down_weights, gs, 0, 1, two), below_2, above_2),
        ],
        1,
    )

    sig = jax.nn.sigmoid(gate)
    silu = gate * sig
    hidden = (silu * upval).astype(BF)
    grad_gate_act = (grad_hidden * upval * sig * (1.0 + gate * (1.0 - sig))).astype(BF)
    grad_up_act = (grad_hidden * silu).astype(BF)

    gate_below, gate_above = x_up(grad_gate_act), x_down(grad_gate_act)
    up_below, up_above = x_up(grad_up_act), x_down(grad_up_act)
    gate_far, up_far = x_up(gate_below), x_down(up_above)
    hidden_below, hidden_above = x_up(hidden), x_down(hidden)
    hidden_far = [x_up(hidden_below[:, :256]), x_down(hidden_above[:, 256:])]
    gate_all = jnp.concatenate([grad_gate_act, gate_above, gate_far, gate_below], 1)
    up_all = jnp.concatenate([grad_up_act, up_above, up_far, up_below], 1)
    hidden_all = jnp.concatenate([hidden, hidden_above, *hidden_far, hidden_below], 1)

    def input_grad(at):
        dims = (((0,), (1,)), ((), ()))
        out = lax.dot_general(gate_all, gate_weights[at], dims, preferred_element_type=F32)
        out = out + lax.dot_general(up_all, up_weights[at], dims, preferred_element_type=F32)
        return out.astype(BF).reshape(4, 2, 2, CAPR, width)

    tiles = jnp.concatenate([input_grad(0), input_grad(1)], 4)
    second_core = r_at % 2 == 1
    kept = jnp.where(second_core, tiles[:, :, 1], tiles[:, :, 0])
    tiles = core(jnp.where(second_core, tiles[:, :, 0], tiles[:, :, 1]))
    tiles = add(kept, tiles).astype(BF)
    tiles = lax.dynamic_slice_in_dim(jnp.concatenate([tiles, tiles]), (4 - x_at) % 4, 4, 0)
    groups = [[i * 2 + c for i in range(OWNERS // 2)] for c in range(2)]
    tiles = lax.all_to_all(
        tiles.reshape(OWNERS // 2, CAPR, 2 * width),
        "row",
        0,
        0,
        axis_index_groups=groups,
        tiled=True,
    )
    tiles = jnp.sum(tiles.astype(F32), axis=0)

    def weight_grad(act, chunks, axis):
        mine, sent = (jnp.concatenate(parts) for parts in chunks)
        if axis == 0:
            mine, sent = (jnp.dot(act, t, preferred_element_type=F32) for t in (mine, sent))
        else:
            dims = (((0,), (1,)), ((), ()))
            mine, sent = (
                lax.dot_general(t, act, dims, preferred_element_type=F32) for t in (mine, sent)
            )
        mine, got = mine.astype(BF), y_lo(sent.astype(BF))
        return jnp.where(
            odd, jnp.concatenate([got, mine], axis), jnp.concatenate([mine, got], axis)
        )

    grad_gate = weight_grad(gate_all, xs, 1)
    grad_up = weight_grad(up_all, xs, 1)
    grad_down = weight_grad(hidden_all, gs, 0)
    grad_input = add(tiles[:, :width], y_lo(tiles[:, width:].astype(BF))).astype(BF)
    return grad_input, grad_gate, grad_up, grad_down


def solution(mesh):
    return jax.shard_map(
        per_device,
        mesh=mesh,
        in_specs=(
            P(("row", "col"), None),
            P(("row", "col"), None),
            P(("row", "col")),
            P(("row", "col")),
            P(("row", "col")),
            P(("row", "col")),
            P("col", "row"),
            P("col", "row"),
            P("row", "col"),
        ),
        out_specs=(P("row", "col"), P("col", "row"), P("col", "row"), P("row", "col")),
        check_vma=False,
    )
```

```python
import jax
import jax.numpy as jnp
from jax import lax
from jax.experimental import pallas as pl
from jax.experimental.pallas import tpu as pltpu
from jax.sharding import PartitionSpec as P

CAPR = 128
OWNERS = 16
PER_OWNER = 8
PROMPTS = 16
SLOTS = 48
spread_floor = 0.7
BF = jnp.bfloat16
F32 = jnp.float32

X_UP = [(i, ((i // 2 + 1) % 4) * 2 + i % 2) for i in range(8)]
X_DOWN = [(i, ((i // 2 + 3) % 4) * 2 + i % 2) for i in range(8)]
Y_LO = [(i, i ^ 1) for i in range(8)]
Z_UP = [(i, ((i // 4 + 1) % 4) * 4 + i % 4) for i in range(16)]
Z_DOWN = [(i, ((i // 4 + 3) % 4) * 4 + i % 4) for i in range(16)]
Y_HI = [(i, i ^ 2) for i in range(16)]
CORE = [(i, i ^ 1) for i in range(16)]


def after(value, *earlier):
    return lax.optimization_barrier((value, *earlier))[0]


class Link:
    def __init__(self, axis, pairs, most=2):
        self.axis, self.pairs, self.most, self.got = axis, pairs, most, []

    def __call__(self, value):
        if len(self.got) >= self.most:
            value = after(value, self.got[-self.most])
        self.got.append(lax.ppermute(value, self.axis, self.pairs))
        return self.got[-1]


def add(*terms):
    total = terms[0].astype(F32)
    for term in terms[1:]:
        total = total + term.astype(F32)
    return total


def row_weights(lengths, prompts, rewards):
    onehot = (prompts[:, None] == jnp.arange(PROMPTS, dtype=jnp.int32)[None, :]).astype(F32)
    counts = jnp.maximum(jnp.sum(onehot, 0), 1.0)
    means = jnp.sum(onehot * rewards[:, None], 0) / counts
    centred = rewards - jnp.sum(onehot * means[None, :], 1)
    spreads = jnp.sqrt(jnp.sum(onehot * (centred * centred)[:, None], 0) / counts)
    divisor = jnp.maximum(jnp.sum(onehot * spreads[None, :], 1), spread_floor)
    return centred / divisor / lengths.astype(F32)


def pack_kernel(weighted, spot_ref, weight_ref, target_ref, *refs):
    *pieces, out_ref, held = refs
    held[...] = jnp.zeros_like(held)
    for p, piece in enumerate(pieces):
        for k in range(PER_OWNER):
            at = p * PER_OWNER + k
            block = piece[k]
            if weighted:
                block = (block.astype(F32) * weight_ref[at]).astype(BF)
            held[pl.ds(pl.multiple_of(spot_ref[at] * SLOTS, SLOTS), SLOTS), :] = block
    span = PER_OWNER * SLOTS
    places = lax.broadcasted_iota(jnp.int32, (CAPR, span), 0)
    for owner in range(OWNERS):
        onehot = (places == target_ref[owner]).astype(F32).astype(BF)
        rows = held[owner * span : (owner + 1) * span, :]
        out_ref[owner * CAPR : (owner + 1) * CAPR, :] = jnp.dot(
            onehot, rows, preferred_element_type=F32
        ).astype(BF)


def pack(spots, weights, targets, pieces, weighted):
    width = pieces[0].shape[2]
    scalars, arrays = pl.BlockSpec(memory_space=pltpu.SMEM), pl.BlockSpec(memory_space=pltpu.VMEM)
    return pl.pallas_call(
        lambda *refs: pack_kernel(weighted, *refs),
        in_specs=[scalars, scalars] + [arrays] * (1 + len(pieces)),
        out_specs=arrays,
        out_shape=jax.ShapeDtypeStruct((OWNERS * CAPR, width), BF),
        scratch_shapes=[pltpu.VMEM((OWNERS * PER_OWNER * SLOTS, width), BF)],
        compiler_params=pltpu.CompilerParams(vmem_limit_bytes=24 << 20),
        cost_estimate=pl.CostEstimate(
            flops=2 * 2048 * 384 * 512, bytes_accessed=9 << 20, transcendentals=0
        ),
    )(spots, weights, targets, *pieces)


def gathered_rows(piece, z_up, z_down, y_hi):
    other = y_hi(piece)
    below, above = z_up(piece), z_down(piece)
    below_other, above_other = z_up(other), z_down(other)
    far, far_other = z_up(below), z_down(above_other)
    return [piece, other, above, above_other, far, far_other, below, below_other]


def per_device(
    roll_hidden,
    roll_cotangent,
    lengths,
    owners,
    prompts,
    rewards,
    gate_weight,
    up_weight,
    down_weight,
):
    slot_count, full = roll_hidden.shape
    cols = lax.axis_size("col")
    width = full // cols
    r_at, c_at = lax.axis_index("row"), lax.axis_index("col")

    high = lax.reduce_precision(rewards, 8, 7)
    middle = lax.reduce_precision(rewards - high, 8, 7)
    low = rewards - high - middle
    numbers = jnp.stack(
        [lengths.astype(F32), owners.astype(F32), prompts.astype(F32), high, middle, low], axis=1
    )
    numbers = jnp.pad(numbers.astype(BF), ((0, SLOTS - slot_count - 1), (0, width - 6)))
    numbers = jnp.broadcast_to(numbers[None], (cols, SLOTS - slot_count, width))

    def blocks(array):
        return jnp.moveaxis(array.reshape(slot_count, cols, width), 1, 0)

    both = jnp.concatenate(
        [
            blocks(roll_hidden),
            numbers,
            blocks(roll_cotangent),
            jnp.zeros((cols, SLOTS - slot_count, width), BF),
        ],
        axis=1,
    )
    both = lax.all_to_all(both, "col", 0, 0, tiled=True)
    hidden_piece, grad_piece = both[:, :SLOTS], both[:, SLOTS:]

    x_at, odd, second_core = c_at // 2, c_at % 2 == 1, r_at % 2 == 1
    x_up, x_down, y_lo = Link("col", X_UP), Link("col", X_DOWN), Link("col", Y_LO, 1)
    z_up, z_down, core = Link("row", Z_UP), Link("row", Z_DOWN), Link("row", CORE)
    y_hi = Link("row", Y_HI, 1)

    units = down_weight.shape[0] // 2
    padded = -(-units // 16) * 16

    def split_units(weight):
        halves = [
            jnp.pad(weight[k * units : (k + 1) * units], ((0, padded - units), (0, 0)))
            for k in range(2)
        ]
        return jnp.where(odd, halves[1], halves[0]), jnp.where(odd, halves[0], halves[1])

    def both_widths(*weights):
        mine, sent = (jnp.concatenate(parts) for parts in zip(*map(split_units, weights)))
        return jnp.concatenate([mine, y_lo(after(sent, both))], 1)

    gate_up_weights = both_widths(gate_weight.T, up_weight.T)
    down_weights = both_widths(down_weight)

    hidden_pieces = gathered_rows(hidden_piece, z_up, z_down, y_hi)
    grad_piece = after(grad_piece, hidden_pieces[4], hidden_pieces[5])
    grad_pieces = gathered_rows(grad_piece, z_up, z_down, y_hi)

    told = jnp.concatenate([piece[:, slot_count, :8] for piece in hidden_pieces]).astype(F32)
    told = jnp.concatenate([told, core(told)])
    all_lengths = told[:, 0].astype(jnp.int32)
    all_owners = told[:, 1].astype(jnp.int32)
    all_prompts = told[:, 2].astype(jnp.int32)
    weights = row_weights(all_lengths, all_prompts, told[:, 3] + told[:, 4] + told[:, 5])
    places = jnp.arange(OWNERS * cols, dtype=jnp.int32)
    step = places // cols
    ids = (
        ((r_at // 4 + step // 2 % 4) % 4) * 4
        + ((r_at // 2 % 2) ^ (step % 2)) * 2
        + ((r_at % 2) ^ (step // 8))
    ) * cols + places % cols
    earlier = (all_owners[None, :] == all_owners[:, None]) & (ids[None, :] < ids[:, None])
    offsets = jnp.sum(jnp.where(earlier, all_lengths[None, :], 0), 1)
    ranks = jnp.sum(earlier.astype(jnp.int32), 1)
    ahead = (all_owners // 4 - x_at) % 4
    ahead = jnp.where(ahead == 0, 3, jnp.where(ahead == 1, 1, jnp.where(ahead == 2, 0, 2)))
    spot = (ahead * 4 + all_owners % 4) * PER_OWNER + ranks
    own = OWNERS * cols // 2
    chosen = (spot[None, :] == places[:, None]) & (places[None, :] < own)

    def sort(values):
        return jnp.sum(jnp.where(chosen, values[None, :], 0), 1)[:, None]

    slots = jnp.arange(SLOTS, dtype=jnp.int32)[None, :]
    targets = jnp.where(slots < sort(all_lengths), sort(offsets) + slots, -1)
    targets = targets.reshape(OWNERS, 1, PER_OWNER * SLOTS)

    def paired(tokens):
        whole = add(tokens, core(tokens)).astype(BF)
        n = whole.shape[0] // 2
        got = y_lo(jnp.where(second_core, whole[n:], whole[:n]))
        other = core(got)
        first, second = jnp.where(second_core, other, got), jnp.where(second_core, got, other)
        return jnp.concatenate([whole, jnp.concatenate([first, second])], 1)

    def multiplied(weights, tokens):
        dims = (((1,), (1,)), ((), ()))
        return lax.dot_general(weights, tokens, dims, preferred_element_type=F32).astype(BF)

    packed = pack(spot[:own], weights[:own], targets, hidden_pieces, False)
    x_far, x_near = paired(packed[:512]), paired(packed[512:])
    gate_up = [multiplied(gate_up_weights, x_far)]
    gate_up += [multiplied(gate_up_weights, x_near[k * 512 : (k + 1) * 512]) for k in range(3)]
    (gate_2, gate_1, gate_3, gate_0) = (part[:padded] for part in gate_up)
    (up_2, up_1, up_3, up_0) = (part[padded:] for part in gate_up)
    gate_far, up_far = x_up(gate_2), x_down(up_2)
    up_below, gate_above = x_up(up_1), x_down(gate_3)
    gate_below = x_up(add(gate_1, gate_far).astype(BF))
    up_above = x_down(add(up_3, up_far).astype(BF))
    gate, upval = add(gate_0, gate_below, gate_above), add(up_0, up_below, up_above)
    sig = jax.nn.sigmoid(gate)
    silu = gate * sig
    hidden = (silu * upval).astype(BF)

    middle = padded // 2
    hidden_below, hidden_above = x_up(hidden), x_down(hidden)
    hidden_far = [x_up(hidden_below[:middle]), x_down(hidden_above[middle:])]
    hidden_all = jnp.concatenate(
        [jnp.concatenate(hidden_far), hidden_above, hidden_below, hidden], 1
    )

    packed_grad = pack(spot[:own], weights[:own], targets, grad_pieces, True)
    g_far, g_near = paired(packed_grad[:512]), paired(packed_grad[512:])
    grad_2 = multiplied(down_weights, g_far)
    grad_1, grad_3, grad_0 = (
        multiplied(down_weights, g_near[k * 512 : (k + 1) * 512]) for k in range(3)
    )
    far_1, far_2 = x_up(grad_2[:middle]), x_down(grad_2[middle:])
    below_2, above_1 = x_up(grad_1[middle:]), x_down(grad_3[:middle])
    below_1 = x_up(add(grad_1[:middle], far_1).astype(BF))
    above_2 = x_down(add(grad_3[middle:], far_2).astype(BF))
    grad_hidden = jnp.concatenate(
        [add(grad_0[:middle], below_1, above_1), add(grad_0[middle:], below_2, above_2)]
    )
    act = jnp.concatenate(
        [
            (grad_hidden * upval * sig * (1.0 + gate * (1.0 - sig))).astype(BF),
            (grad_hidden * silu).astype(BF),
        ]
    )

    act_below, act_above = x_up(act), x_down(act)
    act_far = jnp.concatenate([x_up(act_below[:padded]), x_down(act_above[padded:])])

    def input_grad(part):
        dims = (((0,), (0,)), ((), ()))
        out = lax.dot_general(part, gate_up_weights, dims, preferred_element_type=F32)
        return out.astype(BF).reshape(2, 2, CAPR, 2 * width)

    def core_summed(tiles):
        kept = jnp.where(second_core, tiles[:, :, 1], tiles[:, :, 0])
        return add(kept, core(jnp.where(second_core, tiles[:, :, 0], tiles[:, :, 1]))).astype(BF)

    near = core_summed(jnp.stack([input_grad(act), input_grad(act_above), input_grad(act_below)]))
    far = core_summed(input_grad(act_far)[None])
    tiles = jnp.concatenate([near[:2], far, near[2:]])
    tiles = lax.dynamic_slice_in_dim(jnp.concatenate([tiles, tiles]), (4 - x_at) % 4, 4, 0)
    groups = [[i * 2 + c for i in range(OWNERS // 2)] for c in range(2)]
    tiles = lax.all_to_all(
        tiles.reshape(OWNERS // 2, CAPR, 2 * width),
        "row",
        0,
        0,
        axis_index_groups=groups,
        tiled=True,
    )
    tiles = jnp.sum(tiles.astype(F32), axis=0)

    def exchanged(grads):
        mine, got = grads[:, :width].astype(BF), y_lo(grads[:, width:].astype(BF))
        out = []
        for k in range(grads.shape[0] // padded):
            one, two = (v[k * padded : k * padded + units] for v in (mine, got))
            out.append(
                jnp.where(odd, jnp.concatenate([two, one]), jnp.concatenate([one, two]))
            )
        return out

    (grad_down,) = exchanged(
        jnp.dot(hidden_all, jnp.concatenate([g_far, g_near]), preferred_element_type=F32)
    )
    grads = jnp.dot(
        jnp.concatenate([act_above, act_below, act], 1), x_near, preferred_element_type=F32
    )
    grads = grads + jnp.dot(act_far, x_far, preferred_element_type=F32)
    grad_gate, grad_up = exchanged(grads)
    grad_input = add(tiles[:, :width], y_lo(tiles[:, width:].astype(BF))).astype(BF)
    return grad_input, grad_gate.T, grad_up.T, grad_down


def solution(mesh):
    return jax.shard_map(
        per_device,
        mesh=mesh,
        in_specs=(
            P(("row", "col"), None),
            P(("row", "col"), None),
            P(("row", "col")),
            P(("row", "col")),
            P(("row", "col")),
            P(("row", "col")),
            P("col", "row"),
            P("col", "row"),
            P("row", "col"),
        ),
        out_specs=(P("row", "col"), P("col", "row"), P("col", "row"), P("row", "col")),
        check_vma=False,
    )
```

```python
import jax
import jax.numpy as jnp
from jax import lax
from jax.experimental import pallas as pl
from jax.experimental.pallas import tpu as pltpu
from jax.sharding import PartitionSpec as P

CAPR = 128
OWNERS = 16
PER_OWNER = 8
PROMPTS = 16
SLOTS = 48
spread_floor = 0.7
BF = jnp.bfloat16
F32 = jnp.float32

X_UP = [(i, ((i // 2 + 1) % 4) * 2 + i % 2) for i in range(8)]
X_DOWN = [(i, ((i // 2 + 3) % 4) * 2 + i % 2) for i in range(8)]
Y_LO = [(i, i ^ 1) for i in range(8)]
Z_UP = [(i, ((i // 4 + 1) % 4) * 4 + i % 4) for i in range(16)]
Z_DOWN = [(i, ((i // 4 + 3) % 4) * 4 + i % 4) for i in range(16)]
Y_HI = [(i, i ^ 2) for i in range(16)]
CORE = [(i, i ^ 1) for i in range(16)]


def after(value, *earlier):
    return lax.optimization_barrier((value, *earlier))[0]


class Link:
    def __init__(self, axis, pairs, most=2):
        self.axis, self.pairs, self.most, self.got = axis, pairs, most, []

    def __call__(self, value):
        if len(self.got) >= self.most:
            value = after(value, self.got[-self.most])
        self.got.append(lax.ppermute(value, self.axis, self.pairs))
        return self.got[-1]


def add(*terms):
    total = terms[0].astype(F32)
    for term in terms[1:]:
        total = total + term.astype(F32)
    return total


def row_weights(lengths, prompts, rewards):
    onehot = (prompts[:, None] == jnp.arange(PROMPTS, dtype=jnp.int32)[None, :]).astype(F32)
    counts = jnp.maximum(jnp.sum(onehot, 0), 1.0)
    means = jnp.sum(onehot * rewards[:, None], 0) / counts
    centred = rewards - jnp.sum(onehot * means[None, :], 1)
    spreads = jnp.sqrt(jnp.sum(onehot * (centred * centred)[:, None], 0) / counts)
    divisor = jnp.maximum(jnp.sum(onehot * spreads[None, :], 1), spread_floor)
    return centred / divisor / lengths.astype(F32)


def pack_kernel(weighted, spot_ref, weight_ref, target_ref, *refs):
    pieces, (far_ref, near_ref, stage, held, arrived) = refs[:-5], refs[-5:]
    copies = [
        pltpu.make_async_copy(piece, stage.at[p], arrived.at[p])
        for p, piece in enumerate(pieces)
    ]
    for copy in copies:
        copy.start()
    held[...] = jnp.zeros_like(held)
    for p, copy in enumerate(copies):
        copy.wait()
        for k in range(PER_OWNER):
            at = p * PER_OWNER + k
            block = stage[p, k]
            if weighted:
                block = (block.astype(F32) * weight_ref[at]).astype(BF)
            held[pl.ds(pl.multiple_of(spot_ref[at] * SLOTS, SLOTS), SLOTS), :] = block
    span = PER_OWNER * SLOTS
    places = lax.broadcasted_iota(jnp.int32, (CAPR, span), 0)
    for owner in range(OWNERS):
        onehot = (places == target_ref[owner]).astype(F32).astype(BF)
        rows = held[owner * span : (owner + 1) * span, :]
        out = jnp.dot(onehot, rows, preferred_element_type=F32).astype(BF)
        if owner < 4:
            far_ref[owner * CAPR : (owner + 1) * CAPR, :] = out
        else:
            near_ref[(owner - 4) * CAPR : (owner - 3) * CAPR, :] = out


def pack(spots, weights, targets, pieces, weighted):
    shape = pieces[0].shape
    width, count = shape[2], len(pieces)
    scalars, arrays = pl.BlockSpec(memory_space=pltpu.SMEM), pl.BlockSpec(memory_space=pltpu.VMEM)
    return pl.pallas_call(
        lambda *refs: pack_kernel(weighted, *refs),
        in_specs=[scalars, scalars, arrays] + [pl.BlockSpec(memory_space=pl.ANY)] * count,
        out_specs=[arrays, arrays],
        out_shape=[
            jax.ShapeDtypeStruct((4 * CAPR, width), BF),
            jax.ShapeDtypeStruct((12 * CAPR, width), BF),
        ],
        scratch_shapes=[
            pltpu.VMEM((count, *shape), BF),
            pltpu.VMEM((OWNERS * PER_OWNER * SLOTS, width), BF),
            pltpu.SemaphoreType.DMA((count,)),
        ],
        compiler_params=pltpu.CompilerParams(vmem_limit_bytes=24 << 20),
        cost_estimate=pl.CostEstimate(
            flops=2 * 2048 * 384 * 512, bytes_accessed=9 << 20, transcendentals=0
        ),
    )(spots, weights, targets, *pieces)


def product_kernel(*refs):
    lefts, near_ref, far_ref, mine_ref, sent_ref = refs[:4], *refs[4:]
    for out_ref, first in ((mine_ref, 0), (sent_ref, 512)):
        for at in (first, first + 256):
            total = jnp.dot(
                lefts[3][...], far_ref[:, at : at + 256], preferred_element_type=F32
            )
            for k in range(3):
                total += jnp.dot(
                    lefts[k][...],
                    near_ref[k * 512 : (k + 1) * 512, at : at + 256],
                    preferred_element_type=F32,
                )
            out_ref[:, at - first : at - first + 256] = total.astype(BF)


def token_product(lefts, near, far):
    units = lefts[0].shape[0]
    return pl.pallas_call(
        product_kernel,
        in_specs=[pl.BlockSpec(memory_space=pltpu.VMEM)] * 6,
        out_specs=[pl.BlockSpec(memory_space=pltpu.VMEM)] * 2,
        out_shape=[jax.ShapeDtypeStruct((units, 512), BF)] * 2,
        compiler_params=pltpu.CompilerParams(vmem_limit_bytes=40 << 20),
        cost_estimate=pl.CostEstimate(
            flops=2 * units * 2048 * 1024, bytes_accessed=10 << 20, transcendentals=0
        ),
    )(*lefts, near, far)


def gathered_rows(piece, z_up, z_down, y_hi, beside=None):
    other = y_hi(piece)
    below, above = z_up(piece), z_down(piece)
    below_other, above_other = z_up(other), z_down(other)
    met = () if beside is None else (beside(other),)
    far, far_other = z_up(after(below, *met)), z_down(after(above_other, *met))
    return [piece, other, above, above_other, far, far_other, below, below_other]


def per_device(
    roll_hidden,
    roll_cotangent,
    lengths,
    owners,
    prompts,
    rewards,
    gate_weight,
    up_weight,
    down_weight,
):
    slot_count, full = roll_hidden.shape
    cols = lax.axis_size("col")
    width = full // cols
    r_at, c_at = lax.axis_index("row"), lax.axis_index("col")

    high = lax.reduce_precision(rewards, 8, 7)
    middle = lax.reduce_precision(rewards - high, 8, 7)
    low = rewards - high - middle
    numbers = jnp.stack(
        [lengths.astype(F32), owners.astype(F32), prompts.astype(F32), high, middle, low], axis=1
    )
    numbers = jnp.pad(numbers.astype(BF), ((0, SLOTS - slot_count - 1), (0, width - 6)))
    numbers = jnp.broadcast_to(numbers[None], (cols, SLOTS - slot_count, width))

    def blocks(array):
        return jnp.moveaxis(array.reshape(slot_count, cols, width), 1, 0)

    both = jnp.concatenate(
        [
            blocks(roll_hidden),
            numbers,
            blocks(roll_cotangent),
            jnp.zeros((cols, SLOTS - slot_count, width), BF),
        ],
        axis=1,
    )
    both = lax.all_to_all(both, "col", 0, 0, tiled=True)
    hidden_piece, grad_piece = both[:, :SLOTS], both[:, SLOTS:]

    x_at, odd, second_core = c_at // 2, c_at % 2 == 1, r_at % 2 == 1
    x_up, x_down, y_lo = Link("col", X_UP), Link("col", X_DOWN), Link("col", Y_LO, 1)
    z_up, z_down, core = Link("row", Z_UP, 1), Link("row", Z_DOWN, 1), Link("row", CORE)
    y_hi = Link("row", Y_HI, 1)

    units = down_weight.shape[0] // 2
    padded = -(-units // 16) * 16

    def split_units(weight):
        halves = [
            jnp.pad(weight[k * units : (k + 1) * units], ((0, padded - units), (0, 0)))
            for k in range(2)
        ]
        return jnp.where(odd, halves[1], halves[0]), jnp.where(odd, halves[0], halves[1])

    gate_mine, gate_sent = split_units(gate_weight.T)
    up_mine, up_sent = split_units(up_weight.T)
    down_mine, down_sent = split_units(down_weight)
    received = []

    def send_gate(other):
        received.append(y_lo(after(gate_sent, other)))
        return received[-1]

    hidden_pieces = gathered_rows(hidden_piece, z_up, z_down, y_hi, send_gate)
    received += [y_lo(up_sent), y_lo(down_sent)]
    gate_up_weights = jnp.concatenate(
        [
            jnp.concatenate([gate_mine, received[0]], 1),
            jnp.concatenate([up_mine, received[1]], 1),
        ]
    )
    down_weights = jnp.concatenate([down_mine, received[2]], 1)
    grad_piece = after(grad_piece, hidden_pieces[4], hidden_pieces[5])
    grad_pieces = gathered_rows(grad_piece, z_up, z_down, y_hi)
    early = (grad_pieces[1], grad_pieces[2], grad_pieces[6], received[2])
    later = (grad_pieces[3], grad_pieces[7])

    told = jnp.concatenate([piece[:, slot_count, :8] for piece in hidden_pieces]).astype(F32)
    told = jnp.concatenate([told, core(told)])
    all_lengths = told[:, 0].astype(jnp.int32)
    all_owners = told[:, 1].astype(jnp.int32)
    all_prompts = told[:, 2].astype(jnp.int32)
    weights = row_weights(all_lengths, all_prompts, told[:, 3] + told[:, 4] + told[:, 5])
    places = jnp.arange(OWNERS * cols, dtype=jnp.int32)
    step = places // cols
    ids = (
        ((r_at // 4 + step // 2 % 4) % 4) * 4
        + ((r_at // 2 % 2) ^ (step % 2)) * 2
        + ((r_at % 2) ^ (step // 8))
    ) * cols + places % cols
    earlier = (all_owners[None, :] == all_owners[:, None]) & (ids[None, :] < ids[:, None])
    offsets = jnp.sum(jnp.where(earlier, all_lengths[None, :], 0), 1)
    ranks = jnp.sum(earlier.astype(jnp.int32), 1)
    ahead = (all_owners // 4 - x_at) % 4
    ahead = jnp.where(ahead == 0, 3, jnp.where(ahead == 1, 1, jnp.where(ahead == 2, 0, 2)))
    spot = (ahead * 4 + all_owners % 4) * PER_OWNER + ranks
    own = OWNERS * cols // 2
    chosen = (spot[None, :] == places[:, None]) & (places[None, :] < own)

    def sort(values):
        return jnp.sum(jnp.where(chosen, values[None, :], 0), 1)[:, None]

    slots = jnp.arange(SLOTS, dtype=jnp.int32)[None, :]
    targets = jnp.where(slots < sort(all_lengths), sort(offsets) + slots, -1)
    targets = targets.reshape(OWNERS, 1, PER_OWNER * SLOTS)

    def paired(tokens):
        whole = add(tokens, core(tokens)).astype(BF)
        n = whole.shape[0] // 2
        got = y_lo(jnp.where(second_core, whole[n:], whole[:n]))
        other = core(got)
        first, second = jnp.where(second_core, other, got), jnp.where(second_core, got, other)
        return jnp.concatenate([whole, jnp.concatenate([first, second])], 1)

    def multiplied(weights, tokens):
        dims = (((1,), (1,)), ((), ()))
        return lax.dot_general(weights, tokens, dims, preferred_element_type=F32).astype(BF)

    spots = after(spot[:own], received[1])
    packed_far, packed_near = pack(spots, weights[:own], targets, hidden_pieces, False)
    x_far = after(paired(after(packed_far, *early)), *later)
    x_near = paired(packed_near)
    gate_up = [multiplied(gate_up_weights, x_far)]
    gate_up += [multiplied(gate_up_weights, x_near[k * 512 : (k + 1) * 512]) for k in range(3)]
    (gate_2, gate_1, gate_3, gate_0) = (part[:padded] for part in gate_up)
    (up_2, up_1, up_3, up_0) = (part[padded:] for part in gate_up)
    gate_far, up_far = x_up(gate_2), x_down(up_2)
    up_below, gate_above = x_up(up_1), x_down(gate_3)
    gate_below = x_up(add(gate_1, gate_far).astype(BF))
    up_above = x_down(add(up_3, up_far).astype(BF))
    gate, upval = add(gate_0, gate_below, gate_above), add(up_0, up_below, up_above)
    sig = jax.nn.sigmoid(gate)
    silu = gate * sig
    hidden = (silu * upval).astype(BF)

    middle = padded // 2
    hidden_below, hidden_above = x_up(hidden), x_down(hidden)
    hidden_far = [x_up(hidden_below[:middle]), x_down(hidden_above[middle:])]
    hidden_all = [hidden_above, hidden_below, hidden, jnp.concatenate(hidden_far)]

    spots = after(spots, gate_far, up_far, x_near)
    grad_far, grad_near = pack(spots, weights[:own], targets, grad_pieces, True)
    g_far, g_near = paired(grad_far), paired(grad_near)
    grad_2 = multiplied(down_weights, g_far)
    grad_1, grad_3, grad_0 = (
        multiplied(down_weights, g_near[k * 512 : (k + 1) * 512]) for k in range(3)
    )
    far_1, far_2 = x_up(grad_2[:middle]), x_down(grad_2[middle:])
    below_2, above_1 = x_up(grad_1[middle:]), x_down(grad_3[:middle])
    below_1 = x_up(add(grad_1[:middle], far_1).astype(BF))
    above_2 = x_down(add(grad_3[middle:], far_2).astype(BF))
    grad_hidden = jnp.concatenate(
        [add(grad_0[:middle], below_1, above_1), add(grad_0[middle:], below_2, above_2)]
    )
    act = jnp.concatenate(
        [
            (grad_hidden * upval * sig * (1.0 + gate * (1.0 - sig))).astype(BF),
            (grad_hidden * silu).astype(BF),
        ]
    )

    def exchanged(mine, sent):
        got = y_lo(sent)
        out = []
        for k in range(mine.shape[0] // padded):
            one, two = (v[k * padded : k * padded + units] for v in (mine, got))
            out.append(
                jnp.where(odd, jnp.concatenate([two, one]), jnp.concatenate([one, two]))
            )
        return out, got

    act_below, act_above = x_up(act), x_down(act)
    (grad_down,), got_down = exchanged(*token_product(hidden_all, g_near, g_far))
    act_far = jnp.concatenate(
        [x_up(after(act_below[:padded], got_down)), x_down(act_above[padded:])]
    )

    def input_grad(part):
        dims = (((0,), (0,)), ((), ()))
        out = lax.dot_general(part, gate_up_weights, dims, preferred_element_type=F32)
        return out.astype(BF).reshape(2, 2, CAPR, 2 * width)

    parts = [input_grad(part) for part in (act, act_above, act_far, act_below)]
    parts = [lax.select_n(x_at, *[parts[(z - k) % 4] for k in range(4)]) for z in range(4)]
    kept = jnp.stack([jnp.where(second_core, part[:, 1], part[:, 0]) for part in parts])
    tiles = jnp.stack([jnp.where(second_core, part[:, 0], part[:, 1]) for part in parts])
    tiles = add(kept, core(tiles)).astype(BF)
    groups = [[z * 4 + k for z in range(4)] for k in range(4)]
    tiles = lax.all_to_all(tiles, "row", 0, 0, axis_index_groups=groups, tiled=True)
    tiles = jnp.sum(tiles.astype(F32), axis=0)
    high = r_at // 2 % 2 == 1
    sent, kept = jnp.where(high, tiles[0], tiles[1]), jnp.where(high, tiles[1], tiles[0])
    tiles = add(kept, y_hi(sent.astype(BF)))

    (grad_gate, grad_up), _ = exchanged(
        *token_product([act_above, act_below, act, act_far], x_near, x_far)
    )
    grad_input = add(tiles[:, :width], y_lo(tiles[:, width:].astype(BF))).astype(BF)
    return grad_input, grad_gate.T, grad_up.T, grad_down


def solution(mesh):
    return jax.shard_map(
        per_device,
        mesh=mesh,
        in_specs=(
            P(("row", "col"), None),
            P(("row", "col"), None),
            P(("row", "col")),
            P(("row", "col")),
            P(("row", "col")),
            P(("row", "col")),
            P("col", "row"),
            P("col", "row"),
            P("row", "col"),
        ),
        out_specs=(P("row", "col"), P("col", "row"), P("col", "row"), P("row", "col")),
        check_vma=False,
    )
```

```python
import jax
import jax.numpy as jnp
from jax import lax
from jax.experimental import pallas as pl
from jax.experimental.pallas import tpu as pltpu
from jax.sharding import PartitionSpec as P

CAPR = 128
OWNERS = 16
PER_OWNER = 8
PROMPTS = 16
SLOTS = 48
spread_floor = 0.7
BF = jnp.bfloat16
F32 = jnp.float32

X_UP = [(i, ((i // 2 + 1) % 4) * 2 + i % 2) for i in range(8)]
X_DOWN = [(i, ((i // 2 + 3) % 4) * 2 + i % 2) for i in range(8)]
Y_LO = [(i, i ^ 1) for i in range(8)]
Z_UP = [(i, ((i // 4 + 1) % 4) * 4 + i % 4) for i in range(16)]
Z_DOWN = [(i, ((i // 4 + 3) % 4) * 4 + i % 4) for i in range(16)]
Y_HI = [(i, i ^ 2) for i in range(16)]
CORE = [(i, i ^ 1) for i in range(16)]


def after(value, *earlier):
    return lax.optimization_barrier((value, *earlier))[0]


class Link:
    def __init__(self, axis, pairs, most=2):
        self.axis, self.pairs, self.most, self.got = axis, pairs, most, []

    def __call__(self, value):
        if len(self.got) >= self.most:
            value = after(value, self.got[-self.most])
        self.got.append(lax.ppermute(value, self.axis, self.pairs))
        return self.got[-1]


def add(*terms):
    total = terms[0].astype(F32)
    for term in terms[1:]:
        total = total + term.astype(F32)
    return total


def row_weights(lengths, prompts, rewards):
    onehot = (prompts[:, None] == jnp.arange(PROMPTS, dtype=jnp.int32)[None, :]).astype(F32)
    counts = jnp.maximum(jnp.sum(onehot, 0), 1.0)
    means = jnp.sum(onehot * rewards[:, None], 0) / counts
    centred = rewards - jnp.sum(onehot * means[None, :], 1)
    spreads = jnp.sqrt(jnp.sum(onehot * (centred * centred)[:, None], 0) / counts)
    divisor = jnp.maximum(jnp.sum(onehot * spreads[None, :], 1), spread_floor)
    return centred / divisor / lengths.astype(F32)


def pack_kernel(weighted, spot_ref, weight_ref, target_ref, *refs):
    pieces, (far_ref, near_ref, stage, held, arrived) = refs[:-5], refs[-5:]
    copies = [
        pltpu.make_async_copy(piece, stage.at[p], arrived.at[p])
        for p, piece in enumerate(pieces)
    ]
    for copy in copies:
        copy.start()
    held[...] = jnp.zeros_like(held)
    for p, copy in enumerate(copies):
        copy.wait()
        for k in range(PER_OWNER):
            at = p * PER_OWNER + k
            block = stage[p, k]
            if weighted:
                block = (block.astype(F32) * weight_ref[at]).astype(BF)
            held[pl.ds(pl.multiple_of(spot_ref[at] * SLOTS, SLOTS), SLOTS), :] = block
    span = PER_OWNER * SLOTS
    places = lax.broadcasted_iota(jnp.int32, (CAPR, span), 0)
    for owner in range(OWNERS):
        onehot = (places == target_ref[owner]).astype(F32).astype(BF)
        rows = held[owner * span : (owner + 1) * span, :]
        out = jnp.dot(onehot, rows, preferred_element_type=F32).astype(BF)
        if owner < 4:
            far_ref[owner * CAPR : (owner + 1) * CAPR, :] = out
        else:
            near_ref[(owner - 4) * CAPR : (owner - 3) * CAPR, :] = out


def pack(spots, weights, targets, pieces, weighted):
    shape = pieces[0].shape
    width, count = shape[2], len(pieces)
    scalars, arrays = pl.BlockSpec(memory_space=pltpu.SMEM), pl.BlockSpec(memory_space=pltpu.VMEM)
    return pl.pallas_call(
        lambda *refs: pack_kernel(weighted, *refs),
        in_specs=[scalars, scalars, arrays] + [pl.BlockSpec(memory_space=pltpu.HBM)] * count,
        out_specs=[arrays, arrays],
        out_shape=[
            jax.ShapeDtypeStruct((4 * CAPR, width), BF),
            jax.ShapeDtypeStruct((12 * CAPR, width), BF),
        ],
        scratch_shapes=[
            pltpu.VMEM((count, *shape), BF),
            pltpu.VMEM((OWNERS * PER_OWNER * SLOTS, width), BF),
            pltpu.SemaphoreType.DMA((count,)),
        ],
        compiler_params=pltpu.CompilerParams(vmem_limit_bytes=24 << 20),
        cost_estimate=pl.CostEstimate(
            flops=2 * 2048 * 384 * 512, bytes_accessed=9 << 20, transcendentals=0
        ),
    )(spots, weights, targets, *pieces)


def input_grad_kernel(at_ref, *refs):
    parts, (weights_ref, kept_ref, sent_ref) = refs[:4], refs[4:]
    for ahead, part in enumerate(parts):
        z = lax.rem(at_ref[0] + ahead, 4)
        for first in range(0, weights_ref.shape[1], 256):
            columns = slice(first, first + 256)
            out = lax.dot_general(
                part[...],
                weights_ref[:, columns],
                (((0,), (0,)), ((), ())),
                preferred_element_type=F32,
            ).astype(BF)
            for owner in range(4):
                y = lax.rem(at_ref[1] + owner // 2, 2)
                tile = out[owner * CAPR : (owner + 1) * CAPR]

                @pl.when(at_ref[2] == owner % 2)
                def _(tile=tile, y=y):
                    kept_ref[z, y, :, columns] = tile

                @pl.when(at_ref[2] != owner % 2)
                def _(tile=tile, y=y):
                    sent_ref[z, y, :, columns] = tile


def input_grads(at, parts, weights):
    arrays = pl.BlockSpec(memory_space=pltpu.VMEM)
    units, width = weights.shape
    return pl.pallas_call(
        input_grad_kernel,
        in_specs=[pl.BlockSpec(memory_space=pltpu.SMEM)] + [arrays] * 5,
        out_specs=[arrays] * 2,
        out_shape=[jax.ShapeDtypeStruct((4, 2, CAPR, width), BF)] * 2,
        compiler_params=pltpu.CompilerParams(vmem_limit_bytes=32 << 20),
        cost_estimate=pl.CostEstimate(
            flops=2 * units * 2048 * width, bytes_accessed=10 << 20, transcendentals=0
        ),
    )(at, *parts, weights)


def product_kernel(*refs):
    lefts, near_ref, far_ref, mine_ref, sent_ref = refs[:4], *refs[4:]
    for out_ref, first in ((mine_ref, 0), (sent_ref, 512)):
        for at in (first, first + 256):
            total = jnp.dot(
                lefts[3][...], far_ref[:, at : at + 256], preferred_element_type=F32
            )
            for k in range(3):
                total += jnp.dot(
                    lefts[k][...],
                    near_ref[k * 512 : (k + 1) * 512, at : at + 256],
                    preferred_element_type=F32,
                )
            out_ref[:, at - first : at - first + 256] = total.astype(BF)


def token_product(lefts, near, far):
    units = lefts[0].shape[0]
    return pl.pallas_call(
        product_kernel,
        in_specs=[pl.BlockSpec(memory_space=pltpu.VMEM)] * 6,
        out_specs=[pl.BlockSpec(memory_space=pltpu.VMEM)] * 2,
        out_shape=[jax.ShapeDtypeStruct((units, 512), BF)] * 2,
        compiler_params=pltpu.CompilerParams(vmem_limit_bytes=40 << 20),
        cost_estimate=pl.CostEstimate(
            flops=2 * units * 2048 * 1024, bytes_accessed=10 << 20, transcendentals=0
        ),
    )(*lefts, near, far)


def gathered_rows(piece, z_up, z_down, y_hi, beside=None):
    other = y_hi(piece)
    below, above = z_up(piece), z_down(piece)
    below_other, above_other = z_up(other), z_down(other)
    met = () if beside is None else (beside(other),)
    far, far_other = z_up(after(below, *met)), z_down(after(above_other, *met))
    return [piece, other, above, above_other, far, far_other, below, below_other]


def per_device(
    roll_hidden,
    roll_cotangent,
    lengths,
    owners,
    prompts,
    rewards,
    gate_weight,
    up_weight,
    down_weight,
):
    slot_count, full = roll_hidden.shape
    cols = lax.axis_size("col")
    width = full // cols
    r_at, c_at = lax.axis_index("row"), lax.axis_index("col")

    high = lax.reduce_precision(rewards, 8, 7)
    middle = lax.reduce_precision(rewards - high, 8, 7)
    low = rewards - high - middle
    numbers = jnp.stack(
        [lengths.astype(F32), owners.astype(F32), prompts.astype(F32), high, middle, low], axis=1
    )
    numbers = jnp.pad(numbers.astype(BF), ((0, SLOTS - slot_count - 1), (0, width - 6)))
    numbers = jnp.broadcast_to(numbers[None], (cols, SLOTS - slot_count, width))

    def blocks(array):
        return jnp.moveaxis(array.reshape(slot_count, cols, width), 1, 0)

    both = jnp.concatenate(
        [
            blocks(roll_hidden),
            numbers,
            blocks(roll_cotangent),
            jnp.zeros((cols, SLOTS - slot_count, width), BF),
        ],
        axis=1,
    )
    both = lax.all_to_all(both, "col", 0, 0, tiled=True)
    hidden_piece, grad_piece = both[:, :SLOTS], both[:, SLOTS:]

    x_at, odd, second_core = c_at // 2, c_at % 2 == 1, r_at % 2 == 1
    x_up, x_down, y_lo = Link("col", X_UP), Link("col", X_DOWN), Link("col", Y_LO, 1)
    z_up, z_down, core = Link("row", Z_UP, 1), Link("row", Z_DOWN, 1), Link("row", CORE)
    y_hi = Link("row", Y_HI, 1)

    units = down_weight.shape[0] // 2
    padded = -(-units // 16) * 16

    def split_units(weight):
        halves = [
            jnp.pad(weight[k * units : (k + 1) * units], ((0, padded - units), (0, 0)))
            for k in range(2)
        ]
        return jnp.where(odd, halves[1], halves[0]), jnp.where(odd, halves[0], halves[1])

    gate_mine, gate_sent = split_units(gate_weight.T)
    up_mine, up_sent = split_units(up_weight.T)
    down_mine, down_sent = split_units(down_weight)
    received = []

    def send_gate(other):
        received.append(y_lo(after(gate_sent, other)))
        return received[-1]

    hidden_pieces = gathered_rows(hidden_piece, z_up, z_down, y_hi, send_gate)
    received += [y_lo(up_sent), y_lo(down_sent)]
    gate_up_weights = jnp.concatenate(
        [
            jnp.concatenate([gate_mine, received[0]], 1),
            jnp.concatenate([up_mine, received[1]], 1),
        ]
    )
    down_weights = jnp.concatenate([down_mine, received[2]], 1)
    grad_piece = after(grad_piece, hidden_pieces[4], hidden_pieces[5])
    grad_pieces = gathered_rows(grad_piece, z_up, z_down, y_hi)
    early = (grad_pieces[1], grad_pieces[2], grad_pieces[6], received[2])
    later = (grad_pieces[3], grad_pieces[7])

    told = jnp.concatenate([piece[:, slot_count, :8] for piece in hidden_pieces]).astype(F32)
    told = jnp.concatenate([told, core(after(told, received[1]))])
    all_lengths = told[:, 0].astype(jnp.int32)
    all_owners = told[:, 1].astype(jnp.int32)
    all_prompts = told[:, 2].astype(jnp.int32)
    weights = row_weights(all_lengths, all_prompts, told[:, 3] + told[:, 4] + told[:, 5])
    places = jnp.arange(OWNERS * cols, dtype=jnp.int32)
    step = places // cols
    ids = (
        ((r_at // 4 + step // 2 % 4) % 4) * 4
        + ((r_at // 2 % 2) ^ (step % 2)) * 2
        + ((r_at % 2) ^ (step // 8))
    ) * cols + places % cols
    earlier = (all_owners[None, :] == all_owners[:, None]) & (ids[None, :] < ids[:, None])
    offsets = jnp.sum(jnp.where(earlier, all_lengths[None, :], 0), 1)
    ranks = jnp.sum(earlier.astype(jnp.int32), 1)
    ahead = (all_owners // 4 - x_at) % 4
    ahead = jnp.where(ahead == 0, 3, jnp.where(ahead == 1, 1, jnp.where(ahead == 2, 0, 2)))
    spot = (ahead * 4 + all_owners % 4) * PER_OWNER + ranks
    own = OWNERS * cols // 2
    chosen = (spot[None, :] == places[:, None]) & (places[None, :] < own)

    def sort(values):
        return jnp.sum(jnp.where(chosen, values[None, :], 0), 1)[:, None]

    slots = jnp.arange(SLOTS, dtype=jnp.int32)[None, :]
    targets = jnp.where(slots < sort(all_lengths), sort(offsets) + slots, -1)
    targets = targets.reshape(OWNERS, 1, PER_OWNER * SLOTS)

    def paired(tokens, *met):
        whole = add(tokens, core(tokens)).astype(BF)
        n = whole.shape[0] // 2
        got = y_lo(jnp.where(second_core, whole[n:], whole[:n]))
        got = after(got, *met) if met else got
        other = core(got)
        first, second = jnp.where(second_core, other, got), jnp.where(second_core, got, other)
        return jnp.concatenate([whole, jnp.concatenate([first, second])], 1)

    def multiplied(weights, tokens):
        dims = (((1,), (1,)), ((), ()))
        return lax.dot_general(weights, tokens, dims, preferred_element_type=F32).astype(BF)

    spots = spot[:own]
    packed_far, packed_near = pack(spots, weights[:own], targets, hidden_pieces, False)
    x_far = paired(after(packed_far, *early))
    gate_up = [multiplied(gate_up_weights, x_far)]
    gate_far, up_far = x_up(gate_up[0][:padded]), x_down(gate_up[0][padded:])
    x_near = paired(packed_near, gate_far, up_far, *later)
    gate_up += [multiplied(gate_up_weights, x_near[k * 512 : (k + 1) * 512]) for k in range(3)]
    (gate_1, gate_3, gate_0) = (part[:padded] for part in gate_up[1:])
    (up_1, up_3, up_0) = (part[padded:] for part in gate_up[1:])
    up_below, gate_above = x_up(up_1), x_down(gate_3)
    gate_below = x_up(add(gate_1, gate_far).astype(BF))
    up_above = x_down(add(up_3, up_far).astype(BF))
    gate, upval = add(gate_0, gate_below, gate_above), add(up_0, up_below, up_above)
    sig = jax.nn.sigmoid(gate)
    silu = gate * sig
    hidden = (silu * upval).astype(BF)

    middle = padded // 2
    hidden_below, hidden_above = x_up(hidden), x_down(hidden)
    hidden_far = [x_up(hidden_below[:middle]), x_down(hidden_above[middle:])]
    hidden_all = [hidden_above, hidden_below, hidden, jnp.concatenate(hidden_far)]

    spots = after(spots, gate_up[1], gate_up[2])
    grad_far, grad_near = pack(spots, weights[:own], targets, grad_pieces, True)
    g_far, g_near = paired(grad_far), paired(grad_near)
    grad_2 = multiplied(down_weights, g_far)
    grad_1, grad_3, grad_0 = (
        multiplied(down_weights, g_near[k * 512 : (k + 1) * 512]) for k in range(3)
    )
    far_1, far_2 = x_up(grad_2[:middle]), x_down(grad_2[middle:])
    below_2, above_1 = x_up(grad_1[middle:]), x_down(grad_3[:middle])
    below_1 = x_up(add(grad_1[:middle], far_1).astype(BF))
    above_2 = x_down(add(grad_3[middle:], far_2).astype(BF))
    grad_hidden = jnp.concatenate(
        [add(grad_0[:middle], below_1, above_1), add(grad_0[middle:], below_2, above_2)]
    )
    act = jnp.concatenate(
        [
            (grad_hidden * upval * sig * (1.0 + gate * (1.0 - sig))).astype(BF),
            (grad_hidden * silu).astype(BF),
        ]
    )

    def exchanged(mine, sent):
        got = y_lo(sent)
        out = []
        for k in range(mine.shape[0] // padded):
            one, two = (v[k * padded : k * padded + units] for v in (mine, got))
            out.append(
                jnp.where(odd, jnp.concatenate([two, one]), jnp.concatenate([one, two]))
            )
        return out, got

    act_below, act_above = x_up(act), x_down(act)
    (grad_down,), got_down = exchanged(*token_product(hidden_all, g_near, g_far))
    act_far = jnp.concatenate(
        [x_up(after(act_below[:padded], got_down)), x_down(act_above[padded:])]
    )

    z_at, high = r_at // 4, r_at // 2 % 2
    at = jnp.stack([x_at - z_at + 4, high, r_at % 2]).astype(jnp.int32)
    kept, sent = input_grads(at, (act, act_above, act_far, act_below), gate_up_weights)
    tiles = add(kept, core(sent)).astype(BF)
    far_1, far_0 = z_up(tiles[2, 1]), z_down(tiles[2, 0])
    below_0, above_1 = z_up(tiles[1, 0]), z_down(tiles[3, 1])
    below_1 = z_up(add(tiles[1, 1], far_1).astype(BF))
    above_0 = z_down(add(tiles[3, 0], far_0).astype(BF))
    other = y_hi(add(tiles[0, 1], below_1, above_1).astype(BF))
    tiles = add(tiles[0, 0], below_0, above_0, other)

    (grad_gate, grad_up), _ = exchanged(
        *token_product([act_above, act_below, act, act_far], x_near, x_far)
    )
    grad_input = add(tiles[:, :width], y_lo(tiles[:, width:].astype(BF))).astype(BF)
    return grad_input, grad_gate.T, grad_up.T, grad_down


def solution(mesh):
    return jax.shard_map(
        per_device,
        mesh=mesh,
        in_specs=(
            P(("row", "col"), None),
            P(("row", "col"), None),
            P(("row", "col")),
            P(("row", "col")),
            P(("row", "col")),
            P(("row", "col")),
            P("col", "row"),
            P("col", "row"),
            P("row", "col"),
        ),
        out_specs=(P("row", "col"), P("col", "row"), P("col", "row"), P("row", "col")),
        check_vma=False,
    )
```

```python
import jax
import jax.numpy as jnp
from jax import lax
from jax.experimental import pallas as pl
from jax.experimental.pallas import tpu as pltpu
from jax.sharding import PartitionSpec as P

CAPR = 128
OWNERS = 16
PER_OWNER = 8
PROMPTS = 16
SLOTS = 48
spread_floor = 0.7
BF = jnp.bfloat16
F32 = jnp.float32

X_UP = [(i, ((i // 2 + 1) % 4) * 2 + i % 2) for i in range(8)]
X_DOWN = [(i, ((i // 2 + 3) % 4) * 2 + i % 2) for i in range(8)]
Y_LO = [(i, i ^ 1) for i in range(8)]
Z_UP = [(i, ((i // 4 + 1) % 4) * 4 + i % 4) for i in range(16)]
Z_DOWN = [(i, ((i // 4 + 3) % 4) * 4 + i % 4) for i in range(16)]
Y_HI = [(i, i ^ 2) for i in range(16)]
CORE = [(i, i ^ 1) for i in range(16)]


def after(value, *earlier):
    return lax.optimization_barrier((value, *earlier))[0]


class Link:
    def __init__(self, axis, pairs, most=2):
        self.axis, self.pairs, self.most, self.got = axis, pairs, most, []

    def __call__(self, value):
        if len(self.got) >= self.most:
            value = after(value, self.got[-self.most])
        self.got.append(lax.ppermute(value, self.axis, self.pairs))
        return self.got[-1]


def add(*terms):
    total = terms[0].astype(F32)
    for term in terms[1:]:
        total = total + term.astype(F32)
    return total


def row_weights(lengths, prompts, rewards):
    onehot = (prompts[:, None] == jnp.arange(PROMPTS, dtype=jnp.int32)[None, :]).astype(F32)
    counts = jnp.maximum(jnp.sum(onehot, 0), 1.0)
    means = jnp.sum(onehot * rewards[:, None], 0) / counts
    centred = rewards - jnp.sum(onehot * means[None, :], 1)
    spreads = jnp.sqrt(jnp.sum(onehot * (centred * centred)[:, None], 0) / counts)
    divisor = jnp.maximum(jnp.sum(onehot * spreads[None, :], 1), spread_floor)
    return centred / divisor / lengths.astype(F32)


def pack_kernel(weighted, spot_ref, weight_ref, target_ref, *refs):
    pieces, (far_ref, near_ref, stage, held, arrived) = refs[:-5], refs[-5:]
    copies = [
        pltpu.make_async_copy(piece, stage.at[p], arrived.at[p])
        for p, piece in enumerate(pieces)
    ]
    for copy in copies:
        copy.start()
    held[...] = jnp.zeros_like(held)
    for p, copy in enumerate(copies):
        copy.wait()
        for k in range(PER_OWNER):
            at = p * PER_OWNER + k
            block = stage[p, k]
            if weighted:
                block = (block.astype(F32) * weight_ref[at]).astype(BF)
            held[pl.ds(pl.multiple_of(spot_ref[at] * SLOTS, SLOTS), SLOTS), :] = block
    span = PER_OWNER * SLOTS
    places = lax.broadcasted_iota(jnp.int32, (CAPR, span), 0)
    for owner in range(OWNERS):
        onehot = (places == target_ref[owner]).astype(F32).astype(BF)
        rows = held[owner * span : (owner + 1) * span, :]
        out = jnp.dot(onehot, rows, preferred_element_type=F32).astype(BF)
        if owner < 4:
            far_ref[owner * CAPR : (owner + 1) * CAPR, :] = out
        else:
            near_ref[(owner - 4) * CAPR : (owner - 3) * CAPR, :] = out


def pack(spots, weights, targets, pieces, weighted):
    shape = pieces[0].shape
    width, count = shape[2], len(pieces)
    scalars, arrays = pl.BlockSpec(memory_space=pltpu.SMEM), pl.BlockSpec(memory_space=pltpu.VMEM)
    return pl.pallas_call(
        lambda *refs: pack_kernel(weighted, *refs),
        in_specs=[scalars, scalars, arrays] + [pl.BlockSpec(memory_space=pltpu.HBM)] * count,
        out_specs=[arrays, arrays],
        out_shape=[
            jax.ShapeDtypeStruct((4 * CAPR, width), BF),
            jax.ShapeDtypeStruct((12 * CAPR, width), BF),
        ],
        scratch_shapes=[
            pltpu.VMEM((count, *shape), BF),
            pltpu.VMEM((OWNERS * PER_OWNER * SLOTS, width), BF),
            pltpu.SemaphoreType.DMA((count,)),
        ],
        compiler_params=pltpu.CompilerParams(vmem_limit_bytes=24 << 20),
        cost_estimate=pl.CostEstimate(
            flops=2 * 2048 * 384 * 512, bytes_accessed=9 << 20, transcendentals=0
        ),
    )(spots, weights, targets, *pieces)


def input_grad_kernel(ahead, blocks, at_ref, *refs):
    parts, weights_ref, (kept_ref, sent_ref) = refs[:blocks], refs[blocks], refs[-2:]
    z = lax.rem(at_ref[0] + ahead, 4)
    for first in range(0, weights_ref.shape[1], 512):
        columns = slice(first, first + 512)
        out, row = None, 0
        for part in parts:
            term = lax.dot_general(
                part[...],
                weights_ref[row : row + part.shape[0], columns],
                (((0,), (0,)), ((), ())),
                preferred_element_type=F32,
            )
            out = term if out is None else out + term
            row += part.shape[0]
        out = out.astype(BF)
        for owner in range(4):
            y = lax.rem(at_ref[1] + owner // 2, 2)
            tile = out[owner * CAPR : (owner + 1) * CAPR]

            @pl.when(at_ref[2] == owner % 2)
            def _(tile=tile, y=y, columns=columns):
                kept_ref[z, y, :, columns] = tile

            @pl.when(at_ref[2] != owner % 2)
            def _(tile=tile, y=y, columns=columns):
                sent_ref[z, y, :, columns] = tile


def input_grads(ahead, at, parts, weights, so_far):
    arrays = pl.BlockSpec(memory_space=pltpu.VMEM)
    units, width = weights.shape
    count = 2 + len(parts)
    return pl.pallas_call(
        lambda *refs: input_grad_kernel(ahead, len(parts), *refs),
        in_specs=[pl.BlockSpec(memory_space=pltpu.SMEM)]
        + [arrays] * (count - 1)
        + [pl.BlockSpec(memory_space=pl.ANY)] * len(so_far),
        out_specs=[arrays] * 2,
        out_shape=[jax.ShapeDtypeStruct((4, 2, CAPR, width), BF)] * 2,
        input_output_aliases={count + k: k for k in range(len(so_far))},
        compiler_params=pltpu.CompilerParams(vmem_limit_bytes=24 << 20),
        cost_estimate=pl.CostEstimate(
            flops=2 * units * 512 * width, bytes_accessed=4 << 20, transcendentals=0
        ),
    )(at, *parts, weights, *so_far)


def product_kernel(counts, *refs):
    near_ref, far_ref, mine_ref, sent_ref = refs[-4:]
    chunks, used = [], 0
    for count in counts:
        chunks.append(refs[used : used + count])
        used += count
    rows = chunks[3][0].shape[0]
    for out_ref, first in ((mine_ref, 0), (sent_ref, 512)):
        for block, far in enumerate(chunks[3]):
            at = slice(block * rows, (block + 1) * rows)
            total = jnp.dot(
                far[...], far_ref[:, first : first + 512], preferred_element_type=F32
            )
            for k in range(3):
                total += jnp.dot(
                    chunks[k][0][at, :],
                    near_ref[k * 512 : (k + 1) * 512, first : first + 512],
                    preferred_element_type=F32,
                )
            out_ref[at, :] = total.astype(BF)


def token_product(lefts, far_blocks, near, far):
    units = lefts[0].shape[0]
    counts = [1, 1, 1, len(far_blocks)]
    return pl.pallas_call(
        lambda *refs: product_kernel(counts, *refs),
        in_specs=[pl.BlockSpec(memory_space=pltpu.VMEM)] * (sum(counts) + 2),
        out_specs=[pl.BlockSpec(memory_space=pltpu.VMEM)] * 2,
        out_shape=[jax.ShapeDtypeStruct((units, 512), BF)] * 2,
        compiler_params=pltpu.CompilerParams(vmem_limit_bytes=40 << 20),
        cost_estimate=pl.CostEstimate(
            flops=2 * units * 2048 * 1024, bytes_accessed=10 << 20, transcendentals=0
        ),
    )(*lefts, *far_blocks, near, far)


def gathered_rows(piece, z_up, z_down, y_hi, beside=None):
    other = y_hi(piece)
    below, above = z_up(piece), z_down(piece)
    below_other, above_other = z_up(other), z_down(other)
    met = () if beside is None else (beside(other),)
    far, far_other = z_up(after(below, *met)), z_down(after(above_other, *met))
    return [piece, other, above, above_other, far, far_other, below, below_other]


def per_device(
    roll_hidden,
    roll_cotangent,
    lengths,
    owners,
    prompts,
    rewards,
    gate_weight,
    up_weight,
    down_weight,
):
    slot_count, full = roll_hidden.shape
    cols = lax.axis_size("col")
    width = full // cols
    r_at, c_at = lax.axis_index("row"), lax.axis_index("col")

    high = lax.reduce_precision(rewards, 8, 7)
    middle = lax.reduce_precision(rewards - high, 8, 7)
    low = rewards - high - middle
    numbers = jnp.stack(
        [lengths.astype(F32), owners.astype(F32), prompts.astype(F32), high, middle, low], axis=1
    )
    numbers = jnp.pad(numbers.astype(BF), ((0, SLOTS - slot_count - 1), (0, width - 6)))
    numbers = jnp.broadcast_to(numbers[None], (cols, SLOTS - slot_count, width))

    def blocks(array):
        return jnp.moveaxis(array.reshape(slot_count, cols, width), 1, 0)

    both = jnp.concatenate(
        [
            blocks(roll_hidden),
            numbers,
            blocks(roll_cotangent),
            jnp.zeros((cols, SLOTS - slot_count, width), BF),
        ],
        axis=1,
    )
    both = lax.all_to_all(both, "col", 0, 0, tiled=True)
    hidden_piece, grad_piece = both[:, :SLOTS], both[:, SLOTS:]

    x_at, odd, second_core = c_at // 2, c_at % 2 == 1, r_at % 2 == 1
    x_up, x_down, y_lo = Link("col", X_UP), Link("col", X_DOWN), Link("col", Y_LO, 1)
    z_up, z_down, core = Link("row", Z_UP, 1), Link("row", Z_DOWN, 1), Link("row", CORE)
    y_hi = Link("row", Y_HI, 1)

    units = down_weight.shape[0] // 2
    padded = -(-units // 16) * 16

    def split_units(weight):
        halves = [
            jnp.pad(weight[k * units : (k + 1) * units], ((0, padded - units), (0, 0)))
            for k in range(2)
        ]
        return jnp.where(odd, halves[1], halves[0]), jnp.where(odd, halves[0], halves[1])

    gate_mine, gate_sent = split_units(gate_weight.T)
    up_mine, up_sent = split_units(up_weight.T)
    down_mine, down_sent = split_units(down_weight)
    received = []

    def send_gate(other):
        received.append(y_lo(after(gate_sent, other)))
        return received[-1]

    hidden_pieces = gathered_rows(hidden_piece, z_up, z_down, y_hi, send_gate)
    received.append(y_lo(up_sent))
    gate_up_weights = jnp.concatenate(
        [
            jnp.concatenate([gate_mine, received[0]], 1),
            jnp.concatenate([up_mine, received[1]], 1),
        ]
    )
    grad_piece = after(grad_piece, hidden_pieces[4], hidden_pieces[5])
    grad_pieces = gathered_rows(grad_piece, z_up, z_down, y_hi)
    early = (grad_pieces[1], grad_pieces[2], grad_pieces[6])
    later = (grad_pieces[3], grad_pieces[7])

    told = jnp.concatenate([piece[:, slot_count, :8] for piece in hidden_pieces]).astype(F32)
    told = jnp.concatenate([told, core(after(told, received[1]))])
    all_lengths = told[:, 0].astype(jnp.int32)
    all_owners = told[:, 1].astype(jnp.int32)
    all_prompts = told[:, 2].astype(jnp.int32)
    weights = row_weights(all_lengths, all_prompts, told[:, 3] + told[:, 4] + told[:, 5])
    places = jnp.arange(OWNERS * cols, dtype=jnp.int32)
    step = places // cols
    ids = (
        ((r_at // 4 + step // 2 % 4) % 4) * 4
        + ((r_at // 2 % 2) ^ (step % 2)) * 2
        + ((r_at % 2) ^ (step // 8))
    ) * cols + places % cols
    earlier = (all_owners[None, :] == all_owners[:, None]) & (ids[None, :] < ids[:, None])
    offsets = jnp.sum(jnp.where(earlier, all_lengths[None, :], 0), 1)
    ranks = jnp.sum(earlier.astype(jnp.int32), 1)
    ahead = (all_owners // 4 - x_at) % 4
    ahead = jnp.where(ahead == 0, 3, jnp.where(ahead == 1, 1, jnp.where(ahead == 2, 0, 2)))
    spot = (ahead * 4 + all_owners % 4) * PER_OWNER + ranks
    own = OWNERS * cols // 2
    chosen = (spot[None, :] == places[:, None]) & (places[None, :] < own)

    def sort(values):
        return jnp.sum(jnp.where(chosen, values[None, :], 0), 1)[:, None]

    slots = jnp.arange(SLOTS, dtype=jnp.int32)[None, :]
    targets = jnp.where(slots < sort(all_lengths), sort(offsets) + slots, -1)
    targets = targets.reshape(OWNERS, 1, PER_OWNER * SLOTS)

    def paired(tokens, *met):
        whole = add(tokens, core(tokens)).astype(BF)
        n = whole.shape[0] // 2
        got = y_lo(jnp.where(second_core, whole[n:], whole[:n]))
        got = after(got, *met) if met else got
        other = core(got)
        first, second = jnp.where(second_core, other, got), jnp.where(second_core, got, other)
        return jnp.concatenate([whole, jnp.concatenate([first, second])], 1)

    def multiplied(weights, tokens):
        dims = (((1,), (1,)), ((), ()))
        return lax.dot_general(weights, tokens, dims, preferred_element_type=F32).astype(BF)

    spots = spot[:own]
    packed_far, packed_near = pack(spots, weights[:own], targets, hidden_pieces, False)
    x_far = paired(after(packed_far, *early), *later)
    gate_up = [multiplied(gate_up_weights, x_far)]
    gate_far, up_far = x_up(gate_up[0][:padded]), x_down(gate_up[0][padded:])
    x_near = paired(packed_near, gate_far, up_far)
    down_weights = jnp.concatenate([down_mine, y_lo(down_sent)], 1)
    gate_up += [multiplied(gate_up_weights, x_near[k * 512 : (k + 1) * 512]) for k in range(3)]
    (gate_1, gate_3, gate_0) = (part[:padded] for part in gate_up[1:])
    (up_1, up_3, up_0) = (part[padded:] for part in gate_up[1:])
    up_below, gate_above = x_up(up_1), x_down(gate_3)
    gate_below = x_up(add(gate_1, gate_far).astype(BF))
    up_above = x_down(add(up_3, up_far).astype(BF))
    gate, upval = add(gate_0, gate_below, gate_above), add(up_0, up_below, up_above)
    sig = jax.nn.sigmoid(gate)
    silu = gate * sig
    hidden = (silu * upval).astype(BF)

    middle = padded // 2
    hidden_below, hidden_above = x_up(hidden), x_down(hidden)
    hidden_far = [x_up(hidden_below[:middle]), x_down(hidden_above[middle:])]

    spots = after(spots, up_below, gate_above)
    grad_far, grad_near = pack(spots, weights[:own], targets, grad_pieces, True)
    g_far, g_near = paired(grad_far), paired(grad_near)
    grad_2 = multiplied(down_weights, g_far)
    grad_1, grad_3, grad_0 = (
        multiplied(down_weights, g_near[k * 512 : (k + 1) * 512]) for k in range(3)
    )
    far_1, far_2 = x_up(grad_2[:middle]), x_down(grad_2[middle:])
    below_2, above_1 = x_up(grad_1[middle:]), x_down(grad_3[:middle])
    below_1 = x_up(add(grad_1[:middle], far_1).astype(BF))
    above_2 = x_down(add(grad_3[middle:], far_2).astype(BF))
    grad_hidden = jnp.concatenate(
        [add(grad_0[:middle], below_1, above_1), add(grad_0[middle:], below_2, above_2)]
    )
    act = jnp.concatenate(
        [
            (grad_hidden * upval * sig * (1.0 + gate * (1.0 - sig))).astype(BF),
            (grad_hidden * silu).astype(BF),
        ]
    )

    def exchanged(mine, sent):
        got = y_lo(sent)
        out = []
        for k in range(mine.shape[0] // padded):
            one, two = (v[k * padded : k * padded + units] for v in (mine, got))
            out.append(
                jnp.where(odd, jnp.concatenate([two, one]), jnp.concatenate([one, two]))
            )
        return out, got

    act_below, act_above = x_up(act), x_down(act)
    (grad_down,), got_down = exchanged(
        *token_product([hidden_above, hidden_below, hidden], hidden_far, g_near, g_far)
    )
    at = jnp.stack([x_at - r_at // 4 + 4, r_at // 2 % 2, r_at % 2]).astype(jnp.int32)
    tiles = input_grads(0, at, [act], gate_up_weights, [])
    act_far = [x_up(after(act_below[:padded], got_down)), x_down(act_above[padded:])]

    tiles = input_grads(1, at, [act_above], gate_up_weights, tiles)
    tiles = input_grads(3, at, [act_below], gate_up_weights, tiles)
    kept, sent = input_grads(2, at, act_far, gate_up_weights, tiles)
    z_up, z_down = Link("row", Z_UP), Link("row", Z_DOWN)
    tiles = add(kept, core(sent)).astype(BF)
    far_1, far_0 = z_up(tiles[2, 1]), z_down(tiles[2, 0])
    below_0, above_1 = z_up(tiles[1, 0]), z_down(tiles[3, 1])
    below_1 = z_up(add(tiles[1, 1], far_1).astype(BF))
    above_0 = z_down(add(tiles[3, 0], far_0).astype(BF))
    other = y_hi(add(tiles[0, 1], below_1, above_1).astype(BF))
    tiles = add(tiles[0, 0], below_0, above_0, other)

    (grad_gate, grad_up), _ = exchanged(
        *token_product([act_above, act_below, act], act_far, x_near, x_far)
    )
    grad_input = add(tiles[:, :width], y_lo(tiles[:, width:].astype(BF))).astype(BF)
    return grad_input, grad_gate.T, grad_up.T, grad_down


def solution(mesh):
    return jax.shard_map(
        per_device,
        mesh=mesh,
        in_specs=(
            P(("row", "col"), None),
            P(("row", "col"), None),
            P(("row", "col")),
            P(("row", "col")),
            P(("row", "col")),
            P(("row", "col")),
            P("col", "row"),
            P("col", "row"),
            P("row", "col"),
        ),
        out_specs=(P("row", "col"), P("col", "row"), P("col", "row"), P("row", "col")),
        check_vma=False,
    )
```

```python
import jax
import jax.numpy as jnp
from jax import lax
from jax.experimental import pallas as pl
from jax.experimental.pallas import tpu as pltpu
from jax.sharding import PartitionSpec as P

CAPR = 128
OWNERS = 16
PER_OWNER = 8
PROMPTS = 16
SLOTS = 48
spread_floor = 0.7
BF = jnp.bfloat16
F32 = jnp.float32

X_UP = [(i, ((i // 2 + 1) % 4) * 2 + i % 2) for i in range(8)]
X_DOWN = [(i, ((i // 2 + 3) % 4) * 2 + i % 2) for i in range(8)]
Y_LO = [(i, i ^ 1) for i in range(8)]
Z_UP = [(i, ((i // 4 + 1) % 4) * 4 + i % 4) for i in range(16)]
Z_DOWN = [(i, ((i // 4 + 3) % 4) * 4 + i % 4) for i in range(16)]
Y_HI = [(i, i ^ 2) for i in range(16)]
CORE = [(i, i ^ 1) for i in range(16)]


def after(value, *earlier):
    return lax.optimization_barrier((value, *earlier))[0]


class Link:
    def __init__(self, axis, pairs, most=2):
        self.axis, self.pairs, self.most, self.got = axis, pairs, most, []

    def __call__(self, value):
        if len(self.got) >= self.most:
            value = after(value, self.got[-self.most])
        self.got.append(lax.ppermute(value, self.axis, self.pairs))
        return self.got[-1]


def add(*terms):
    total = terms[0].astype(F32)
    for term in terms[1:]:
        total = total + term.astype(F32)
    return total


def row_weights(lengths, prompts, rewards):
    onehot = (prompts[:, None] == jnp.arange(PROMPTS, dtype=jnp.int32)[None, :]).astype(F32)
    counts = jnp.maximum(jnp.sum(onehot, 0), 1.0)
    means = jnp.sum(onehot * rewards[:, None], 0) / counts
    centred = rewards - jnp.sum(onehot * means[None, :], 1)
    spreads = jnp.sqrt(jnp.sum(onehot * (centred * centred)[:, None], 0) / counts)
    divisor = jnp.maximum(jnp.sum(onehot * spreads[None, :], 1), spread_floor)
    return centred / divisor / lengths.astype(F32)


def pack_kernel(weighted, spot_ref, weight_ref, target_ref, *refs):
    pieces, (far_ref, near_ref, stage, held, arrived) = refs[:-5], refs[-5:]
    copies = [
        pltpu.make_async_copy(piece, stage.at[p], arrived.at[p])
        for p, piece in enumerate(pieces)
    ]
    for copy in copies:
        copy.start()
    held[...] = jnp.zeros_like(held)
    for p, copy in enumerate(copies):
        copy.wait()
        for k in range(PER_OWNER):
            at = p * PER_OWNER + k
            block = stage[p, k]
            if weighted:
                block = (block.astype(F32) * weight_ref[at]).astype(BF)
            held[pl.ds(pl.multiple_of(spot_ref[at] * SLOTS, SLOTS), SLOTS), :] = block
    span = PER_OWNER * SLOTS
    places = lax.broadcasted_iota(jnp.int32, (CAPR, span), 0)
    for owner in range(OWNERS):
        onehot = (places == target_ref[owner]).astype(F32).astype(BF)
        rows = held[owner * span : (owner + 1) * span, :]
        out = jnp.dot(onehot, rows, preferred_element_type=F32).astype(BF)
        if owner < 4:
            far_ref[owner * CAPR : (owner + 1) * CAPR, :] = out
        else:
            near_ref[(owner - 4) * CAPR : (owner - 3) * CAPR, :] = out


def pack(spots, weights, targets, pieces, weighted):
    shape = pieces[0].shape
    width, count = shape[2], len(pieces)
    scalars, arrays = pl.BlockSpec(memory_space=pltpu.SMEM), pl.BlockSpec(memory_space=pltpu.VMEM)
    return pl.pallas_call(
        lambda *refs: pack_kernel(weighted, *refs),
        in_specs=[scalars, scalars, arrays] + [pl.BlockSpec(memory_space=pltpu.HBM)] * count,
        out_specs=[arrays, arrays],
        out_shape=[
            jax.ShapeDtypeStruct((4 * CAPR, width), BF),
            jax.ShapeDtypeStruct((12 * CAPR, width), BF),
        ],
        scratch_shapes=[
            pltpu.VMEM((count, *shape), BF),
            pltpu.VMEM((OWNERS * PER_OWNER * SLOTS, width), BF),
            pltpu.SemaphoreType.DMA((count,)),
        ],
        compiler_params=pltpu.CompilerParams(vmem_limit_bytes=24 << 20),
        cost_estimate=pl.CostEstimate(
            flops=2 * 2048 * 384 * 512, bytes_accessed=9 << 20, transcendentals=0
        ),
    )(spots, weights, targets, *pieces)


def input_grad_kernel(ahead, blocks, at_ref, *refs):
    parts, weights_ref, (kept_ref, sent_ref) = refs[:blocks], refs[blocks], refs[-2:]
    z = lax.rem(at_ref[0] + ahead, 4)
    for first in range(0, weights_ref.shape[1], 512):
        columns = slice(first, first + 512)
        out, row = None, 0
        for part in parts:
            term = lax.dot_general(
                part[...],
                weights_ref[row : row + part.shape[0], columns],
                (((0,), (0,)), ((), ())),
                preferred_element_type=F32,
            )
            out = term if out is None else out + term
            row += part.shape[0]
        out = out.astype(BF)
        for owner in range(4):
            y = lax.rem(at_ref[1] + owner // 2, 2)
            tile = out[owner * CAPR : (owner + 1) * CAPR]

            @pl.when(at_ref[2] == owner % 2)
            def _(tile=tile, y=y, columns=columns):
                kept_ref[z, y, :, columns] = tile

            @pl.when(at_ref[2] != owner % 2)
            def _(tile=tile, y=y, columns=columns):
                sent_ref[z, y, :, columns] = tile


def input_grads(ahead, at, parts, weights, so_far):
    arrays = pl.BlockSpec(memory_space=pltpu.VMEM)
    units, width = weights.shape
    count = 2 + len(parts)
    return pl.pallas_call(
        lambda *refs: input_grad_kernel(ahead, len(parts), *refs),
        in_specs=[pl.BlockSpec(memory_space=pltpu.SMEM)]
        + [arrays] * (count - 1)
        + [pl.BlockSpec(memory_space=pl.ANY)] * len(so_far),
        out_specs=[arrays] * 2,
        out_shape=[jax.ShapeDtypeStruct((4, 2, CAPR, width), BF)] * 2,
        input_output_aliases={count + k: k for k in range(len(so_far))},
        compiler_params=pltpu.CompilerParams(vmem_limit_bytes=24 << 20),
        cost_estimate=pl.CostEstimate(
            flops=2 * units * 512 * width, bytes_accessed=4 << 20, transcendentals=0
        ),
    )(at, *parts, weights, *so_far)


def product_kernel(counts, *refs):
    near_ref, far_ref, mine_ref, sent_ref = refs[-4:]
    chunks, used = [], 0
    for count in counts:
        chunks.append(refs[used : used + count])
        used += count
    rows = mine_ref.shape[0] // len(chunks[3])
    for out_ref, first in ((mine_ref, 0), (sent_ref, 512)):
        for block in range(len(chunks[3])):
            at = slice(block * rows, (block + 1) * rows)
            total = jnp.dot(
                chunks[3][block][...], far_ref[:, first : first + 512], preferred_element_type=F32
            )
            for k in range(3):
                left = chunks[k][0][at, :] if len(chunks[k]) == 1 else chunks[k][block][...]
                total += jnp.dot(
                    left,
                    near_ref[k * 512 : (k + 1) * 512, first : first + 512],
                    preferred_element_type=F32,
                )
            out_ref[at, :] = total.astype(BF)


def token_product(chunks, near, far):
    units = sum(block.shape[0] for block in chunks[0])
    counts = [len(chunk) for chunk in chunks]
    return pl.pallas_call(
        lambda *refs: product_kernel(counts, *refs),
        in_specs=[pl.BlockSpec(memory_space=pltpu.VMEM)] * (sum(counts) + 2),
        out_specs=[pl.BlockSpec(memory_space=pltpu.VMEM)] * 2,
        out_shape=[jax.ShapeDtypeStruct((units, 512), BF)] * 2,
        compiler_params=pltpu.CompilerParams(vmem_limit_bytes=40 << 20),
        cost_estimate=pl.CostEstimate(
            flops=2 * units * 2048 * 1024, bytes_accessed=10 << 20, transcendentals=0
        ),
    )(*[block for chunk in chunks for block in chunk], near, far)


def gathered_rows(piece, z_up, z_down, y_hi, beside=None):
    other = y_hi(piece)
    below, above = z_up(piece), z_down(piece)
    below_other, above_other = z_up(other), z_down(other)
    met = () if beside is None else (beside(other),)
    far, far_other = z_up(after(below, *met)), z_down(after(above_other, *met))
    return [piece, other, above, above_other, far, far_other, below, below_other]


def per_device(
    roll_hidden,
    roll_cotangent,
    lengths,
    owners,
    prompts,
    rewards,
    gate_weight,
    up_weight,
    down_weight,
):
    slot_count, full = roll_hidden.shape
    cols = lax.axis_size("col")
    width = full // cols
    r_at, c_at = lax.axis_index("row"), lax.axis_index("col")

    high = lax.reduce_precision(rewards, 8, 7)
    middle = lax.reduce_precision(rewards - high, 8, 7)
    low = rewards - high - middle
    numbers = jnp.stack(
        [lengths.astype(F32), owners.astype(F32), prompts.astype(F32), high, middle, low], axis=1
    )
    numbers = jnp.pad(numbers.astype(BF), ((0, SLOTS - slot_count - 1), (0, width - 6)))
    numbers = jnp.broadcast_to(numbers[None], (cols, SLOTS - slot_count, width))

    def blocks(array):
        return jnp.moveaxis(array.reshape(slot_count, cols, width), 1, 0)

    both = jnp.concatenate(
        [
            blocks(roll_hidden),
            numbers,
            blocks(roll_cotangent),
            jnp.zeros((cols, SLOTS - slot_count, width), BF),
        ],
        axis=1,
    )
    both = lax.all_to_all(both, "col", 0, 0, tiled=True)
    hidden_piece, grad_piece = both[:, :SLOTS], both[:, SLOTS:]

    x_at, odd, second_core = c_at // 2, c_at % 2 == 1, r_at % 2 == 1
    x_up, x_down, y_lo = Link("col", X_UP), Link("col", X_DOWN), Link("col", Y_LO, 1)
    z_up, z_down, core = Link("row", Z_UP, 1), Link("row", Z_DOWN, 1), Link("row", CORE)
    y_hi = Link("row", Y_HI, 1)

    units = down_weight.shape[0] // 2
    padded = -(-units // 16) * 16

    def split_units(weight):
        halves = [
            jnp.pad(weight[k * units : (k + 1) * units], ((0, padded - units), (0, 0)))
            for k in range(2)
        ]
        return jnp.where(odd, halves[1], halves[0]), jnp.where(odd, halves[0], halves[1])

    gate_mine, gate_sent = split_units(gate_weight.T)
    up_mine, up_sent = split_units(up_weight.T)
    down_mine, down_sent = split_units(down_weight)
    received = []

    def send_gate(other):
        received.append(y_lo(after(gate_sent, other)))
        return received[-1]

    hidden_pieces = gathered_rows(hidden_piece, z_up, z_down, y_hi, send_gate)
    received.append(y_lo(up_sent))
    gate_up_weights = jnp.concatenate(
        [
            jnp.concatenate([gate_mine, received[0]], 1),
            jnp.concatenate([up_mine, received[1]], 1),
        ]
    )
    grad_piece = after(grad_piece, hidden_pieces[4], hidden_pieces[5])
    grad_pieces = gathered_rows(grad_piece, z_up, z_down, y_hi)
    early = (grad_pieces[1], grad_pieces[2], grad_pieces[6])
    later, last = (grad_pieces[3], grad_pieces[7]), (grad_pieces[4], grad_pieces[5])

    told = jnp.concatenate([piece[:, slot_count, :8] for piece in hidden_pieces]).astype(F32)
    told = jnp.concatenate([told, core(after(told, received[1]))])
    all_lengths = told[:, 0].astype(jnp.int32)
    all_owners = told[:, 1].astype(jnp.int32)
    all_prompts = told[:, 2].astype(jnp.int32)
    weights = row_weights(all_lengths, all_prompts, told[:, 3] + told[:, 4] + told[:, 5])
    places = jnp.arange(OWNERS * cols, dtype=jnp.int32)
    step = places // cols
    ids = (
        ((r_at // 4 + step // 2 % 4) % 4) * 4
        + ((r_at // 2 % 2) ^ (step % 2)) * 2
        + ((r_at % 2) ^ (step // 8))
    ) * cols + places % cols
    earlier = (all_owners[None, :] == all_owners[:, None]) & (ids[None, :] < ids[:, None])
    offsets = jnp.sum(jnp.where(earlier, all_lengths[None, :], 0), 1)
    ranks = jnp.sum(earlier.astype(jnp.int32), 1)
    ahead = (all_owners // 4 - x_at) % 4
    ahead = jnp.where(ahead == 0, 3, jnp.where(ahead == 1, 1, jnp.where(ahead == 2, 0, 2)))
    spot = (ahead * 4 + all_owners % 4) * PER_OWNER + ranks
    own = OWNERS * cols // 2
    chosen = (spot[None, :] == places[:, None]) & (places[None, :] < own)

    def sort(values):
        return jnp.sum(jnp.where(chosen, values[None, :], 0), 1)[:, None]

    slots = jnp.arange(SLOTS, dtype=jnp.int32)[None, :]
    targets = jnp.where(slots < sort(all_lengths), sort(offsets) + slots, -1)
    targets = targets.reshape(OWNERS, 1, PER_OWNER * SLOTS)

    def paired(tokens, *met):
        whole = add(tokens, core(tokens)).astype(BF)
        n = whole.shape[0] // 2
        got = y_lo(jnp.where(second_core, whole[n:], whole[:n]))
        got = after(got, *met) if met else got
        other = core(got)
        first, second = jnp.where(second_core, other, got), jnp.where(second_core, got, other)
        return jnp.concatenate([whole, jnp.concatenate([first, second])], 1)

    def multiplied(weights, tokens):
        dims = (((1,), (1,)), ((), ()))
        return lax.dot_general(weights, tokens, dims, preferred_element_type=F32).astype(BF)

    spots = spot[:own]
    packed_far, packed_near = pack(spots, weights[:own], targets, hidden_pieces, False)
    x_far = paired(after(packed_far, *early), *later)
    gate_up = [multiplied(gate_up_weights, x_far)]
    gate_far, up_far = x_up(gate_up[0][:padded]), x_down(gate_up[0][padded:])
    spots = after(spots, gate_up[0])
    grad_far, grad_near = pack(spots, weights[:own], targets, grad_pieces, True)
    x_near = paired(packed_near, gate_far, up_far, grad_far, *last)
    gate_up += [multiplied(gate_up_weights, x_near[k * 512 : (k + 1) * 512]) for k in range(3)]
    (gate_1, gate_3, gate_0) = (part[:padded] for part in gate_up[1:])
    (up_1, up_3, up_0) = (part[padded:] for part in gate_up[1:])
    up_below, gate_above = x_up(up_1), x_down(gate_3)
    gate_below = x_up(add(gate_1, gate_far).astype(BF))
    up_above = x_down(add(up_3, up_far).astype(BF))
    gate, upval = add(gate_0, gate_below, gate_above), add(up_0, up_below, up_above)
    sig = jax.nn.sigmoid(gate)
    silu = gate * sig
    hidden = (silu * upval).astype(BF)

    middle = padded // 2
    hidden_below, hidden_above = x_up(hidden), x_down(hidden)
    hidden_far = [x_up(hidden_below[:middle]), x_down(hidden_above[middle:])]

    g_far, g_near = paired(grad_far), paired(grad_near)
    down_weights = jnp.concatenate([down_mine, y_lo(down_sent)], 1)
    grad_2 = multiplied(down_weights, g_far)
    grad_1, grad_3, grad_0 = (
        multiplied(down_weights, g_near[k * 512 : (k + 1) * 512]) for k in range(3)
    )
    far_1, far_2 = x_up(grad_2[:middle]), x_down(grad_2[middle:])
    below_2, above_1 = x_up(grad_1[middle:]), x_down(grad_3[:middle])
    below_1 = x_up(add(grad_1[:middle], far_1).astype(BF))
    above_2 = x_down(add(grad_3[middle:], far_2).astype(BF))
    grad_hidden = jnp.concatenate(
        [add(grad_0[:middle], below_1, above_1), add(grad_0[middle:], below_2, above_2)]
    )
    gate_act = (grad_hidden * upval * sig * (1.0 + gate * (1.0 - sig))).astype(BF)
    up_act = (grad_hidden * silu).astype(BF)

    def exchanged(mine, sent):
        got = y_lo(sent)
        out = []
        for k in range(mine.shape[0] // padded):
            one, two = (v[k * padded : k * padded + units] for v in (mine, got))
            out.append(
                jnp.where(odd, jnp.concatenate([two, one]), jnp.concatenate([one, two]))
            )
        return out, got

    gate_act_below, up_act_above = x_up(gate_act), x_down(up_act)
    up_act_below, gate_act_above = x_up(up_act), x_down(gate_act)
    act, act_below = [gate_act, up_act], [gate_act_below, up_act_below]
    act_above = [gate_act_above, up_act_above]
    (grad_down,), got_down = exchanged(
        *token_product([[hidden_above], [hidden_below], [hidden], hidden_far], g_near, g_far)
    )
    at = jnp.stack([x_at - r_at // 4 + 4, r_at // 2 % 2, r_at % 2]).astype(jnp.int32)
    tiles = input_grads(0, at, act, gate_up_weights, [])
    act_far = [x_up(after(gate_act_below, got_down)), x_down(up_act_above)]

    tiles = input_grads(1, at, act_above, gate_up_weights, tiles)
    tiles = input_grads(3, at, act_below, gate_up_weights, tiles)
    kept, sent = input_grads(2, at, act_far, gate_up_weights, tiles)
    z_up, z_down = Link("row", Z_UP), Link("row", Z_DOWN)
    sent = core(sent)
    weight_grads = token_product([act_above, act_below, act, act_far], x_near, x_far)
    (grad_gate, grad_up), _ = exchanged(*weight_grads)
    tiles = add(after(kept, weight_grads[0]), sent).astype(BF)
    far_1, far_0 = z_up(tiles[2, 1]), z_down(tiles[2, 0])
    below_0, above_1 = z_up(tiles[1, 0]), z_down(tiles[3, 1])
    below_1 = z_up(add(tiles[1, 1], far_1).astype(BF))
    above_0 = z_down(add(tiles[3, 0], far_0).astype(BF))
    other = y_hi(add(tiles[0, 1], below_1, above_1).astype(BF))
    tiles = add(tiles[0, 0], below_0, above_0, other)

    grad_input = add(tiles[:, :width], y_lo(tiles[:, width:].astype(BF))).astype(BF)
    return grad_input, grad_gate.T, grad_up.T, grad_down


def solution(mesh):
    return jax.shard_map(
        per_device,
        mesh=mesh,
        in_specs=(
            P(("row", "col"), None),
            P(("row", "col"), None),
            P(("row", "col")),
            P(("row", "col")),
            P(("row", "col")),
            P(("row", "col")),
            P("col", "row"),
            P("col", "row"),
            P("row", "col"),
        ),
        out_specs=(P("row", "col"), P("col", "row"), P("col", "row"), P("row", "col")),
        check_vma=False,
    )
```

```python
import jax
import jax.numpy as jnp
from jax import lax
from jax.experimental import pallas as pl
from jax.experimental.pallas import tpu as pltpu
from jax.sharding import PartitionSpec as P

CAPR = 128
OWNERS = 16
PER_OWNER = 8
PROMPTS = 16
SLOTS = 48
spread_floor = 0.7
BF = jnp.bfloat16
F32 = jnp.float32

X_UP = [(i, ((i // 2 + 1) % 4) * 2 + i % 2) for i in range(8)]
X_DOWN = [(i, ((i // 2 + 3) % 4) * 2 + i % 2) for i in range(8)]
Y_LO = [(i, i ^ 1) for i in range(8)]
Z_UP = [(i, ((i // 4 + 1) % 4) * 4 + i % 4) for i in range(16)]
Z_DOWN = [(i, ((i // 4 + 3) % 4) * 4 + i % 4) for i in range(16)]
Y_HI = [(i, i ^ 2) for i in range(16)]
CORE = [(i, i ^ 1) for i in range(16)]


def after(value, *earlier):
    return lax.optimization_barrier((value, *earlier))[0]


def row(value, pairs):
    return lax.ppermute(value, "row", pairs)


class Link:
    def __init__(self, axis, pairs, most=2):
        self.axis, self.pairs, self.most, self.got = axis, pairs, most, []

    def __call__(self, value):
        if len(self.got) >= self.most:
            value = after(value, self.got[-self.most])
        self.got.append(lax.ppermute(value, self.axis, self.pairs))
        return self.got[-1]


def add(*terms):
    total = terms[0].astype(F32)
    for term in terms[1:]:
        total = total + term.astype(F32)
    return total


def row_weights(lengths, prompts, rewards):
    onehot = (prompts[:, None] == jnp.arange(PROMPTS, dtype=jnp.int32)[None, :]).astype(F32)
    counts = jnp.maximum(jnp.sum(onehot, 0), 1.0)
    means = jnp.sum(onehot * rewards[:, None], 0) / counts
    centred = rewards - jnp.sum(onehot * means[None, :], 1)
    spreads = jnp.sqrt(jnp.sum(onehot * (centred * centred)[:, None], 0) / counts)
    divisor = jnp.maximum(jnp.sum(onehot * spreads[None, :], 1), spread_floor)
    return centred / divisor / lengths.astype(F32)


def pack_kernel(weighted, spot_ref, weight_ref, target_ref, *refs):
    pieces, (far_ref, near_ref, stage, held, arrived) = refs[:-5], refs[-5:]
    copies = [
        pltpu.make_async_copy(piece, stage.at[p], arrived.at[p])
        for p, piece in enumerate(pieces)
    ]
    for copy in copies:
        copy.start()
    held[...] = jnp.zeros_like(held)
    for p, copy in enumerate(copies):
        copy.wait()
        for k in range(PER_OWNER):
            at = p * PER_OWNER + k
            block = stage[p, k]
            if weighted:
                block = (block.astype(F32) * weight_ref[at]).astype(BF)
            held[pl.ds(pl.multiple_of(spot_ref[at] * SLOTS, SLOTS), SLOTS), :] = block
    span = PER_OWNER * SLOTS
    places = lax.broadcasted_iota(jnp.int32, (CAPR, span), 0)
    for owner in range(OWNERS):
        onehot = (places == target_ref[owner]).astype(F32).astype(BF)
        rows = held[owner * span : (owner + 1) * span, :]
        out = jnp.dot(onehot, rows, preferred_element_type=F32).astype(BF)
        if owner < 4:
            far_ref[owner * CAPR : (owner + 1) * CAPR, :] = out
        else:
            near_ref[(owner - 4) * CAPR : (owner - 3) * CAPR, :] = out


def pack(spots, weights, targets, pieces, weighted):
    shape = pieces[0].shape
    width, count = shape[2], len(pieces)
    scalars, arrays = pl.BlockSpec(memory_space=pltpu.SMEM), pl.BlockSpec(memory_space=pltpu.VMEM)
    return pl.pallas_call(
        lambda *refs: pack_kernel(weighted, *refs),
        in_specs=[scalars, scalars, arrays] + [pl.BlockSpec(memory_space=pltpu.HBM)] * count,
        out_specs=[arrays, arrays],
        out_shape=[
            jax.ShapeDtypeStruct((4 * CAPR, width), BF),
            jax.ShapeDtypeStruct((12 * CAPR, width), BF),
        ],
        scratch_shapes=[
            pltpu.VMEM((count, *shape), BF),
            pltpu.VMEM((OWNERS * PER_OWNER * SLOTS, width), BF),
            pltpu.SemaphoreType.DMA((count,)),
        ],
        compiler_params=pltpu.CompilerParams(vmem_limit_bytes=24 << 20),
        cost_estimate=pl.CostEstimate(
            flops=2 * 2048 * 384 * 512, bytes_accessed=9 << 20, transcendentals=0
        ),
    )(spots, weights, targets, *pieces)


def input_grad_kernel(ahead, blocks, at_ref, *refs):
    parts, weights_ref, (kept_ref, sent_ref) = refs[:blocks], refs[blocks], refs[-2:]
    z = lax.rem(at_ref[0] + ahead, 4)
    for first in range(0, weights_ref.shape[1], 512):
        columns = slice(first, first + 512)
        out, row = None, 0
        for part in parts:
            term = lax.dot_general(
                part[...],
                weights_ref[row : row + part.shape[0], columns],
                (((0,), (0,)), ((), ())),
                preferred_element_type=F32,
            )
            out = term if out is None else out + term
            row += part.shape[0]
        out = out.astype(BF)
        for owner in range(4):
            y = lax.rem(at_ref[1] + owner // 2, 2)
            tile = out[owner * CAPR : (owner + 1) * CAPR]

            @pl.when(at_ref[2] == owner % 2)
            def _(tile=tile, y=y, columns=columns):
                kept_ref[z, y, :, columns] = tile

            @pl.when(at_ref[2] != owner % 2)
            def _(tile=tile, y=y, columns=columns):
                sent_ref[z, y, :, columns] = tile


def input_grads(ahead, at, parts, weights, so_far):
    arrays = pl.BlockSpec(memory_space=pltpu.VMEM)
    units, width = weights.shape
    count = 2 + len(parts)
    return pl.pallas_call(
        lambda *refs: input_grad_kernel(ahead, len(parts), *refs),
        in_specs=[pl.BlockSpec(memory_space=pltpu.SMEM)]
        + [arrays] * (count - 1)
        + [pl.BlockSpec(memory_space=pl.ANY)] * len(so_far),
        out_specs=[arrays] * 2,
        out_shape=[jax.ShapeDtypeStruct((4, 2, CAPR, width), BF)] * 2,
        input_output_aliases={count + k: k for k in range(len(so_far))},
        compiler_params=pltpu.CompilerParams(vmem_limit_bytes=24 << 20),
        cost_estimate=pl.CostEstimate(
            flops=2 * units * 512 * width, bytes_accessed=4 << 20, transcendentals=0
        ),
    )(at, *parts, weights, *so_far)


def product_kernel(counts, *refs):
    near_ref, far_ref, mine_ref, sent_ref = refs[-4:]
    chunks, used = [], 0
    for count in counts:
        chunks.append(refs[used : used + count])
        used += count
    rows = mine_ref.shape[0] // len(chunks[3])
    for out_ref, first in ((mine_ref, 0), (sent_ref, 512)):
        for block in range(len(chunks[3])):
            at = slice(block * rows, (block + 1) * rows)
            total = jnp.dot(
                chunks[3][block][...], far_ref[:, first : first + 512], preferred_element_type=F32
            )
            for k in range(3):
                left = chunks[k][0][at, :] if len(chunks[k]) == 1 else chunks[k][block][...]
                total += jnp.dot(
                    left,
                    near_ref[k * 512 : (k + 1) * 512, first : first + 512],
                    preferred_element_type=F32,
                )
            out_ref[at, :] = total.astype(BF)


def token_product(chunks, near, far):
    units = sum(block.shape[0] for block in chunks[0])
    counts = [len(chunk) for chunk in chunks]
    return pl.pallas_call(
        lambda *refs: product_kernel(counts, *refs),
        in_specs=[pl.BlockSpec(memory_space=pltpu.VMEM)] * (sum(counts) + 2),
        out_specs=[pl.BlockSpec(memory_space=pltpu.VMEM)] * 2,
        out_shape=[jax.ShapeDtypeStruct((units, 512), BF)] * 2,
        compiler_params=pltpu.CompilerParams(vmem_limit_bytes=40 << 20),
        cost_estimate=pl.CostEstimate(
            flops=2 * units * 2048 * 1024, bytes_accessed=10 << 20, transcendentals=0
        ),
    )(*[block for chunk in chunks for block in chunk], near, far)


def gathered_rows(piece, other, z_up, z_down, met=()):
    below, above = z_up(piece), z_down(piece)
    below_other, above_other = z_up(other), z_down(other)
    far, far_other = z_up(after(below, *met)), z_down(after(above_other, *met))
    return [piece, other, above, above_other, far, far_other, below, below_other]


def per_device(
    roll_hidden,
    roll_cotangent,
    lengths,
    owners,
    prompts,
    rewards,
    gate_weight,
    up_weight,
    down_weight,
):
    slot_count, full = roll_hidden.shape
    cols = lax.axis_size("col")
    width = full // cols
    r_at, c_at = lax.axis_index("row"), lax.axis_index("col")

    high = lax.reduce_precision(rewards, 8, 7)
    middle = lax.reduce_precision(rewards - high, 8, 7)
    low = rewards - high - middle
    numbers = jnp.stack(
        [lengths.astype(F32), owners.astype(F32), prompts.astype(F32), high, middle, low], axis=1
    )
    numbers = jnp.pad(numbers.astype(BF), ((0, SLOTS - slot_count - 1), (0, width - 6)))
    numbers = jnp.broadcast_to(numbers[None], (cols, SLOTS - slot_count, width))

    def blocks(array):
        return jnp.moveaxis(array.reshape(slot_count, cols, width), 1, 0)

    both = jnp.concatenate(
        [
            blocks(roll_hidden),
            numbers,
            blocks(roll_cotangent),
            jnp.zeros((cols, SLOTS - slot_count, width), BF),
        ],
        axis=1,
    )
    both = lax.all_to_all(both, "col", 0, 0, tiled=True)
    hidden_piece, grad_piece = both[:, :SLOTS], both[:, SLOTS:]

    x_at, odd, second_core = c_at // 2, c_at % 2 == 1, r_at % 2 == 1
    x_up, x_down, y_lo = Link("col", X_UP), Link("col", X_DOWN), Link("col", Y_LO, 1)
    z_up, z_down, core = Link("row", Z_UP, 1), Link("row", Z_DOWN, 1), Link("row", CORE)
    y_hi = Link("row", Y_HI, 1)

    units = down_weight.shape[0] // 2
    padded = -(-units // 16) * 16

    def split_units(weight):
        halves = [
            jnp.pad(weight[k * units : (k + 1) * units], ((0, padded - units), (0, 0)))
            for k in range(2)
        ]
        return jnp.where(odd, halves[1], halves[0]), jnp.where(odd, halves[0], halves[1])

    gate_mine, gate_sent = split_units(gate_weight.T)
    up_mine, up_sent = split_units(up_weight.T)
    down_mine, down_sent = split_units(down_weight)
    received = []

    hidden_other = y_hi(hidden_piece)
    received.append(y_lo(after(gate_sent, hidden_other)))

    told = both[:, slot_count, :8].astype(F32)
    told = jnp.concatenate([told, row(told, CORE)])
    told = jnp.concatenate([told, row(told, Y_HI)])
    told = after(told, hidden_other)
    told_below, told_above = row(told, Z_UP), row(told, Z_DOWN)
    told = jnp.stack([told, told_above, row(told_below, Z_UP), told_below])
    told = told.reshape(4, 2, 2, cols, 8).transpose(2, 0, 1, 3, 4).reshape(OWNERS * cols, 8)
    all_lengths = told[:, 0].astype(jnp.int32)
    all_owners = told[:, 1].astype(jnp.int32)
    all_prompts = told[:, 2].astype(jnp.int32)
    weights = row_weights(all_lengths, all_prompts, told[:, 3] + told[:, 4] + told[:, 5])
    places = jnp.arange(OWNERS * cols, dtype=jnp.int32)
    step = places // cols
    ids = (
        ((r_at // 4 + step // 2 % 4) % 4) * 4
        + ((r_at // 2 % 2) ^ (step % 2)) * 2
        + ((r_at % 2) ^ (step // 8))
    ) * cols + places % cols
    earlier = (all_owners[None, :] == all_owners[:, None]) & (ids[None, :] < ids[:, None])
    offsets = jnp.sum(jnp.where(earlier, all_lengths[None, :], 0), 1)
    ranks = jnp.sum(earlier.astype(jnp.int32), 1)
    ahead = (all_owners // 4 - x_at) % 4
    ahead = jnp.where(ahead == 0, 3, jnp.where(ahead == 1, 1, jnp.where(ahead == 2, 0, 2)))
    spot = (ahead * 4 + all_owners % 4) * PER_OWNER + ranks
    own = OWNERS * cols // 2
    chosen = (spot[None, :] == places[:, None]) & (places[None, :] < own)

    def sort(values):
        return jnp.sum(jnp.where(chosen, values[None, :], 0), 1)[:, None]

    slots = jnp.arange(SLOTS, dtype=jnp.int32)[None, :]
    targets = jnp.where(slots < sort(all_lengths), sort(offsets) + slots, -1)
    targets = targets.reshape(OWNERS, 1, PER_OWNER * SLOTS)

    spots = spot[:own]
    met = (received[0], spots, targets)
    hidden_pieces = gathered_rows(hidden_piece, hidden_other, z_up, z_down, met)
    received.append(y_lo(up_sent))
    gate_up_weights = jnp.concatenate(
        [
            jnp.concatenate([gate_mine, received[0]], 1),
            jnp.concatenate([up_mine, received[1]], 1),
        ]
    )
    grad_piece = after(grad_piece, hidden_pieces[4], hidden_pieces[5])
    grad_pieces = gathered_rows(grad_piece, y_hi(grad_piece), z_up, z_down)
    early = (grad_pieces[1], grad_pieces[2], grad_pieces[6], received[1])
    later, last = (grad_pieces[3], grad_pieces[7]), (grad_pieces[4], grad_pieces[5])

    def paired(tokens, *met):
        whole = add(tokens, core(tokens)).astype(BF)
        n = whole.shape[0] // 2
        got = y_lo(jnp.where(second_core, whole[n:], whole[:n]))
        got = after(got, *met) if met else got
        other = core(got)
        first, second = jnp.where(second_core, other, got), jnp.where(second_core, got, other)
        return jnp.concatenate([whole, jnp.concatenate([first, second])], 1)

    def multiplied(weights, tokens):
        dims = (((1,), (1,)), ((), ()))
        return lax.dot_general(weights, tokens, dims, preferred_element_type=F32).astype(BF)

    packed_far, packed_near = pack(spots, weights[:own], targets, hidden_pieces, False)
    x_far = paired(after(packed_far, *early), *later)
    gate_up = [multiplied(gate_up_weights, x_far)]
    gate_far, up_far = x_up(gate_up[0][:padded]), x_down(gate_up[0][padded:])
    spots = after(spots, gate_up[0])
    grad_far, grad_near = pack(spots, weights[:own], targets, grad_pieces, True)
    x_near = paired(packed_near, gate_far, up_far, grad_far, *last)
    gate_up += [multiplied(gate_up_weights, x_near[k * 512 : (k + 1) * 512]) for k in range(3)]
    (gate_1, gate_3, gate_0) = (part[:padded] for part in gate_up[1:])
    (up_1, up_3, up_0) = (part[padded:] for part in gate_up[1:])
    up_below, gate_above = x_up(up_1), x_down(gate_3)
    gate_below = x_up(add(gate_1, gate_far).astype(BF))
    up_above = x_down(add(up_3, up_far).astype(BF))
    gate, upval = add(gate_0, gate_below, gate_above), add(up_0, up_below, up_above)
    sig = jax.nn.sigmoid(gate)
    silu = gate * sig
    hidden = (silu * upval).astype(BF)

    middle = padded // 2
    hidden_below, hidden_above = x_up(hidden), x_down(hidden)
    hidden_far = [x_up(hidden_below[:middle]), x_down(hidden_above[middle:])]

    g_far, g_near = paired(grad_far), paired(grad_near)
    down_weights = jnp.concatenate([down_mine, y_lo(down_sent)], 1)
    grad_2 = multiplied(down_weights, g_far)
    grad_1, grad_3, grad_0 = (
        multiplied(down_weights, g_near[k * 512 : (k + 1) * 512]) for k in range(3)
    )
    far_1, far_2 = x_up(grad_2[:middle]), x_down(grad_2[middle:])
    below_2, above_1 = x_up(grad_1[middle:]), x_down(grad_3[:middle])
    below_1 = x_up(add(grad_1[:middle], far_1).astype(BF))
    above_2 = x_down(add(grad_3[middle:], far_2).astype(BF))
    grad_hidden = jnp.concatenate(
        [add(grad_0[:middle], below_1, above_1), add(grad_0[middle:], below_2, above_2)]
    )
    gate_act = (grad_hidden * upval * sig * (1.0 + gate * (1.0 - sig))).astype(BF)
    up_act = (grad_hidden * silu).astype(BF)

    def exchanged(mine, sent):
        got = y_lo(sent)
        out = []
        for k in range(mine.shape[0] // padded):
            one, two = (v[k * padded : k * padded + units] for v in (mine, got))
            out.append(
                jnp.where(odd, jnp.concatenate([two, one]), jnp.concatenate([one, two]))
            )
        return out, got

    gate_act_below, up_act_above = x_up(gate_act), x_down(up_act)
    up_act_below, gate_act_above = x_up(up_act), x_down(gate_act)
    act, act_below = [gate_act, up_act], [gate_act_below, up_act_below]
    act_above = [gate_act_above, up_act_above]
    (grad_down,), got_down = exchanged(
        *token_product([[hidden_above], [hidden_below], [hidden], hidden_far], g_near, g_far)
    )
    at = jnp.stack([x_at - r_at // 4 + 4, r_at // 2 % 2, r_at % 2]).astype(jnp.int32)
    tiles = input_grads(0, at, act, gate_up_weights, [])
    act_far = [x_up(after(gate_act_below, got_down)), x_down(up_act_above)]

    tiles = input_grads(1, at, act_above, gate_up_weights, tiles)
    tiles = input_grads(3, at, act_below, gate_up_weights, tiles)
    kept, sent = input_grads(2, at, act_far, gate_up_weights, tiles)
    z_up, z_down = Link("row", Z_UP), Link("row", Z_DOWN)
    sent = core(sent)
    weight_grads = token_product([act_above, act_below, act, act_far], x_near, x_far)
    (grad_gate, grad_up), _ = exchanged(*weight_grads)
    tiles = add(after(kept, weight_grads[0]), sent).astype(BF)
    far_1, far_0 = z_up(tiles[2, 1]), z_down(tiles[2, 0])
    above_1 = z_down(tiles[3, 1])
    below_1 = z_up(add(tiles[1, 1], far_1).astype(BF))
    below_0 = z_up(tiles[1, 0])
    above_0 = z_down(add(tiles[3, 0], far_0).astype(BF))
    other = y_hi(add(tiles[0, 1], below_1, above_1).astype(BF))
    tiles = add(tiles[0, 0], below_0, above_0, other)

    grad_input = add(tiles[:, :width], y_lo(tiles[:, width:].astype(BF))).astype(BF)
    return grad_input, grad_gate.T, grad_up.T, grad_down


def solution(mesh):
    return jax.shard_map(
        per_device,
        mesh=mesh,
        in_specs=(
            P(("row", "col"), None),
            P(("row", "col"), None),
            P(("row", "col")),
            P(("row", "col")),
            P(("row", "col")),
            P(("row", "col")),
            P("col", "row"),
            P("col", "row"),
            P("row", "col"),
        ),
        out_specs=(P("row", "col"), P("col", "row"), P("col", "row"), P("row", "col")),
        check_vma=False,
    )
```

```python
import jax
import jax.numpy as jnp
from jax import lax
from jax.experimental import pallas as pl
from jax.experimental.pallas import tpu as pltpu
from jax.sharding import PartitionSpec as P

CAPR = 128
OWNERS = 16
PER_OWNER = 8
PROMPTS = 16
SLOTS = 48
spread_floor = 0.7
BF = jnp.bfloat16
F32 = jnp.float32

X_UP = [(i, ((i // 2 + 1) % 4) * 2 + i % 2) for i in range(8)]
X_DOWN = [(i, ((i // 2 + 3) % 4) * 2 + i % 2) for i in range(8)]
Y_LO = [(i, i ^ 1) for i in range(8)]
Z_UP = [(i, ((i // 4 + 1) % 4) * 4 + i % 4) for i in range(16)]
Z_DOWN = [(i, ((i // 4 + 3) % 4) * 4 + i % 4) for i in range(16)]
Y_HI = [(i, i ^ 2) for i in range(16)]
CORE = [(i, i ^ 1) for i in range(16)]


def after(value, *earlier):
    return lax.optimization_barrier((value, *earlier))[0]


def row(value, pairs):
    return lax.ppermute(value, "row", pairs)


class Link:
    def __init__(self, axis, pairs, most=2):
        self.axis, self.pairs, self.most, self.got = axis, pairs, most, []

    def __call__(self, value):
        if len(self.got) >= self.most:
            value = after(value, self.got[-self.most])
        self.got.append(lax.ppermute(value, self.axis, self.pairs))
        return self.got[-1]


def add(*terms):
    total = terms[0].astype(F32)
    for term in terms[1:]:
        total = total + term.astype(F32)
    return total


def row_weights(lengths, prompts, rewards):
    onehot = (prompts[:, None] == jnp.arange(PROMPTS, dtype=jnp.int32)[None, :]).astype(F32)
    counts = jnp.maximum(jnp.sum(onehot, 0), 1.0)
    means = jnp.sum(onehot * rewards[:, None], 0) / counts
    centred = rewards - jnp.sum(onehot * means[None, :], 1)
    spreads = jnp.sqrt(jnp.sum(onehot * (centred * centred)[:, None], 0) / counts)
    divisor = jnp.maximum(jnp.sum(onehot * spreads[None, :], 1), spread_floor)
    return centred / divisor / lengths.astype(F32)


def pack_kernel(weighted, spot_ref, weight_ref, target_ref, *refs):
    pieces, (far_ref, near_ref, stage, held, arrived) = refs[:-5], refs[-5:]
    copies = [
        pltpu.make_async_copy(piece, stage.at[p], arrived.at[p])
        for p, piece in enumerate(pieces)
    ]
    for copy in copies:
        copy.start()
    held[...] = jnp.zeros_like(held)
    for p, copy in enumerate(copies):
        copy.wait()
        for k in range(PER_OWNER):
            at = p * PER_OWNER + k
            block = stage[p, k]
            if weighted:
                block = (block.astype(F32) * weight_ref[at]).astype(BF)
            held[pl.ds(pl.multiple_of(spot_ref[at] * SLOTS, SLOTS), SLOTS), :] = block
    span = PER_OWNER * SLOTS
    places = lax.broadcasted_iota(jnp.int32, (CAPR, span), 0)
    for owner in range(OWNERS):
        onehot = (places == target_ref[owner]).astype(F32).astype(BF)
        rows = held[owner * span : (owner + 1) * span, :]
        out = jnp.dot(onehot, rows, preferred_element_type=F32).astype(BF)
        if owner < 4:
            far_ref[owner * CAPR : (owner + 1) * CAPR, :] = out
        else:
            near_ref[(owner - 4) * CAPR : (owner - 3) * CAPR, :] = out


def pack(spots, weights, targets, pieces, weighted):
    shape = pieces[0].shape
    width, count = shape[2], len(pieces)
    scalars, arrays = pl.BlockSpec(memory_space=pltpu.SMEM), pl.BlockSpec(memory_space=pltpu.VMEM)
    return pl.pallas_call(
        lambda *refs: pack_kernel(weighted, *refs),
        in_specs=[scalars, scalars, arrays] + [pl.BlockSpec(memory_space=pltpu.HBM)] * count,
        out_specs=[arrays, arrays],
        out_shape=[
            jax.ShapeDtypeStruct((4 * CAPR, width), BF),
            jax.ShapeDtypeStruct((12 * CAPR, width), BF),
        ],
        scratch_shapes=[
            pltpu.VMEM((count, *shape), BF),
            pltpu.VMEM((OWNERS * PER_OWNER * SLOTS, width), BF),
            pltpu.SemaphoreType.DMA((count,)),
        ],
        compiler_params=pltpu.CompilerParams(vmem_limit_bytes=24 << 20),
        cost_estimate=pl.CostEstimate(
            flops=2 * 2048 * 384 * 512, bytes_accessed=9 << 20, transcendentals=0
        ),
    )(spots, weights, targets, *pieces)


def input_grad_kernel(ahead, blocks, at_ref, *refs):
    parts, weights_ref, (kept_ref, sent_ref) = refs[:blocks], refs[blocks], refs[-2:]
    z = lax.rem(at_ref[0] + ahead, 4)
    for first in range(0, weights_ref.shape[1], 512):
        columns = slice(first, first + 512)
        out, row = None, 0
        for part in parts:
            term = lax.dot_general(
                part[...],
                weights_ref[row : row + part.shape[0], columns],
                (((0,), (0,)), ((), ())),
                preferred_element_type=F32,
            )
            out = term if out is None else out + term
            row += part.shape[0]
        out = out.astype(BF)
        for owner in range(4):
            y = lax.rem(at_ref[1] + owner // 2, 2)
            tile = out[owner * CAPR : (owner + 1) * CAPR]

            @pl.when(at_ref[2] == owner % 2)
            def _(tile=tile, y=y, columns=columns):
                kept_ref[z, y, :, columns] = tile

            @pl.when(at_ref[2] != owner % 2)
            def _(tile=tile, y=y, columns=columns):
                sent_ref[z, y, :, columns] = tile


def input_grads(ahead, at, parts, weights, so_far):
    arrays = pl.BlockSpec(memory_space=pltpu.VMEM)
    units, width = weights.shape
    count = 2 + len(parts)
    return pl.pallas_call(
        lambda *refs: input_grad_kernel(ahead, len(parts), *refs),
        in_specs=[pl.BlockSpec(memory_space=pltpu.SMEM)]
        + [arrays] * (count - 1)
        + [pl.BlockSpec(memory_space=pl.ANY)] * len(so_far),
        out_specs=[arrays] * 2,
        out_shape=[jax.ShapeDtypeStruct((4, 2, CAPR, width), BF)] * 2,
        input_output_aliases={count + k: k for k in range(len(so_far))},
        compiler_params=pltpu.CompilerParams(vmem_limit_bytes=24 << 20),
        cost_estimate=pl.CostEstimate(
            flops=2 * units * 512 * width, bytes_accessed=4 << 20, transcendentals=0
        ),
    )(at, *parts, weights, *so_far)


def product_kernel(counts, *refs):
    near_ref, far_ref, mine_ref, sent_ref = refs[-4:]
    chunks, used = [], 0
    for count in counts:
        chunks.append(refs[used : used + count])
        used += count
    rows = mine_ref.shape[0] // len(chunks[3])
    for out_ref, first in ((mine_ref, 0), (sent_ref, 512)):
        for block in range(len(chunks[3])):
            at = slice(block * rows, (block + 1) * rows)
            total = jnp.dot(
                chunks[3][block][...], far_ref[:, first : first + 512], preferred_element_type=F32
            )
            for k in range(3):
                left = chunks[k][0][at, :] if len(chunks[k]) == 1 else chunks[k][block][...]
                total += jnp.dot(
                    left,
                    near_ref[k * 512 : (k + 1) * 512, first : first + 512],
                    preferred_element_type=F32,
                )
            out_ref[at, :] = total.astype(BF)


def token_product(chunks, near, far):
    units = sum(block.shape[0] for block in chunks[0])
    counts = [len(chunk) for chunk in chunks]
    return pl.pallas_call(
        lambda *refs: product_kernel(counts, *refs),
        in_specs=[pl.BlockSpec(memory_space=pltpu.VMEM)] * (sum(counts) + 2),
        out_specs=[pl.BlockSpec(memory_space=pltpu.VMEM)] * 2,
        out_shape=[jax.ShapeDtypeStruct((units, 512), BF)] * 2,
        compiler_params=pltpu.CompilerParams(vmem_limit_bytes=40 << 20),
        cost_estimate=pl.CostEstimate(
            flops=2 * units * 2048 * 1024, bytes_accessed=10 << 20, transcendentals=0
        ),
    )(*[block for chunk in chunks for block in chunk], near, far)


def gathered_rows(piece, other, z_up, z_down, soon=(), met=()):
    below, above = z_up(piece), z_down(piece)
    other = after(other, *soon)
    below_other, above_other = z_up(other), z_down(other)
    far, far_other = z_up(after(below, *met)), z_down(after(above_other, *met))
    return [piece, other, above, above_other, far, far_other, below, below_other]


def per_device(
    roll_hidden,
    roll_cotangent,
    lengths,
    owners,
    prompts,
    rewards,
    gate_weight,
    up_weight,
    down_weight,
):
    slot_count, full = roll_hidden.shape
    cols = lax.axis_size("col")
    width = full // cols
    r_at, c_at = lax.axis_index("row"), lax.axis_index("col")

    high = lax.reduce_precision(rewards, 8, 7)
    middle = lax.reduce_precision(rewards - high, 8, 7)
    low = rewards - high - middle
    numbers = jnp.stack(
        [lengths.astype(F32), owners.astype(F32), prompts.astype(F32), high, middle, low], axis=1
    )
    numbers = jnp.pad(numbers.astype(BF), ((0, SLOTS - slot_count - 1), (0, width - 6)))
    numbers = jnp.broadcast_to(numbers[None], (cols, SLOTS - slot_count, width))

    def blocks(array):
        return jnp.moveaxis(array.reshape(slot_count, cols, width), 1, 0)

    both = jnp.concatenate(
        [
            blocks(roll_hidden),
            numbers,
            blocks(roll_cotangent),
            jnp.zeros((cols, SLOTS - slot_count, width), BF),
        ],
        axis=1,
    )
    both = lax.all_to_all(both, "col", 0, 0, tiled=True)
    hidden_piece, grad_piece = both[:, :SLOTS], both[:, SLOTS:]

    x_at, odd, second_core = c_at // 2, c_at % 2 == 1, r_at % 2 == 1
    x_up, x_down, y_lo = Link("col", X_UP), Link("col", X_DOWN), Link("col", Y_LO, 1)
    z_up, z_down, core = Link("row", Z_UP, 1), Link("row", Z_DOWN, 1), Link("row", CORE)
    y_hi = Link("row", Y_HI, 1)

    units = down_weight.shape[0] // 2
    padded = -(-units // 16) * 16

    def split_units(weight):
        halves = [
            jnp.pad(weight[k * units : (k + 1) * units], ((0, padded - units), (0, 0)))
            for k in range(2)
        ]
        return jnp.where(odd, halves[1], halves[0]), jnp.where(odd, halves[0], halves[1])

    gate_mine, gate_sent = split_units(gate_weight.T)
    up_mine, up_sent = split_units(up_weight.T)
    down_mine, down_sent = split_units(down_weight)
    received = []

    hidden_other = y_hi(hidden_piece)
    received.append(y_lo(after(gate_sent, hidden_other)))

    told = both[:, slot_count, :8].astype(F32)
    told = jnp.concatenate([told, row(told, CORE)])
    told = jnp.concatenate([told, row(told, Y_HI)])
    told = after(told, hidden_other)
    told_below, told_above = row(told, Z_UP), row(told, Z_DOWN)
    told = jnp.stack([told, told_above, row(told_below, Z_UP), told_below])
    told = told.reshape(4, 2, 2, cols, 8).transpose(2, 0, 1, 3, 4).reshape(OWNERS * cols, 8)
    all_lengths = told[:, 0].astype(jnp.int32)
    all_owners = told[:, 1].astype(jnp.int32)
    all_prompts = told[:, 2].astype(jnp.int32)
    weights = row_weights(all_lengths, all_prompts, told[:, 3] + told[:, 4] + told[:, 5])
    places = jnp.arange(OWNERS * cols, dtype=jnp.int32)
    step = places // cols
    ids = (
        ((r_at // 4 + step // 2 % 4) % 4) * 4
        + ((r_at // 2 % 2) ^ (step % 2)) * 2
        + ((r_at % 2) ^ (step // 8))
    ) * cols + places % cols
    earlier = (all_owners[None, :] == all_owners[:, None]) & (ids[None, :] < ids[:, None])
    offsets = jnp.sum(jnp.where(earlier, all_lengths[None, :], 0), 1)
    ranks = jnp.sum(earlier.astype(jnp.int32), 1)
    ahead = (all_owners // 4 - x_at) % 4
    ahead = jnp.where(ahead == 0, 3, jnp.where(ahead == 1, 1, jnp.where(ahead == 2, 0, 2)))
    spot = (ahead * 4 + all_owners % 4) * PER_OWNER + ranks
    own = OWNERS * cols // 2
    chosen = (spot[None, :] == places[:, None]) & (places[None, :] < own)

    def sort(values):
        return jnp.sum(jnp.where(chosen, values[None, :], 0), 1)[:, None]

    slots = jnp.arange(SLOTS, dtype=jnp.int32)[None, :]
    targets = jnp.where(slots < sort(all_lengths), sort(offsets) + slots, -1)
    targets = targets.reshape(OWNERS, 1, PER_OWNER * SLOTS)

    spots = spot[:own]
    received.append(y_lo(up_sent))
    hidden_pieces = gathered_rows(
        hidden_piece, hidden_other, z_up, z_down, (), (received[0], told_above)
    )
    spots = after(spots, received[1])
    packed_far, packed_near = pack(spots, weights[:own], targets, hidden_pieces, False)
    gate_up_weights = jnp.concatenate(
        [
            jnp.concatenate([gate_mine, received[0]], 1),
            jnp.concatenate([up_mine, received[1]], 1),
        ]
    )
    def both_cores(tokens):
        whole = add(tokens, core(tokens)).astype(BF)
        n = whole.shape[0] // 2
        return whole, jnp.where(second_core, whole[n:], whole[:n])

    cores_far, cores_near = both_cores(packed_far), both_cores(packed_near)
    far_got = y_lo(cores_far[1])
    grad_piece = after(grad_piece, packed_far)
    grad_pieces = gathered_rows(grad_piece, y_hi(grad_piece), z_up, z_down, (far_got,))
    early = (grad_pieces[1], grad_pieces[2], grad_pieces[6])
    last = (grad_pieces[4], grad_pieces[5])

    def paired(whole, got, *met):
        got = after(got, *met) if met else got
        other = core(got)
        first, second = jnp.where(second_core, other, got), jnp.where(second_core, got, other)
        return jnp.concatenate([whole, jnp.concatenate([first, second])], 1)

    def multiplied(weights, tokens):
        dims = (((1,), (1,)), ((), ()))
        return lax.dot_general(weights, tokens, dims, preferred_element_type=F32).astype(BF)

    x_far = paired(cores_far[0], far_got, cores_near[1], *early)
    gate_up = [multiplied(gate_up_weights, x_far)]
    gate_far, up_far = x_up(gate_up[0][:padded]), x_down(gate_up[0][padded:])
    spots = after(spots, gate_up[0])
    grad_far, grad_near = pack(spots, weights[:own], targets, grad_pieces, True)
    x_near = paired(cores_near[0], y_lo(cores_near[1]), gate_far, up_far, grad_far, *last)
    gate_up += [multiplied(gate_up_weights, x_near[k * 512 : (k + 1) * 512]) for k in range(3)]
    (gate_1, gate_3, gate_0) = (part[:padded] for part in gate_up[1:])
    (up_1, up_3, up_0) = (part[padded:] for part in gate_up[1:])
    up_below, gate_above = x_up(up_1), x_down(gate_3)
    gate_below = x_up(add(gate_1, gate_far).astype(BF))
    up_above = x_down(add(up_3, up_far).astype(BF))
    gate, upval = add(gate_0, gate_below, gate_above), add(up_0, up_below, up_above)
    sig = jax.nn.sigmoid(gate)
    silu = gate * sig
    hidden = (silu * upval).astype(BF)

    middle = padded // 2
    hidden_below, hidden_above = x_up(hidden), x_down(hidden)
    hidden_far = [x_up(hidden_below[:middle]), x_down(hidden_above[middle:])]

    g_far, g_near = (
        paired(whole, y_lo(half)) for whole, half in map(both_cores, (grad_far, grad_near))
    )
    down_weights = jnp.concatenate([down_mine, y_lo(down_sent)], 1)
    grad_2 = multiplied(down_weights, g_far)
    grad_1, grad_3, grad_0 = (
        multiplied(down_weights, g_near[k * 512 : (k + 1) * 512]) for k in range(3)
    )
    far_1, far_2 = x_up(grad_2[:middle]), x_down(grad_2[middle:])
    below_2, above_1 = x_up(grad_1[middle:]), x_down(grad_3[:middle])
    below_1 = x_up(add(grad_1[:middle], far_1).astype(BF))
    above_2 = x_down(add(grad_3[middle:], far_2).astype(BF))
    grad_hidden = jnp.concatenate(
        [add(grad_0[:middle], below_1, above_1), add(grad_0[middle:], below_2, above_2)]
    )
    gate_act = (grad_hidden * upval * sig * (1.0 + gate * (1.0 - sig))).astype(BF)
    up_act = (grad_hidden * silu).astype(BF)

    def exchanged(mine, sent):
        got = y_lo(sent)
        out = []
        for k in range(mine.shape[0] // padded):
            one, two = (v[k * padded : k * padded + units] for v in (mine, got))
            out.append(
                jnp.where(odd, jnp.concatenate([two, one]), jnp.concatenate([one, two]))
            )
        return out, got

    gate_act_below, up_act_above = x_up(gate_act), x_down(up_act)
    up_act_below, gate_act_above = x_up(up_act), x_down(gate_act)
    act, act_below = [gate_act, up_act], [gate_act_below, up_act_below]
    act_above = [gate_act_above, up_act_above]
    (grad_down,), got_down = exchanged(
        *token_product([[hidden_above], [hidden_below], [hidden], hidden_far], g_near, g_far)
    )
    at = jnp.stack([x_at - r_at // 4 + 4, r_at // 2 % 2, r_at % 2]).astype(jnp.int32)
    tiles = input_grads(0, at, act, gate_up_weights, [])
    act_far = [x_up(after(gate_act_below, got_down)), x_down(up_act_above)]

    tiles = input_grads(1, at, act_above, gate_up_weights, tiles)
    tiles = input_grads(3, at, act_below, gate_up_weights, tiles)
    kept, sent = input_grads(2, at, act_far, gate_up_weights, tiles)
    z_up, z_down = Link("row", Z_UP), Link("row", Z_DOWN)
    sent = core(sent)
    weight_grads = token_product([act_above, act_below, act, act_far], x_near, x_far)
    (grad_gate, grad_up), _ = exchanged(*weight_grads)
    tiles = add(after(kept, weight_grads[0]), sent).astype(BF)
    far_1, far_0 = z_up(tiles[2, 1]), z_down(tiles[2, 0])
    above_1 = z_down(tiles[3, 1])
    below_1 = z_up(add(tiles[1, 1], far_1).astype(BF))
    below_0 = z_up(tiles[1, 0])
    above_0 = z_down(add(tiles[3, 0], far_0).astype(BF))
    other = y_hi(add(tiles[0, 1], below_1, above_1).astype(BF))
    tiles = add(tiles[0, 0], below_0, above_0, other)

    grad_input = add(tiles[:, :width], y_lo(tiles[:, width:].astype(BF))).astype(BF)
    return grad_input, grad_gate.T, grad_up.T, grad_down


def solution(mesh):
    return jax.shard_map(
        per_device,
        mesh=mesh,
        in_specs=(
            P(("row", "col"), None),
            P(("row", "col"), None),
            P(("row", "col")),
            P(("row", "col")),
            P(("row", "col")),
            P(("row", "col")),
            P("col", "row"),
            P("col", "row"),
            P("row", "col"),
        ),
        out_specs=(P("row", "col"), P("col", "row"), P("col", "row"), P("row", "col")),
        check_vma=False,
    )
```

```python
import jax
import jax.numpy as jnp
from jax import lax
from jax.experimental import pallas as pl
from jax.experimental.pallas import tpu as pltpu
from jax.sharding import PartitionSpec as P

CAPR = 128
OWNERS = 16
PER_OWNER = 8
PROMPTS = 16
SLOTS = 48
spread_floor = 0.7
BF = jnp.bfloat16
F32 = jnp.float32

X_UP = [(i, ((i // 2 + 1) % 4) * 2 + i % 2) for i in range(8)]
X_DOWN = [(i, ((i // 2 + 3) % 4) * 2 + i % 2) for i in range(8)]
Y_LO = [(i, i ^ 1) for i in range(8)]
Z_UP = [(i, ((i // 4 + 1) % 4) * 4 + i % 4) for i in range(16)]
Z_DOWN = [(i, ((i // 4 + 3) % 4) * 4 + i % 4) for i in range(16)]
Y_HI = [(i, i ^ 2) for i in range(16)]
CORE = [(i, i ^ 1) for i in range(16)]


def after(value, *earlier):
    return lax.optimization_barrier((value, *earlier))[0]


def row(value, pairs):
    return lax.ppermute(value, "row", pairs)


class Link:
    def __init__(self, axis, pairs, most=2):
        self.axis, self.pairs, self.most, self.got = axis, pairs, most, []

    def __call__(self, value):
        if len(self.got) >= self.most:
            value = after(value, self.got[-self.most])
        self.got.append(lax.ppermute(value, self.axis, self.pairs))
        return self.got[-1]


def add(*terms):
    total = terms[0].astype(F32)
    for term in terms[1:]:
        total = total + term.astype(F32)
    return total


def row_weights(lengths, prompts, rewards):
    onehot = (prompts[:, None] == jnp.arange(PROMPTS, dtype=jnp.int32)[None, :]).astype(F32)
    counts = jnp.maximum(jnp.sum(onehot, 0), 1.0)
    means = jnp.sum(onehot * rewards[:, None], 0) / counts
    centred = rewards - jnp.sum(onehot * means[None, :], 1)
    spreads = jnp.sqrt(jnp.sum(onehot * (centred * centred)[:, None], 0) / counts)
    divisor = jnp.maximum(jnp.sum(onehot * spreads[None, :], 1), spread_floor)
    return centred / divisor / lengths.astype(F32)


def pack_kernel(weighted, spot_ref, weight_ref, target_ref, *refs):
    pieces, (far_ref, near_ref, stage, held, arrived) = refs[:-5], refs[-5:]
    copies = [
        pltpu.make_async_copy(piece, stage.at[p], arrived.at[p])
        for p, piece in enumerate(pieces)
    ]
    for copy in copies:
        copy.start()
    held[...] = jnp.zeros_like(held)
    for p, copy in enumerate(copies):
        copy.wait()
        for k in range(PER_OWNER):
            at = p * PER_OWNER + k
            block = stage[p, k]
            if weighted:
                block = (block.astype(F32) * weight_ref[at]).astype(BF)
            held[pl.ds(pl.multiple_of(spot_ref[at] * SLOTS, SLOTS), SLOTS), :] = block
    span = PER_OWNER * SLOTS
    places = lax.broadcasted_iota(jnp.int32, (CAPR, span), 0)
    for owner in range(OWNERS):
        onehot = (places == target_ref[owner]).astype(F32).astype(BF)
        rows = held[owner * span : (owner + 1) * span, :]
        out = jnp.dot(onehot, rows, preferred_element_type=F32).astype(BF)
        if owner < 4:
            far_ref[owner * CAPR : (owner + 1) * CAPR, :] = out
        else:
            near_ref[(owner - 4) * CAPR : (owner - 3) * CAPR, :] = out


def pack(spots, weights, targets, pieces, weighted):
    shape = pieces[0].shape
    width, count = shape[2], len(pieces)
    scalars, arrays = pl.BlockSpec(memory_space=pltpu.SMEM), pl.BlockSpec(memory_space=pltpu.VMEM)
    return pl.pallas_call(
        lambda *refs: pack_kernel(weighted, *refs),
        in_specs=[scalars, scalars, arrays] + [pl.BlockSpec(memory_space=pltpu.HBM)] * count,
        out_specs=[arrays, arrays],
        out_shape=[
            jax.ShapeDtypeStruct((4 * CAPR, width), BF),
            jax.ShapeDtypeStruct((12 * CAPR, width), BF),
        ],
        scratch_shapes=[
            pltpu.VMEM((count, *shape), BF),
            pltpu.VMEM((OWNERS * PER_OWNER * SLOTS, width), BF),
            pltpu.SemaphoreType.DMA((count,)),
        ],
        compiler_params=pltpu.CompilerParams(vmem_limit_bytes=24 << 20),
        cost_estimate=pl.CostEstimate(
            flops=2 * 2048 * 384 * 512, bytes_accessed=9 << 20, transcendentals=0
        ),
    )(spots, weights, targets, *pieces)


def input_grad_kernel(ahead, blocks, at_ref, *refs):
    parts, weights_ref, (kept_ref, sent_ref) = refs[:blocks], refs[blocks], refs[-2:]
    z = lax.rem(at_ref[0] + ahead, 4)
    for first in range(0, weights_ref.shape[1], 512):
        columns = slice(first, first + 512)
        out, row = None, 0
        for part in parts:
            term = lax.dot_general(
                part[...],
                weights_ref[row : row + part.shape[0], columns],
                (((0,), (0,)), ((), ())),
                preferred_element_type=F32,
            )
            out = term if out is None else out + term
            row += part.shape[0]
        out = out.astype(BF)
        for owner in range(4):
            y = lax.rem(at_ref[1] + owner // 2, 2)
            tile = out[owner * CAPR : (owner + 1) * CAPR]

            @pl.when(at_ref[2] == owner % 2)
            def _(tile=tile, y=y, columns=columns):
                kept_ref[z, y, :, columns] = tile

            @pl.when(at_ref[2] != owner % 2)
            def _(tile=tile, y=y, columns=columns):
                sent_ref[z, y, :, columns] = tile


def input_grads(ahead, at, parts, weights, so_far):
    arrays = pl.BlockSpec(memory_space=pltpu.VMEM)
    units, width = weights.shape
    count = 2 + len(parts)
    return pl.pallas_call(
        lambda *refs: input_grad_kernel(ahead, len(parts), *refs),
        in_specs=[pl.BlockSpec(memory_space=pltpu.SMEM)]
        + [arrays] * (count - 1)
        + [pl.BlockSpec(memory_space=pl.ANY)] * len(so_far),
        out_specs=[arrays] * 2,
        out_shape=[jax.ShapeDtypeStruct((4, 2, CAPR, width), BF)] * 2,
        input_output_aliases={count + k: k for k in range(len(so_far))},
        compiler_params=pltpu.CompilerParams(vmem_limit_bytes=24 << 20),
        cost_estimate=pl.CostEstimate(
            flops=2 * units * 512 * width, bytes_accessed=4 << 20, transcendentals=0
        ),
    )(at, *parts, weights, *so_far)


def product_kernel(counts, *refs):
    near_ref, far_ref, mine_ref, sent_ref = refs[-4:]
    chunks, used = [], 0
    for count in counts:
        chunks.append(refs[used : used + count])
        used += count
    rows = mine_ref.shape[0] // len(chunks[3])
    for out_ref, first in ((mine_ref, 0), (sent_ref, 512)):
        for block in range(len(chunks[3])):
            at = slice(block * rows, (block + 1) * rows)
            total = jnp.dot(
                chunks[3][block][...], far_ref[:, first : first + 512], preferred_element_type=F32
            )
            for k in range(3):
                left = chunks[k][0][at, :] if len(chunks[k]) == 1 else chunks[k][block][...]
                total += jnp.dot(
                    left,
                    near_ref[k * 512 : (k + 1) * 512, first : first + 512],
                    preferred_element_type=F32,
                )
            out_ref[at, :] = total.astype(BF)


def token_product(chunks, near, far):
    units = sum(block.shape[0] for block in chunks[0])
    counts = [len(chunk) for chunk in chunks]
    return pl.pallas_call(
        lambda *refs: product_kernel(counts, *refs),
        in_specs=[pl.BlockSpec(memory_space=pltpu.VMEM)] * (sum(counts) + 2),
        out_specs=[pl.BlockSpec(memory_space=pltpu.VMEM)] * 2,
        out_shape=[jax.ShapeDtypeStruct((units, 512), BF)] * 2,
        compiler_params=pltpu.CompilerParams(vmem_limit_bytes=40 << 20),
        cost_estimate=pl.CostEstimate(
            flops=2 * units * 2048 * 1024, bytes_accessed=10 << 20, transcendentals=0
        ),
    )(*[block for chunk in chunks for block in chunk], near, far)


def gathered_rows(piece, other, below, above, z_up, z_down, soon=(), met=()):
    other = after(other, *soon) if soon else other
    below_other, above_other = z_up(other), z_down(other)
    start, start_other = below, above_other
    if met:
        start, start_other = after(below, *met), after(above_other, *met)
    far, far_other = z_up(start), z_down(start_other)
    return [piece, other, above, above_other, far, far_other, below, below_other]


def per_device(
    roll_hidden,
    roll_cotangent,
    lengths,
    owners,
    prompts,
    rewards,
    gate_weight,
    up_weight,
    down_weight,
):
    slot_count, full = roll_hidden.shape
    cols = lax.axis_size("col")
    width = full // cols
    r_at, c_at = lax.axis_index("row"), lax.axis_index("col")

    high = lax.reduce_precision(rewards, 8, 7)
    middle = lax.reduce_precision(rewards - high, 8, 7)
    low = rewards - high - middle
    numbers = jnp.stack(
        [lengths.astype(F32), owners.astype(F32), prompts.astype(F32), high, middle, low], axis=1
    )
    numbers = jnp.pad(numbers.astype(BF), ((0, SLOTS - slot_count - 1), (0, width - 6)))
    numbers = jnp.broadcast_to(numbers[None], (cols, SLOTS - slot_count, width))

    def blocks(array):
        return jnp.moveaxis(array.reshape(slot_count, cols, width), 1, 0)

    both = jnp.concatenate(
        [
            blocks(roll_hidden),
            numbers,
            blocks(roll_cotangent),
            jnp.zeros((cols, SLOTS - slot_count, width), BF),
        ],
        axis=1,
    )
    both = lax.all_to_all(both, "col", 0, 0, tiled=True)
    hidden_piece, grad_piece = both[:, :SLOTS], both[:, SLOTS:]

    x_at, odd, second_core = c_at // 2, c_at % 2 == 1, r_at % 2 == 1
    x_up, x_down, y_lo = Link("col", X_UP), Link("col", X_DOWN), Link("col", Y_LO, 1)
    z_up, z_down, core = Link("row", Z_UP, 1), Link("row", Z_DOWN, 1), Link("row", CORE)
    y_hi = Link("row", Y_HI, 1)

    units = down_weight.shape[0] // 2
    padded = -(-units // 16) * 16

    def split_units(weight):
        halves = [
            jnp.pad(weight[k * units : (k + 1) * units], ((0, padded - units), (0, 0)))
            for k in range(2)
        ]
        return jnp.where(odd, halves[1], halves[0]), jnp.where(odd, halves[0], halves[1])

    gate_mine, gate_sent = split_units(gate_weight.T)
    up_mine, up_sent = split_units(up_weight.T)
    down_mine, down_sent = split_units(down_weight)
    received = []

    hidden_other = y_hi(hidden_piece)
    received.append(y_lo(after(gate_sent, hidden_other)))

    told = both[:, slot_count, :8].astype(F32)
    told = jnp.concatenate([told, row(told, CORE)])
    told = jnp.concatenate([told, row(told, Y_HI)])
    told = after(told, hidden_other)
    told_below, told_above = row(told, Z_UP), row(told, Z_DOWN)
    told = jnp.stack([told, told_above, row(told_below, Z_UP), told_below])
    told = told.reshape(4, 2, 2, cols, 8).transpose(2, 0, 1, 3, 4).reshape(OWNERS * cols, 8)
    all_lengths = told[:, 0].astype(jnp.int32)
    all_owners = told[:, 1].astype(jnp.int32)
    all_prompts = told[:, 2].astype(jnp.int32)
    weights = row_weights(all_lengths, all_prompts, told[:, 3] + told[:, 4] + told[:, 5])
    places = jnp.arange(OWNERS * cols, dtype=jnp.int32)
    step = places // cols
    ids = (
        ((r_at // 4 + step // 2 % 4) % 4) * 4
        + ((r_at // 2 % 2) ^ (step % 2)) * 2
        + ((r_at % 2) ^ (step // 8))
    ) * cols + places % cols
    earlier = (all_owners[None, :] == all_owners[:, None]) & (ids[None, :] < ids[:, None])
    offsets = jnp.sum(jnp.where(earlier, all_lengths[None, :], 0), 1)
    ranks = jnp.sum(earlier.astype(jnp.int32), 1)
    ahead = (all_owners // 4 - x_at) % 4
    ahead = jnp.where(ahead == 0, 3, jnp.where(ahead == 1, 1, jnp.where(ahead == 2, 0, 2)))
    spot = (ahead * 4 + all_owners % 4) * PER_OWNER + ranks
    own = OWNERS * cols // 2
    chosen = (spot[None, :] == places[:, None]) & (places[None, :] < own)

    def sort(values):
        return jnp.sum(jnp.where(chosen, values[None, :], 0), 1)[:, None]

    slots = jnp.arange(SLOTS, dtype=jnp.int32)[None, :]
    targets = jnp.where(slots < sort(all_lengths), sort(offsets) + slots, -1)
    targets = targets.reshape(OWNERS, 1, PER_OWNER * SLOTS)

    spots = spot[:own]
    received.append(y_lo(up_sent))
    hidden_pieces = gathered_rows(
        hidden_piece,
        hidden_other,
        z_up(hidden_piece),
        z_down(hidden_piece),
        z_up,
        z_down,
        (),
        (received[0], told_above),
    )
    spots = after(spots, received[1])
    packed_far, packed_near = pack(spots, weights[:own], targets, hidden_pieces, False)
    gate_up_weights = jnp.concatenate(
        [
            jnp.concatenate([gate_mine, received[0]], 1),
            jnp.concatenate([up_mine, received[1]], 1),
        ]
    )
    def both_cores(tokens):
        whole = add(tokens, core(tokens)).astype(BF)
        n = whole.shape[0] // 2
        return whole, jnp.where(second_core, whole[n:], whole[:n])

    cores_far, cores_near = both_cores(packed_far), both_cores(packed_near)
    far_got = y_lo(cores_far[1])
    grad_piece = after(grad_piece, packed_far)
    early = (z_up(grad_piece), z_down(grad_piece))

    def paired(whole, got, *met):
        got = after(got, *met) if met else got
        other = core(got)
        first, second = jnp.where(second_core, other, got), jnp.where(second_core, got, other)
        return jnp.concatenate([whole, jnp.concatenate([first, second])], 1)

    def multiplied(weights, tokens):
        dims = (((1,), (1,)), ((), ()))
        return lax.dot_general(weights, tokens, dims, preferred_element_type=F32).astype(BF)

    x_far = paired(cores_far[0], far_got, cores_near[1], *early)
    gate_up = [multiplied(gate_up_weights, x_far)]
    gate_2, up_2 = lax.optimization_barrier((gate_up[0][:padded], gate_up[0][padded:]))
    gate_far, up_far = x_up(gate_2), x_down(up_2)
    near_got = y_lo(cores_near[1])
    grad_pieces = gathered_rows(
        grad_piece, y_hi(grad_piece), *early, z_up, z_down, (far_got,), (gate_2, up_2)
    )
    grad_far, grad_near = pack(spots, weights[:own], targets, grad_pieces, True)
    x_near = paired(cores_near[0], near_got, gate_far, up_far, grad_pieces[3], grad_pieces[7])
    gate_up += [multiplied(gate_up_weights, x_near[k * 512 : (k + 1) * 512]) for k in range(3)]
    (gate_1, gate_3, gate_0) = (part[:padded] for part in gate_up[1:])
    (up_1, up_3, up_0) = (part[padded:] for part in gate_up[1:])
    up_below, gate_above = x_up(up_1), x_down(gate_3)
    gate_below = x_up(add(gate_1, gate_far).astype(BF))
    up_above = x_down(add(up_3, up_far).astype(BF))
    gate, upval = add(gate_0, gate_below, gate_above), add(up_0, up_below, up_above)
    sig = jax.nn.sigmoid(gate)
    silu = gate * sig
    hidden = (silu * upval).astype(BF)

    middle = padded // 2
    hidden_below, hidden_above = x_up(hidden), x_down(hidden)
    hidden_far = [x_up(hidden_below[:middle]), x_down(hidden_above[middle:])]

    g_far, g_near = (
        paired(whole, y_lo(half)) for whole, half in map(both_cores, (grad_far, grad_near))
    )
    down_weights = jnp.concatenate([down_mine, y_lo(down_sent)], 1)
    grad_2 = multiplied(down_weights, g_far)
    grad_1, grad_3, grad_0 = (
        multiplied(down_weights, g_near[k * 512 : (k + 1) * 512]) for k in range(3)
    )
    far_1, far_2 = x_up(grad_2[:middle]), x_down(grad_2[middle:])
    below_2, above_1 = x_up(grad_1[middle:]), x_down(grad_3[:middle])
    below_1 = x_up(add(grad_1[:middle], far_1).astype(BF))
    above_2 = x_down(add(grad_3[middle:], far_2).astype(BF))
    grad_hidden = jnp.concatenate(
        [add(grad_0[:middle], below_1, above_1), add(grad_0[middle:], below_2, above_2)]
    )
    gate_act = (grad_hidden * upval * sig * (1.0 + gate * (1.0 - sig))).astype(BF)
    up_act = (grad_hidden * silu).astype(BF)

    def exchanged(mine, sent):
        got = y_lo(sent)
        out = []
        for k in range(mine.shape[0] // padded):
            one, two = (v[k * padded : k * padded + units] for v in (mine, got))
            out.append(
                jnp.where(odd, jnp.concatenate([two, one]), jnp.concatenate([one, two]))
            )
        return out, got

    gate_act_below, up_act_above = x_up(gate_act), x_down(up_act)
    up_act_below, gate_act_above = x_up(up_act), x_down(gate_act)
    act, act_below = [gate_act, up_act], [gate_act_below, up_act_below]
    act_above = [gate_act_above, up_act_above]
    (grad_down,), got_down = exchanged(
        *token_product([[hidden_above], [hidden_below], [hidden], hidden_far], g_near, g_far)
    )
    at = jnp.stack([x_at - r_at // 4 + 4, r_at // 2 % 2, r_at % 2]).astype(jnp.int32)
    tiles = input_grads(0, at, act, gate_up_weights, [])
    act_far = [x_up(after(gate_act_below, got_down)), x_down(up_act_above)]

    tiles = input_grads(1, at, act_above, gate_up_weights, tiles)
    tiles = input_grads(3, at, act_below, gate_up_weights, tiles)
    kept, sent = input_grads(2, at, act_far, gate_up_weights, tiles)
    z_up, z_down = Link("row", Z_UP), Link("row", Z_DOWN)
    sent = core(sent)
    weight_grads = token_product([act_above, act_below, act, act_far], x_near, x_far)
    (grad_gate, grad_up), _ = exchanged(*weight_grads)
    tiles = add(after(kept, weight_grads[0]), sent).astype(BF)
    far_1, far_0 = z_up(tiles[2, 1]), z_down(tiles[2, 0])
    above_1 = z_down(tiles[3, 1])
    below_1 = z_up(add(tiles[1, 1], far_1).astype(BF))
    below_0 = z_up(tiles[1, 0])
    above_0 = z_down(add(tiles[3, 0], far_0).astype(BF))
    other = y_hi(add(tiles[0, 1], below_1, above_1).astype(BF))
    tiles = add(tiles[0, 0], below_0, above_0, other)

    grad_input = add(tiles[:, :width], y_lo(tiles[:, width:].astype(BF))).astype(BF)
    return grad_input, grad_gate.T, grad_up.T, grad_down


def solution(mesh):
    return jax.shard_map(
        per_device,
        mesh=mesh,
        in_specs=(
            P(("row", "col"), None),
            P(("row", "col"), None),
            P(("row", "col")),
            P(("row", "col")),
            P(("row", "col")),
            P(("row", "col")),
            P("col", "row"),
            P("col", "row"),
            P("row", "col"),
        ),
        out_specs=(P("row", "col"), P("col", "row"), P("col", "row"), P("row", "col")),
        check_vma=False,
    )
```

```python
import jax
import jax.numpy as jnp
from jax import lax
from jax.experimental import pallas as pl
from jax.experimental.pallas import tpu as pltpu
from jax.sharding import PartitionSpec as P

CAPR = 128
OWNERS = 16
PER_OWNER = 8
PROMPTS = 16
SLOTS = 48
spread_floor = 0.7
BF = jnp.bfloat16
F32 = jnp.float32

X_UP = [(i, ((i // 2 + 1) % 4) * 2 + i % 2) for i in range(8)]
X_DOWN = [(i, ((i // 2 + 3) % 4) * 2 + i % 2) for i in range(8)]
Y_LO = [(i, i ^ 1) for i in range(8)]
Z_UP = [(i, ((i // 4 + 1) % 4) * 4 + i % 4) for i in range(16)]
Z_DOWN = [(i, ((i // 4 + 3) % 4) * 4 + i % 4) for i in range(16)]
Y_HI = [(i, i ^ 2) for i in range(16)]
CORE = [(i, i ^ 1) for i in range(16)]


def after(value, *earlier):
    return lax.optimization_barrier((value, *earlier))[0]


class Link:
    def __init__(self, axis, pairs, most=2):
        self.axis, self.pairs, self.most, self.got = axis, pairs, most, []

    def __call__(self, value):
        if len(self.got) >= self.most:
            value = after(value, self.got[-self.most])
        self.got.append(lax.ppermute(value, self.axis, self.pairs))
        return self.got[-1]


def add(*terms):
    total = terms[0].astype(F32)
    for term in terms[1:]:
        total = total + term.astype(F32)
    return total


def row_weights(lengths, prompts, rewards):
    onehot = (prompts[:, None] == jnp.arange(PROMPTS, dtype=jnp.int32)[None, :]).astype(F32)
    counts = jnp.maximum(jnp.sum(onehot, 0), 1.0)
    means = jnp.sum(onehot * rewards[:, None], 0) / counts
    centred = rewards - jnp.sum(onehot * means[None, :], 1)
    spreads = jnp.sqrt(jnp.sum(onehot * (centred * centred)[:, None], 0) / counts)
    divisor = jnp.maximum(jnp.sum(onehot * spreads[None, :], 1), spread_floor)
    return centred / divisor / lengths.astype(F32)


def pack_kernel(weighted, spot_ref, weight_ref, target_ref, *refs):
    pieces, (far_ref, near_ref, stage, held, arrived) = refs[:-5], refs[-5:]
    copies = [
        pltpu.make_async_copy(piece, stage.at[p], arrived.at[p])
        for p, piece in enumerate(pieces)
    ]
    for copy in copies:
        copy.start()
    held[...] = jnp.zeros_like(held)
    for p, copy in enumerate(copies):
        copy.wait()
        for k in range(PER_OWNER):
            at = p * PER_OWNER + k
            block = stage[p, k]
            if weighted:
                block = (block.astype(F32) * weight_ref[at]).astype(BF)
            held[pl.ds(pl.multiple_of(spot_ref[at] * SLOTS, SLOTS), SLOTS), :] = block
    span = PER_OWNER * SLOTS
    places = lax.broadcasted_iota(jnp.int32, (CAPR, span), 0)
    for owner in range(OWNERS):
        onehot = (places == target_ref[owner]).astype(F32).astype(BF)
        rows = held[owner * span : (owner + 1) * span, :]
        out = jnp.dot(onehot, rows, preferred_element_type=F32).astype(BF)
        if owner < 4:
            far_ref[owner * CAPR : (owner + 1) * CAPR, :] = out
        else:
            near_ref[(owner - 4) * CAPR : (owner - 3) * CAPR, :] = out


def pack(spots, weights, targets, pieces, weighted):
    shape = pieces[0].shape
    width, count = shape[2], len(pieces)
    scalars, arrays = pl.BlockSpec(memory_space=pltpu.SMEM), pl.BlockSpec(memory_space=pltpu.VMEM)
    return pl.pallas_call(
        lambda *refs: pack_kernel(weighted, *refs),
        in_specs=[scalars, scalars, arrays] + [pl.BlockSpec(memory_space=pltpu.HBM)] * count,
        out_specs=[arrays, arrays],
        out_shape=[
            jax.ShapeDtypeStruct((4 * CAPR, width), BF),
            jax.ShapeDtypeStruct((12 * CAPR, width), BF),
        ],
        scratch_shapes=[
            pltpu.VMEM((count, *shape), BF),
            pltpu.VMEM((OWNERS * PER_OWNER * SLOTS, width), BF),
            pltpu.SemaphoreType.DMA((count,)),
        ],
        compiler_params=pltpu.CompilerParams(vmem_limit_bytes=24 << 20),
        cost_estimate=pl.CostEstimate(
            flops=2 * 2048 * 384 * 512, bytes_accessed=9 << 20, transcendentals=0
        ),
    )(spots, weights, targets, *pieces)


def input_grad_kernel(ahead, blocks, at_ref, *refs):
    parts, weights_ref, (kept_ref, sent_ref) = refs[:blocks], refs[blocks], refs[-2:]
    z = lax.rem(at_ref[0] + ahead, 4)
    for first in range(0, weights_ref.shape[1], 512):
        columns = slice(first, first + 512)
        out, row = None, 0
        for part in parts:
            term = lax.dot_general(
                part[...],
                weights_ref[row : row + part.shape[0], columns],
                (((0,), (0,)), ((), ())),
                preferred_element_type=F32,
            )
            out = term if out is None else out + term
            row += part.shape[0]
        out = out.astype(BF)
        for owner in range(4):
            y = lax.rem(at_ref[1] + owner // 2, 2)
            tile = out[owner * CAPR : (owner + 1) * CAPR]

            @pl.when(at_ref[2] == owner % 2)
            def _(tile=tile, y=y, columns=columns):
                kept_ref[z, y, :, columns] = tile

            @pl.when(at_ref[2] != owner % 2)
            def _(tile=tile, y=y, columns=columns):
                sent_ref[z, y, :, columns] = tile


def input_grads(ahead, at, parts, weights, so_far):
    arrays = pl.BlockSpec(memory_space=pltpu.VMEM)
    units, width = weights.shape
    count = 2 + len(parts)
    return pl.pallas_call(
        lambda *refs: input_grad_kernel(ahead, len(parts), *refs),
        in_specs=[pl.BlockSpec(memory_space=pltpu.SMEM)]
        + [arrays] * (count - 1)
        + [pl.BlockSpec(memory_space=pl.ANY)] * len(so_far),
        out_specs=[arrays] * 2,
        out_shape=[jax.ShapeDtypeStruct((4, 2, CAPR, width), BF)] * 2,
        input_output_aliases={count + k: k for k in range(len(so_far))},
        compiler_params=pltpu.CompilerParams(vmem_limit_bytes=24 << 20),
        cost_estimate=pl.CostEstimate(
            flops=2 * units * 512 * width, bytes_accessed=4 << 20, transcendentals=0
        ),
    )(at, *parts, weights, *so_far)


def product_kernel(counts, *refs):
    near_ref, far_ref, mine_ref, sent_ref = refs[-4:]
    chunks, used = [], 0
    for count in counts:
        chunks.append(refs[used : used + count])
        used += count
    rows = mine_ref.shape[0] // len(chunks[3])
    for out_ref, first in ((mine_ref, 0), (sent_ref, 512)):
        for block in range(len(chunks[3])):
            at = slice(block * rows, (block + 1) * rows)
            total = jnp.dot(
                chunks[3][block][...], far_ref[:, first : first + 512], preferred_element_type=F32
            )
            for k in range(3):
                left = chunks[k][0][at, :] if len(chunks[k]) == 1 else chunks[k][block][...]
                total += jnp.dot(
                    left,
                    near_ref[k * 512 : (k + 1) * 512, first : first + 512],
                    preferred_element_type=F32,
                )
            out_ref[at, :] = total.astype(BF)


def token_product(chunks, near, far):
    units = sum(block.shape[0] for block in chunks[0])
    counts = [len(chunk) for chunk in chunks]
    return pl.pallas_call(
        lambda *refs: product_kernel(counts, *refs),
        in_specs=[pl.BlockSpec(memory_space=pltpu.VMEM)] * (sum(counts) + 2),
        out_specs=[pl.BlockSpec(memory_space=pltpu.VMEM)] * 2,
        out_shape=[jax.ShapeDtypeStruct((units, 512), BF)] * 2,
        compiler_params=pltpu.CompilerParams(vmem_limit_bytes=40 << 20),
        cost_estimate=pl.CostEstimate(
            flops=2 * units * 2048 * 1024, bytes_accessed=10 << 20, transcendentals=0
        ),
    )(*[block for chunk in chunks for block in chunk], near, far)


def gathered_rows(piece, z_up, z_down, y_hi, beside=None):
    other = y_hi(piece)
    below, above = z_up(piece), z_down(piece)
    below_other, above_other = z_up(other), z_down(other)
    met = () if beside is None else (beside(other),)
    far, far_other = z_up(after(below, *met)), z_down(after(above_other, *met))
    return [piece, other, above, above_other, far, far_other, below, below_other]


def per_device(
    roll_hidden,
    roll_cotangent,
    lengths,
    owners,
    prompts,
    rewards,
    gate_weight,
    up_weight,
    down_weight,
):
    slot_count, full = roll_hidden.shape
    cols = lax.axis_size("col")
    width = full // cols
    r_at, c_at = lax.axis_index("row"), lax.axis_index("col")

    high = lax.reduce_precision(rewards, 8, 7)
    middle = lax.reduce_precision(rewards - high, 8, 7)
    low = rewards - high - middle
    numbers = jnp.stack(
        [lengths.astype(F32), owners.astype(F32), prompts.astype(F32), high, middle, low], axis=1
    )
    numbers = jnp.pad(numbers.astype(BF), ((0, SLOTS - slot_count - 1), (0, width - 6)))
    numbers = jnp.broadcast_to(numbers[None], (cols, SLOTS - slot_count, width))

    def blocks(array):
        return jnp.moveaxis(array.reshape(slot_count, cols, width), 1, 0)

    both = jnp.concatenate(
        [
            blocks(roll_hidden),
            numbers,
            blocks(roll_cotangent),
            jnp.zeros((cols, SLOTS - slot_count, width), BF),
        ],
        axis=1,
    )
    both = lax.all_to_all(both, "col", 0, 0, tiled=True)
    hidden_piece, grad_piece = both[:, :SLOTS], both[:, SLOTS:]

    x_at, odd, second_core = c_at // 2, c_at % 2 == 1, r_at % 2 == 1
    x_up, x_down, y_lo = Link("col", X_UP), Link("col", X_DOWN), Link("col", Y_LO, 1)
    z_up, z_down, core = Link("row", Z_UP, 1), Link("row", Z_DOWN, 1), Link("row", CORE)
    y_hi = Link("row", Y_HI, 1)

    units = down_weight.shape[0] // 2
    padded = -(-units // 16) * 16

    def split_units(weight):
        halves = [
            jnp.pad(weight[k * units : (k + 1) * units], ((0, padded - units), (0, 0)))
            for k in range(2)
        ]
        return jnp.where(odd, halves[1], halves[0]), jnp.where(odd, halves[0], halves[1])

    gate_mine, gate_sent = split_units(gate_weight.T)
    up_mine, up_sent = split_units(up_weight.T)
    down_mine, down_sent = split_units(down_weight)
    received = []

    def send_gate(other):
        received.append(y_lo(after(gate_sent, other)))
        return received[-1]

    hidden_piece = after(hidden_piece, gate_sent)
    hidden_pieces = gathered_rows(hidden_piece, z_up, z_down, y_hi, send_gate)
    received.append(y_lo(up_sent))
    gate_up_weights = jnp.concatenate(
        [
            jnp.concatenate([gate_mine, received[0]], 1),
            jnp.concatenate([up_mine, received[1]], 1),
        ]
    )
    grad_piece = after(grad_piece, hidden_pieces[4], hidden_pieces[5])
    grad_pieces = gathered_rows(grad_piece, z_up, z_down, y_hi)
    early = (grad_pieces[1], grad_pieces[2], grad_pieces[6])
    later, last = (grad_pieces[3], grad_pieces[7]), (grad_pieces[4], grad_pieces[5])

    told = jnp.concatenate([piece[:, slot_count, :8] for piece in hidden_pieces]).astype(F32)
    told = jnp.concatenate([told, core(after(told, received[1]))])
    all_lengths = told[:, 0].astype(jnp.int32)
    all_owners = told[:, 1].astype(jnp.int32)
    all_prompts = told[:, 2].astype(jnp.int32)
    weights = row_weights(all_lengths, all_prompts, told[:, 3] + told[:, 4] + told[:, 5])
    places = jnp.arange(OWNERS * cols, dtype=jnp.int32)
    step = places // cols
    ids = (
        ((r_at // 4 + step // 2 % 4) % 4) * 4
        + ((r_at // 2 % 2) ^ (step % 2)) * 2
        + ((r_at % 2) ^ (step // 8))
    ) * cols + places % cols
    earlier = (all_owners[None, :] == all_owners[:, None]) & (ids[None, :] < ids[:, None])
    offsets = jnp.sum(jnp.where(earlier, all_lengths[None, :], 0), 1)
    ranks = jnp.sum(earlier.astype(jnp.int32), 1)
    ahead = (all_owners // 4 - x_at) % 4
    ahead = jnp.where(ahead == 0, 3, jnp.where(ahead == 1, 1, jnp.where(ahead == 2, 0, 2)))
    spot = (ahead * 4 + all_owners % 4) * PER_OWNER + ranks
    own = OWNERS * cols // 2
    chosen = (spot[None, :] == places[:, None]) & (places[None, :] < own)

    def sort(values):
        return jnp.sum(jnp.where(chosen, values[None, :], 0), 1)[:, None]

    slots = jnp.arange(SLOTS, dtype=jnp.int32)[None, :]
    targets = jnp.where(slots < sort(all_lengths), sort(offsets) + slots, -1)
    targets = targets.reshape(OWNERS, 1, PER_OWNER * SLOTS)

    def paired(tokens, *met):
        whole = add(tokens, core(tokens)).astype(BF)
        n = whole.shape[0] // 2
        got = y_lo(jnp.where(second_core, whole[n:], whole[:n]))
        got = after(got, *met) if met else got
        other = core(got)
        first, second = jnp.where(second_core, other, got), jnp.where(second_core, got, other)
        return jnp.concatenate([whole, jnp.concatenate([first, second])], 1)

    def multiplied(weights, tokens):
        dims = (((1,), (1,)), ((), ()))
        return lax.dot_general(weights, tokens, dims, preferred_element_type=F32).astype(BF)

    spots = spot[:own]
    packed_far, packed_near = pack(spots, weights[:own], targets, hidden_pieces, False)
    x_far = paired(after(packed_far, *early), *later)
    gate_up = [multiplied(gate_up_weights, x_far)]
    gate_far, up_far = x_up(gate_up[0][:padded]), x_down(gate_up[0][padded:])
    spots = after(spots, gate_up[0])
    grad_far, grad_near = pack(spots, weights[:own], targets, grad_pieces, True)
    x_near = paired(packed_near, gate_far, up_far, grad_far, *last)
    gate_up += [multiplied(gate_up_weights, x_near[k * 512 : (k + 1) * 512]) for k in range(3)]
    (gate_1, gate_3, gate_0) = (part[:padded] for part in gate_up[1:])
    (up_1, up_3, up_0) = (part[padded:] for part in gate_up[1:])
    up_below, gate_above = x_up(up_1), x_down(gate_3)
    gate_below = x_up(add(gate_1, gate_far).astype(BF))
    up_above = x_down(add(up_3, up_far).astype(BF))
    gate, upval = add(gate_0, gate_below, gate_above), add(up_0, up_below, up_above)
    sig = jax.nn.sigmoid(gate)
    silu = gate * sig
    hidden = (silu * upval).astype(BF)

    middle = padded // 2
    hidden_below, hidden_above = x_up(hidden), x_down(hidden)
    hidden_far = [x_up(hidden_below[:middle]), x_down(hidden_above[middle:])]

    g_far, g_near = paired(grad_far), paired(grad_near)
    down_weights = jnp.concatenate([down_mine, y_lo(down_sent)], 1)
    grad_2 = multiplied(down_weights, g_far)
    grad_1, grad_3, grad_0 = (
        multiplied(down_weights, g_near[k * 512 : (k + 1) * 512]) for k in range(3)
    )
    far_1, far_2 = x_up(grad_2[:middle]), x_down(grad_2[middle:])
    below_2, above_1 = x_up(grad_1[middle:]), x_down(grad_3[:middle])
    below_1 = x_up(add(grad_1[:middle], far_1).astype(BF))
    above_2 = x_down(add(grad_3[middle:], far_2).astype(BF))
    grad_hidden = jnp.concatenate(
        [add(grad_0[:middle], below_1, above_1), add(grad_0[middle:], below_2, above_2)]
    )
    gate_act = (grad_hidden * upval * sig * (1.0 + gate * (1.0 - sig))).astype(BF)
    up_act = (grad_hidden * silu).astype(BF)

    def exchanged(mine, sent):
        got = y_lo(sent)
        out = []
        for k in range(mine.shape[0] // padded):
            one, two = (v[k * padded : k * padded + units] for v in (mine, got))
            out.append(
                jnp.where(odd, jnp.concatenate([two, one]), jnp.concatenate([one, two]))
            )
        return out, got

    gate_act_below, up_act_above = x_up(gate_act), x_down(up_act)
    up_act_below, gate_act_above = x_up(up_act), x_down(gate_act)
    act, act_below = [gate_act, up_act], [gate_act_below, up_act_below]
    act_above = [gate_act_above, up_act_above]
    (grad_down,), got_down = exchanged(
        *token_product([[hidden_above], [hidden_below], [hidden], hidden_far], g_near, g_far)
    )
    at = jnp.stack([x_at - r_at // 4 + 4, r_at // 2 % 2, r_at % 2]).astype(jnp.int32)
    tiles = input_grads(0, at, act, gate_up_weights, [])
    act_far = [x_up(after(gate_act_below, got_down)), x_down(up_act_above)]

    tiles = input_grads(1, at, act_above, gate_up_weights, tiles)
    tiles = input_grads(3, at, act_below, gate_up_weights, tiles)
    kept, sent = input_grads(2, at, act_far, gate_up_weights, tiles)
    z_up, z_down = Link("row", Z_UP), Link("row", Z_DOWN)
    sent = core(sent)
    weight_grads = token_product([act_above, act_below, act, act_far], x_near, x_far)
    (grad_gate, grad_up), _ = exchanged(*weight_grads)
    tiles = add(after(kept, weight_grads[0]), sent).astype(BF)
    far_1, far_0 = z_up(tiles[2, 1]), z_down(tiles[2, 0])
    above_1 = z_down(tiles[3, 1])
    below_1 = z_up(add(tiles[1, 1], far_1).astype(BF))
    below_0 = z_up(tiles[1, 0])
    above_0 = z_down(add(tiles[3, 0], far_0).astype(BF))
    other = y_hi(add(tiles[0, 1], below_1, above_1).astype(BF))
    tiles = add(tiles[0, 0], below_0, above_0, other)

    grad_input = add(tiles[:, :width], y_lo(tiles[:, width:].astype(BF))).astype(BF)
    return grad_input, grad_gate.T, grad_up.T, grad_down


def solution(mesh):
    return jax.shard_map(
        per_device,
        mesh=mesh,
        in_specs=(
            P(("row", "col"), None),
            P(("row", "col"), None),
            P(("row", "col")),
            P(("row", "col")),
            P(("row", "col")),
            P(("row", "col")),
            P("col", "row"),
            P("col", "row"),
            P("row", "col"),
        ),
        out_specs=(P("row", "col"), P("col", "row"), P("col", "row"), P("row", "col")),
        check_vma=False,
    )
```
